32 devices in a mesh: crop: 2 (over x), row: 16 (over z, y, core).
Axes of the slice: x: 2, y: 2, z: 4, core: 2. Of those that a mesh axis runs over, the one named last changes fastest.
Arguments:
- pair: bfloat16 [2, 384, 384, 128], P('crop', 'row'), may hold values from -6 to 6
- crop_len: int32 [2], P('crop'), may hold values from 192 to 384, as said below
- targets: int32 [2, 384, 384], P('crop', 'row'), may hold values from 0 to 63
- neighbours: int32 [2, 384, 384], P('crop', 'row'), may hold values 0 or 1
- wide: float32 [128, 1152], P('row', 'crop'), may hold values from -0.5 to 0.5
- wide_rows: float32 [128], P('row'), may hold values from 2.0345052e-07 to 2.0616319e-05, as said below
- wide_cols: float32 [1152], P('crop'), may hold values from 2.0345052e-07 to 2.0616319e-05, as said below
- down: float32 [512, 128], P('row', 'crop'), may hold values from -0.25 to 0.25
- down_rows: float32 [512], P('row'), may hold values from 2.0345052e-07 to 2.0616319e-05, as said below
- down_cols: float32 [128], P('crop'), may hold values from 2.0345052e-07 to 2.0616319e-05, as said below
- gains: float32 [3, 128], replicated, may hold values from 0.45 to 2.75, as said below
- gain_second: float32 [3, 128], replicated, may hold values from 1e-05 to 4e-05
- small: float32 [128, 68], replicated, may hold values from -0.5 to 0.5
- small_second: float32 [128, 68], replicated, may hold values from 1.2885199e-06 to 5.1540796e-06
Outputs:
- loss_sum: float32 [], replicated
- pair_count: float32 [], replicated
- wide_grad: float32 [128, 1152], P('row', 'crop')
- wide_rows_new: float32 [128], P('row')
- wide_cols_new: float32 [1152], P('crop')
- wide_new: float32 [128, 1152], P('row', 'crop')
- down_grad: float32 [512, 128], P('row', 'crop')
- down_rows_new: float32 [512], P('row')
- down_cols_new: float32 [128], P('crop')
- down_new: float32 [512, 128], P('row', 'crop')
- gain_grad: float32 [3, 128], replicated
- gain_second_new: float32 [3, 128], replicated
- gains_new: float32 [3, 128], replicated
- small_grad: float32 [128, 68], replicated
- small_second_new: float32 [128, 68], replicated
- small_new: float32 [128, 68], replicated
The draws below stay inside these ranges and needn't reach their ends.
Inputs may be any that keep to these rules, and one draw needn't show every extreme that they name: `crop_len`: the first entry is 384; the others lie between 192 and 384. `wide_rows`: Positive. `wide_cols`: Positive. `down_rows`: Positive. `down_cols`: Positive. `gains`: Positive.
All inputs are finite; a program needn't handle non-finite values. No bound on the sum of `neighbours` on one device may be relied on, other than what follows from the above.
Results may differ from the reference program's by a relative error of at most 0.0052.
The reference program's roundings to bfloat16 on the way count: a program that leaves them out, or rounds other values in their place, can miss the bound.
Values may be sent and summed in bfloat16 or wider, within the bound.
No kernel may reach another device: no remote copies, remote signals or barrier semaphores. Data moves between devices by JAX's collectives and lax.ppermute only.
A program may use at most 320 MiB of HBM per device.

```python
import math
import jax
import jax.numpy as jnp
from jax import lax

CZ = 128
HEADS = 4
HEAD_DIM = 32
FF = 512
BINS = 64
N = 384
CROPS = 2
WIDE = 1152
SMALL_COLS = 68


def draw_crop_len(key, part):
    key = jax.random.fold_in(key, 7)
    others = jax.random.randint(key, (CROPS - 1,), N // 2, N + 1).astype(jnp.int32)
    return jnp.concatenate([jnp.full((1,), N, jnp.int32), others])


def falling(key, length, top):
    base = jax.random.uniform(key, (length,), jnp.float32, math.log(0.19), math.log(0.76))
    ramp = jnp.arange(length, dtype=jnp.float32) / (length - 1)
    return jnp.exp(base + math.log(4.0) - math.log(top) * ramp) / (N * N)


def draw_wide_rows(key, part):
    key = jax.random.fold_in(key, 11)
    return falling(key, CZ, 16.0)


def draw_wide_cols(key, part):
    key = jax.random.fold_in(key, 12)
    return falling(key, WIDE, 16.0)


def draw_down_rows(key, part):
    key = jax.random.fold_in(key, 13)
    return falling(key, FF, 16.0)


def draw_down_cols(key, part):
    key = jax.random.fold_in(key, 14)
    return falling(key, CZ, 16.0)


def rising(key, start, factor, spread):
    ramp = jnp.arange(CZ, dtype=jnp.float32) / (CZ - 1)
    noise = jax.random.uniform(key, (3, CZ), jnp.float32, 1.0 - spread, 1.0 + spread)
    return start * jnp.exp(math.log(factor) * ramp)[None, :] * noise


def draw_gains(key, part):
    key = jax.random.fold_in(key, 15)
    return rising(key, 0.6, 3.0, 0.15)


def with_ends(values, rng, low, high):
    longest = values.shape.index(max(values.shape))
    spots = []
    for shift in (0, 1):
        where = [jax.random.randint(jax.random.fold_in(rng, axis), (), 0, length) for axis, length in enumerate(values.shape)]
        where[longest] = (where[longest] + shift) % values.shape[longest]
        spots.append(tuple(where))
    return values.at[spots[0]].set(low).at[spots[1]].set(high)


def block_scale(key, shape, split, least, largest):
    def one(dim, blocks):
        heights = jax.random.uniform(jax.random.fold_in(jax.random.fold_in(key, 6), dim), (blocks,), jnp.float32, least / len(split), largest / len(split))
        return jnp.repeat(jnp.exp(heights), shape[dim] // blocks).reshape((-1,) + (1,) * (len(shape) - dim - 1))

    loudness = one(*split[0])
    for cut in split[1:]:
        loudness = loudness * one(*cut)
    return loudness


def gaussian(stream_key, extent, scale, limit, cuts=(), kind=jnp.bfloat16):
    level = block_scale(stream_key, extent, cuts, -0.22, 0.18) if cuts else 1.0
    drawn = jax.random.normal(stream_key, extent, jnp.float32) * scale * level
    return jnp.minimum(jnp.maximum(drawn, -limit), limit).astype(kind)


def setup_inputs(seed: int = 0) -> dict:
    streams_of = jax.random.split(jax.random.key(seed), 15)
    return {
        "pair": gaussian(streams_of[0], (CROPS, N, N, CZ), 1.0, 6.0, ((0, 2), (1, 16))),
        "crop_len": draw_crop_len(jax.random.fold_in(streams_of[14], 71), 0),
        "targets": with_ends(jax.random.randint(streams_of[2], (CROPS, N, N), 0, BINS), jax.random.fold_in(streams_of[2], 1), 0, BINS - 1).astype(jnp.int32),
        "neighbours": with_ends((jax.random.randint(streams_of[3], (CROPS, N, N), 0, 4) < 3).astype(jnp.int32), jax.random.fold_in(streams_of[3], 1), 0, 1),
        "wide": gaussian(streams_of[4], (CZ, WIDE), CZ ** -0.5, 0.5, ((0, 16), (1, 2)), jnp.float32),
        "wide_rows": draw_wide_rows(jax.random.fold_in(streams_of[14], 71), 0),
        "wide_cols": draw_wide_cols(jax.random.fold_in(streams_of[14], 71), 0),
        "down": gaussian(streams_of[7], (FF, CZ), FF ** -0.5, 0.25, ((0, 16), (1, 2)), jnp.float32),
        "down_rows": draw_down_rows(jax.random.fold_in(streams_of[14], 71), 0),
        "down_cols": draw_down_cols(jax.random.fold_in(streams_of[14], 71), 0),
        "gains": draw_gains(jax.random.fold_in(streams_of[14], 71), 0),
        "gain_second": jnp.clip(jnp.exp(jax.random.uniform(streams_of[11], (3, CZ), jnp.float32, math.log(9.999999747378752e-06), math.log(3.9999998989515007e-05))), 9.999999747378752e-06, 3.9999998989515007e-05),
        "small": gaussian(streams_of[12], (CZ, SMALL_COLS), CZ ** -0.5, 0.5, (), jnp.float32),
        "small_second": jnp.clip(jnp.exp(jax.random.uniform(streams_of[13], (CZ, SMALL_COLS), jnp.float32, math.log(1.2885199112133705e-06), math.log(5.154079644853482e-06))), 1.2885199112133705e-06, 5.154079644853482e-06),
    }


@jax.custom_vjp
def low(v):
    return lax.optimization_barrier(v.astype(jnp.bfloat16)).astype(jnp.float32)

@jax.custom_vjp
def low_back(v):
    return v

def low_keep(v):
    return (low(v), None)

def low_pass(kept, grad):
    return (grad,)

def back_keep(v):
    return (v, None)

def back_low(kept, grad):
    return (low(grad),)
low.defvjp(low_keep, low_pass)
low_back.defvjp(back_keep, back_low)
HIGH = lax.Precision.HIGHEST
DECAY = 1.0 - 10.0 ** (-0.8)
TINY = 1e-30

def rounded(v):
    return low_back(low(v))

def normed(x, gain):
    centre = x - lax.optimization_barrier(jnp.mean(x, -1, keepdims=True))
    var = lax.optimization_barrier(jnp.mean(centre * centre, -1, keepdims=True))
    return centre * lax.rsqrt(var + 1e-05) * gain

def crop_loss(z, valid, nbr, tgt, wide, down, gains, small):
    zb = rounded(normed(z, gains[0]))
    proj = jnp.einsum('ijc,cd->ijd', zb, wide[:, :4 * CZ], precision=HIGH)
    query = rounded(proj[..., :CZ])
    keys = rounded(proj[..., CZ:2 * CZ])
    values = rounded(proj[..., 2 * CZ:3 * CZ])
    gate = proj[..., 3 * CZ:]
    bias = rounded(jnp.einsum('ijc,ch->hij', zb, small[:, :HEADS], precision=HIGH))
    key_bias = jnp.where(valid, 0.0, -1000000000.0).astype(jnp.float32)

    def one_row(items):
        qrow, krow, vrow, grow = items
        qh = qrow.reshape(N, HEADS, HEAD_DIM)
        kh = krow.reshape(N, HEADS, HEAD_DIM)
        vh = vrow.reshape(N, HEADS, HEAD_DIM)
        score = jnp.einsum('jhd,khd->hjk', qh, kh, precision=HIGH) / jnp.sqrt(jnp.float32(HEAD_DIM))
        score = score + bias + key_bias[None, None, :]
        probs = rounded(jax.nn.softmax(score, -1))
        outs = jnp.einsum('hjk,khd->jhd', probs, vh, precision=HIGH).reshape(N, CZ)
        return rounded(outs * jax.nn.sigmoid(grow))
    attended = lax.map(jax.checkpoint(one_row), (query, keys, values, gate))
    z1 = z + jnp.einsum('ijc,cd->ijd', attended, wide[:, 4 * CZ:5 * CZ], precision=HIGH)
    zb2 = rounded(normed(z1, gains[1]))
    hidden = rounded(jax.nn.silu(jnp.einsum('ijc,cd->ijd', zb2, wide[:, 5 * CZ:], precision=HIGH)))
    z2 = z1 + jnp.einsum('ijd,dc->ijc', hidden, down, precision=HIGH)
    zb3 = rounded(normed(z2, gains[2]))
    logits = jnp.einsum('ijc,cb->ijb', zb3, small[:, HEADS:], precision=HIGH)
    logp = jax.nn.log_softmax(logits, -1)
    onehot = (tgt[..., None] == jnp.arange(BINS, dtype=jnp.int32)).astype(jnp.float32)
    mask = (valid[:, None] & valid[None, :] & (nbr > 0)).astype(jnp.float32)
    return -jnp.sum(lax.optimization_barrier(jnp.sum(logp * onehot, -1)) * mask)

def factored(weight, grad, rows, cols):
    sq = grad * grad
    rows_new = DECAY * rows + (1.0 - DECAY) * (lax.optimization_barrier(jnp.mean(sq, 1)) + TINY)
    cols_new = DECAY * cols + (1.0 - DECAY) * (lax.optimization_barrier(jnp.mean(sq, 0)) + TINY)
    second = rows_new[:, None] * cols_new[None, :] / jnp.mean(rows_new)
    update = grad * lax.rsqrt(second)
    clip = jnp.maximum(0.1, jnp.sqrt(jnp.mean(update * update)))
    return (rows_new, cols_new, weight - 0.03 * update / clip)

def plain(weight, grad, second, rate):
    second_new = DECAY * second + (1.0 - DECAY) * (grad * grad + TINY)
    update = grad * lax.rsqrt(second_new)
    clip = jnp.maximum(1.0, jnp.sqrt(jnp.mean(update * update)))
    return (second_new, weight - rate * update / clip)

def reference(pair, crop_len, targets, neighbours, wide, wide_rows, wide_cols, down, down_rows, down_cols, gains, gain_second, small, small_second):
    index = jnp.arange(N, dtype=jnp.int32)

    def total(wide_w, down_w, gain_w, small_w):
        wide_b, down_b, small_b = (low(wide_w), low(down_w), low(small_w))
        acc = jnp.float32(0.0)
        for crop in range(CROPS):
            valid = index < crop_len[crop]
            acc = acc + crop_loss(pair[crop].astype(jnp.float32), valid, neighbours[crop], targets[crop], wide_b, down_b, gain_w, small_b)
        return acc
    count = jnp.float32(0.0)
    for crop in range(CROPS):
        valid = index < crop_len[crop]
        count = count + jnp.sum((valid[:, None] & valid[None, :] & (neighbours[crop] > 0)).astype(jnp.float32))
    loss_sum, backward = jax.vjp(total, wide, down, gains, small)
    wide_g, down_g, gain_g, small_g = backward(jnp.float32(1.0) / count)
    wide_r, wide_c, wide_n = factored(wide, wide_g, wide_rows, wide_cols)
    down_r, down_c, down_n = factored(down, down_g, down_rows, down_cols)
    gain_s, gain_n = plain(gains, gain_g, gain_second, 0.3)
    small_s, small_n = plain(small, small_g, small_second, 0.03)
    return (loss_sum, count, wide_g, wide_r, wide_c, wide_n, down_g, down_r, down_c, down_n, gain_g, gain_s, gain_n, small_g, small_s, small_n)
```

```python
import math

import jax
import jax.numpy as jnp
from jax import lax
from jax.experimental import pallas as pl
from jax.experimental.pallas import tpu as pltpu
from jax.sharding import PartitionSpec as P

CZ = 128
HEADS = 4
HEAD_DIM = 32
FF = 512
BINS = 64
WIDE = 5 * CZ + FF

DECAY = 1.0 - 10.0 ** (-0.8)
TINY = 1e-30
LOG2E = math.log2(math.e)
ROOT = 1.0 / math.sqrt(HEAD_DIM)
BLK = 256

f32 = jnp.float32
bf16 = jnp.bfloat16


def dot(a, b):
    return lax.dot_general(a, b, (((1,), (0,)), ((), ())), preferred_element_type=f32)


def dot_nt(a, b):
    return lax.dot_general(a, b, (((1,), (1,)), ((), ())), preferred_element_type=f32)


def rounded(v):
    return v.astype(bf16).astype(f32)


def halves(v):
    high = v.astype(bf16)
    return high, (v - high.astype(f32)).astype(bf16)


def normed(x):
    centre = x - jnp.sum(x, 0, keepdims=True) * (1.0 / CZ)
    var = jnp.sum(centre * centre, 0, keepdims=True) * (1.0 / CZ)
    inv = lax.rsqrt(var + 1e-05)
    return centre * inv, inv


def normed_back(d, xhat, inv):
    one = jnp.sum(d, 0, keepdims=True) * (1.0 / CZ)
    two = jnp.sum(d * xhat, 0, keepdims=True) * (1.0 / CZ)
    return inv * (d - one - xhat * two)


def sigmoid(x):
    return 0.5 * jnp.tanh(0.5 * x) + 0.5


def front_kernel(pair_ref, gain_ref, wb_ref, zt_ref, zbt_ref, bias_ref):
    x = pair_ref[0].astype(f32).T
    zt_ref[0] = x.astype(bf16)
    xhat, _ = normed(x)
    zb = (xhat * gain_ref[...]).astype(bf16)
    zbt_ref[0] = zb
    bias_ref[0] = dot(wb_ref[...], zb)[:HEADS].astype(bf16)


def middle_kernel(
    order_ref,
    scale_ref,
    bias_ref,
    kb_ref,
    wide_ref,
    down_ref,
    head_ref,
    g1_ref,
    g2_ref,
    zt_ref,
    zbt_ref,
    tgt_ref,
    msk_ref,
    p_ref,
    qkvd_ref,
    dgt_ref,
    dd_ref,
    dwo_ref,
    dwin_ref,
    ddown_ref,
    dhead_ref,
    loss_ref,
    biast,
    nat,
    wqt,
    wot,
    wint,
    wdownt,
    wht,
    wo2,
    wdown2,
    wh2,
    qbd,
):
    width = zt_ref.shape[2]
    shards, _, rows, _ = bias_ref.shape

    @pl.when(pl.program_id(0) == 0)
    def _():
        for h in range(HEADS):
            for s in range(shards):
                nat[s * rows : (s + 1) * rows, :] = bias_ref[order_ref[s], h].astype(f32)
            biast[:, h * width : (h + 1) * width] = (nat[...] * LOG2E + kb_ref[...]).T
        wide = wide_ref[...].astype(f32)
        wqt[...] = wide[:, : 4 * CZ].T.astype(bf16)
        wot[...] = wide[:, 4 * CZ : 5 * CZ].T.astype(bf16)
        wint[...] = wide[:, 5 * CZ :].T.astype(bf16)
        wdownt[...] = down_ref[...].astype(f32).T.astype(bf16)
        wht[...] = head_ref[...].astype(f32).T.astype(bf16)
        wo = wide_ref[:, 4 * CZ : 5 * CZ]
        wo2[...] = jnp.concatenate([wo, wo], 1)
        wdown2[...] = jnp.concatenate([down_ref[...], down_ref[...]], 1)
        wh2[...] = jnp.concatenate([head_ref[...], head_ref[...]], 1)
        qbd[...] = jnp.zeros_like(qbd)
        dwo_ref[...] = jnp.zeros_like(dwo_ref)
        dwin_ref[...] = jnp.zeros_like(dwin_ref)
        ddown_ref[...] = jnp.zeros_like(ddown_ref)
        dhead_ref[...] = jnp.zeros_like(dhead_ref)
        loss_ref[...] = jnp.zeros_like(loss_ref)

    proj = dot(wqt[...], zbt_ref[0])
    q = proj[:CZ].astype(bf16)
    k = proj[CZ : 2 * CZ].astype(bf16)
    v = proj[2 * CZ : 3 * CZ].astype(bf16)
    gate = sigmoid(proj[3 * CZ :])
    qkvd_ref[0, :CZ] = q
    qkvd_ref[0, CZ : 2 * CZ] = k
    qkvd_ref[0, 2 * CZ : 3 * CZ] = v
    kn = k.T
    kk = jnp.concatenate([kn, kn], 1)
    high, low = halves(q.astype(f32) * (LOG2E * ROOT))
    for h in range(HEADS):
        a, b = h * HEAD_DIM, (h + 1) * HEAD_DIM
        qbd[a:b, h * width : (h + 1) * width] = high[a:b]
        qbd[CZ + a : CZ + b, h * width : (h + 1) * width] = low[a:b]
    for c in range(0, HEADS * width, BLK):
        s = dot(kk, qbd[:, c : c + BLK]) + biast[:, c : c + BLK]
        e = jnp.exp2(s - jnp.max(s, 0, keepdims=True))
        r = 1.0 / jnp.sum(e, 0, keepdims=True)
        p_ref[0, :, c : c + BLK] = (e * r).astype(bf16)
    o = jnp.concatenate(
        [
            dot(v[h * HEAD_DIM : (h + 1) * HEAD_DIM], p_ref[0, :, h * width : (h + 1) * width])
            for h in range(HEADS)
        ],
        0,
    )
    og = (o * gate).astype(bf16)

    z1 = zt_ref[0].astype(f32) + dot(wot[...], og)
    xhat1, inv1 = normed(z1)
    zb2 = (xhat1 * g1_ref[...]).astype(bf16)
    hid = dot(wint[...], zb2)
    sg = sigmoid(hid)
    a = (hid * sg).astype(bf16)
    z2 = z1 + dot(wdownt[...], a)
    xhat2, inv2 = normed(z2)
    zb3 = (xhat2 * g2_ref[...]).astype(bf16)
    logits = dot(wht[...], zb3)
    top = jnp.max(logits, 0, keepdims=True)
    ex = jnp.exp(logits - top)
    total = jnp.sum(ex, 0, keepdims=True)
    hot = lax.broadcasted_iota(jnp.int32, logits.shape, 0) == tgt_ref[0]
    picked = jnp.sum(jnp.where(hot, logits, 0.0), 0, keepdims=True)
    mask = msk_ref[0]
    loss_ref[...] += (jnp.log(total) + top - picked) * mask

    weight = mask * scale_ref[0]
    dl = ex * (weight / total) - jnp.where(hot, weight, 0.0)
    dl2 = jnp.concatenate(halves(dl), 0)
    dhead_ref[...] += dot_nt(dl2, zb3)
    dzb3 = rounded(dot(wh2[...], dl2))
    dz2 = normed_back(dzb3 * g2_ref[...], xhat2, inv2)
    high2, low2 = halves(dz2)
    da = rounded(dot(wdown2[...], jnp.concatenate([high2, low2], 0)))
    dh = (da * (sg * (1.0 + hid * (1.0 - sg)))).astype(bf16)
    ddown_ref[...] += dot_nt(high2, a)
    dzb2 = rounded(dot(wide_ref[:, 5 * CZ :], dh))
    dwin_ref[...] += dot_nt(zb2, dh)
    dz1 = dz2 + normed_back(dzb2 * g1_ref[...], xhat1, inv1)
    high1, low1 = halves(dz1)
    dwo_ref[...] += dot_nt(og, high1)
    dog = rounded(dot(wo2[...], jnp.concatenate([high1, low1], 0)))
    do = dog * gate
    doo = do * o
    dgt_ref[0] = (doo * (1.0 - gate)).astype(bf16)
    qkvd_ref[0, 3 * CZ :] = do.astype(bf16)
    for h in range(HEADS):
        dd_ref[0, :, h * width : (h + 1) * width] = jnp.sum(
            doo[h * HEAD_DIM : (h + 1) * HEAD_DIM], 0, keepdims=True
        )


def back_kernel(
    p_ref, qkvd_ref, dgt_ref, dd_ref, zbt_ref, dbias_ref, dwq_ref, acc, dobd, dst
):
    width = zbt_ref.shape[2]
    step = pl.program_id(0)

    @pl.when(step == 0)
    def _():
        dobd[...] = jnp.zeros_like(dobd)
        acc[...] = jnp.zeros_like(acc)
        dwq_ref[...] = jnp.zeros_like(dwq_ref)

    q = qkvd_ref[0, :CZ]
    k = qkvd_ref[0, CZ : 2 * CZ]
    v = qkvd_ref[0, 2 * CZ : 3 * CZ]
    do = qkvd_ref[0, 3 * CZ :]
    vv = jnp.concatenate([v.T, jnp.ones((width, CZ), bf16)], 1)
    minus = -dd_ref[0]
    high = rounded(minus)
    dobd[CZ : CZ + 16, :] = jnp.concatenate(
        [high, minus - high, jnp.zeros((14, HEADS * width), f32)], 0
    ).astype(bf16)
    for h in range(HEADS):
        a, b = h * HEAD_DIM, (h + 1) * HEAD_DIM
        dobd[a:b, h * width : (h + 1) * width] = do[a:b]
    for c in range(0, HEADS * width, BLK):
        ds = dot(vv, dobd[:, c : c + BLK]) * p_ref[0, :, c : c + BLK].astype(f32)
        acc[:, c : c + BLK] += ds
        dst[:, c : c + BLK] = ds.astype(bf16)
    dq, dk, dv = [], [], []
    for h in range(HEADS):
        a, b = h * HEAD_DIM, (h + 1) * HEAD_DIM
        mine = dst[:, h * width : (h + 1) * width]
        dq.append(dot(k[a:b], mine) * ROOT)
        dk.append(dot_nt(q[a:b], mine) * ROOT)
        dv.append(dot_nt(do[a:b], p_ref[0, :, h * width : (h + 1) * width]))
    dproj = jnp.concatenate(dq + dk + dv, 0).astype(bf16)
    dproj = jnp.concatenate([dproj, dgt_ref[0]], 0)
    dwq_ref[...] += dot_nt(zbt_ref[0], dproj)

    @pl.when(step == pl.num_programs(0) - 1)
    def _():
        for h in range(HEADS):
            dbias_ref[h] = acc[:, h * width : (h + 1) * width].T.astype(bf16)


def whole(shape):
    return pl.BlockSpec(shape, lambda i: (0,) * len(shape))


def by_row(shape):
    return pl.BlockSpec((1,) + shape, lambda i: (i,) + (0,) * len(shape))


SMEM = pl.BlockSpec(memory_space=pltpu.SMEM)
PARAMS = pltpu.CompilerParams(vmem_limit_bytes=56 * 1024 * 1024)


def front(pair, gain, w_bias):
    count_rows, width = pair.shape[0], pair.shape[1]
    return pl.pallas_call(
        front_kernel,
        grid=(count_rows,),
        in_specs=[by_row((width, CZ)), whole((CZ, width)), whole((16, CZ))],
        out_specs=[by_row((CZ, width)), by_row((CZ, width)), by_row((HEADS, width))],
        out_shape=[
            jax.ShapeDtypeStruct((count_rows, CZ, width), bf16),
            jax.ShapeDtypeStruct((count_rows, CZ, width), bf16),
            jax.ShapeDtypeStruct((count_rows, HEADS, width), bf16),
        ],
        compiler_params=PARAMS,
        name="front",
    )(pair, gain, w_bias)


def middle(order, scale, bias, kb, wide, down, head, g1, g2, zt, zbt, tgt, msk):
    count_rows, _, width = zt.shape
    return pl.pallas_call(
        middle_kernel,
        grid=(count_rows,),
        in_specs=[
            SMEM,
            SMEM,
            whole(bias.shape),
            whole((1, width)),
            whole((CZ, WIDE)),
            whole((FF, CZ)),
            whole((CZ, BINS)),
            whole((CZ, width)),
            whole((CZ, width)),
            by_row((CZ, width)),
            by_row((CZ, width)),
            by_row((1, width)),
            by_row((1, width)),
        ],
        out_specs=[
            by_row((width, HEADS * width)),
            by_row((4 * CZ, width)),
            by_row((CZ, width)),
            by_row((1, HEADS * width)),
            whole((CZ, CZ)),
            whole((CZ, FF)),
            whole((CZ, FF)),
            whole((2 * BINS, CZ)),
            whole((1, width)),
        ],
        out_shape=[
            jax.ShapeDtypeStruct((count_rows, width, HEADS * width), bf16),
            jax.ShapeDtypeStruct((count_rows, 4 * CZ, width), bf16),
            jax.ShapeDtypeStruct((count_rows, CZ, width), bf16),
            jax.ShapeDtypeStruct((count_rows, 1, HEADS * width), f32),
            jax.ShapeDtypeStruct((CZ, CZ), f32),
            jax.ShapeDtypeStruct((CZ, FF), f32),
            jax.ShapeDtypeStruct((CZ, FF), f32),
            jax.ShapeDtypeStruct((2 * BINS, CZ), f32),
            jax.ShapeDtypeStruct((1, width), f32),
        ],
        scratch_shapes=[
            pltpu.VMEM((width, HEADS * width), f32),
            pltpu.VMEM((width, width), f32),
            pltpu.VMEM((4 * CZ, CZ), bf16),
            pltpu.VMEM((CZ, CZ), bf16),
            pltpu.VMEM((FF, CZ), bf16),
            pltpu.VMEM((CZ, FF), bf16),
            pltpu.VMEM((BINS, CZ), bf16),
            pltpu.VMEM((CZ, 2 * CZ), bf16),
            pltpu.VMEM((FF, 2 * CZ), bf16),
            pltpu.VMEM((CZ, 2 * BINS), bf16),
            pltpu.VMEM((2 * CZ, HEADS * width), bf16),
        ],
        compiler_params=PARAMS,
        name="middle",
    )(order, scale, bias, kb, wide, down, head, g1, g2, zt, zbt, tgt, msk)


def back(p, qkvd, dgt, dd, zbt):
    count_rows, _, width = zbt.shape
    return pl.pallas_call(
        back_kernel,
        grid=(count_rows,),
        in_specs=[
            by_row((width, HEADS * width)),
            by_row((4 * CZ, width)),
            by_row((CZ, width)),
            by_row((1, HEADS * width)),
            by_row((CZ, width)),
        ],
        out_specs=[whole((HEADS, width, width)), whole((CZ, 4 * CZ))],
        out_shape=[
            jax.ShapeDtypeStruct((HEADS, width, width), bf16),
            jax.ShapeDtypeStruct((CZ, 4 * CZ), f32),
        ],
        scratch_shapes=[
            pltpu.VMEM((width, HEADS * width), f32),
            pltpu.VMEM((2 * CZ, HEADS * width), bf16),
            pltpu.VMEM((width, HEADS * width), bf16),
        ],
        compiler_params=PARAMS,
        name="back",
    )(p, qkvd, dgt, dd, zbt)


def bits(n):
    return [1 << t for t in reversed(range(n.bit_length() - 1))]


def swap(x, axes, size, mask):
    return lax.ppermute(x, axes, [(i, i ^ mask) for i in range(size)])


def gathered(x, axes, size, masks):
    x = x[None]
    for mask in masks:
        x = jnp.concatenate([x, swap(x, axes, size, mask)], 0)
    return x


def places(me, size, masks):
    apart = jnp.arange(size, dtype=jnp.int32) ^ me
    place = jnp.zeros((size,), jnp.int32)
    for t, mask in enumerate(masks):
        place = place + jnp.where((apart & mask) != 0, 1 << t, 0)
    return place


def summed(x, axes, size, masks):
    for mask in masks:
        x = x + swap(x, axes, size, mask)
    return x


def plain(weight, grad, second, rate):
    second_new = DECAY * second + (1.0 - DECAY) * (grad * grad + TINY)
    update = grad * lax.rsqrt(second_new)
    clip = jnp.maximum(1.0, jnp.sqrt(jnp.mean(update * update)))
    return (second_new, weight - rate * update / clip)


def factored(grad_all, rows_all, cols_all, grad, weight, row_start, col_start):
    sq = grad_all * grad_all
    rows_new = DECAY * rows_all + (1.0 - DECAY) * (jnp.mean(sq, 1) + TINY)
    cols_new = DECAY * cols_all + (1.0 - DECAY) * (jnp.mean(sq, 0) + TINY)
    mean = jnp.mean(rows_new)
    size = jnp.mean(sq * (mean / (rows_new[:, None] * cols_new[None, :])))
    clip = jnp.maximum(0.1, jnp.sqrt(size))
    rows_mine = lax.dynamic_slice_in_dim(rows_new, row_start, grad.shape[0])
    cols_mine = lax.dynamic_slice_in_dim(cols_new, col_start, grad.shape[1])
    second = rows_mine[:, None] * cols_mine[None, :] / mean
    return rows_mine, cols_mine, weight - 0.03 * (grad * lax.rsqrt(second)) / clip


def build(crops, rows):
    both = ("crop", "row")
    devices = crops * rows
    row_masks = bits(rows)
    all_masks = row_masks[:-1] + [m * rows for m in bits(crops)] + row_masks[-1:]

    def split(x):
        r, c = x.shape[0] // rows, x.shape[1] // crops
        return x.reshape(rows, r, crops, c).transpose(2, 0, 1, 3).reshape(devices, r * c)

    def joined(x, r, c):
        return x.reshape(crops, rows, r, c).transpose(1, 2, 0, 3).reshape(rows * r, crops * c)

    def body(
        pair,
        crop_len,
        targets,
        neighbours,
        wide,
        wide_rows,
        wide_cols,
        down,
        down_rows,
        down_cols,
        gains,
        gain_second,
        small,
        small_second,
    ):
        row_index = lax.axis_index("row")
        crop_index = lax.axis_index("crop")
        me = crop_index * rows + row_index
        count_rows, width = pair.shape[1], pair.shape[2]
        length = crop_len[0]
        columns = jnp.arange(width, dtype=jnp.int32)
        valid_col = columns < length
        valid_row = row_index * count_rows + jnp.arange(count_rows, dtype=jnp.int32) < length
        mask = (valid_row[:, None] & valid_col[None, :] & (neighbours[0] > 0)).astype(f32)
        kb = jnp.where(valid_col, 0.0, -1000000000.0 * LOG2E).astype(f32)[None, :]

        wide_size, down_size = wide.size, down.size
        stat_size = wide_rows.size + wide_cols.size + down_rows.size + down_cols.size
        count = jnp.sum(mask)
        digit = jnp.floor(count * (1.0 / 128.0))
        sizes = wide_size + down_size
        pad = -(sizes + 2) % 1024
        packed = jnp.concatenate(
            [
                wide.astype(bf16).reshape(-1),
                down.astype(bf16).reshape(-1),
                jnp.stack([digit, count - 128.0 * digit]).astype(bf16),
                jnp.zeros((pad,), bf16),
            ]
        ).reshape(-1, 128)
        packs = gathered(packed, both, devices, all_masks)
        packs = jnp.take(packs, places(me, devices, all_masks), axis=0).reshape(devices, -1)
        wide_full = joined(packs[:, :wide_size], *wide.shape)
        down_full = joined(packs[:, wide_size:sizes], *down.shape)
        digits = packs[:, sizes : sizes + 2].astype(f32)
        pair_count = jnp.sum(digits[:, 0]) * 128.0 + jnp.sum(digits[:, 1])

        gain_wide = jnp.broadcast_to(gains[:, :, None], (3, CZ, width))
        w_bias = jnp.zeros((16, CZ), bf16).at[:HEADS].set(small[:, :HEADS].T.astype(bf16))
        zt, zbt, bias_part = front(pair[0], gain_wide[0], w_bias)
        bias = gathered(bias_part.transpose(1, 0, 2), "row", rows, row_masks)
        order = places(row_index, rows, row_masks)
        if count_rows % 8:
            bias = jnp.take(bias, order, axis=0).transpose(1, 0, 2, 3)
            bias = bias.reshape(1, HEADS, width, width)
            order = jnp.zeros((1,), jnp.int32)

        p, qkvd, dgt, dd, d_out, d_in, d_down, d_head, loss = middle(
            order,
            (1.0 / pair_count).reshape(1),
            bias,
            kb,
            wide_full,
            down_full,
            small[:, HEADS:].astype(bf16),
            gain_wide[1],
            gain_wide[2],
            zt,
            zbt,
            targets[0][:, None, :],
            mask[:, None, :],
        )
        d_bias, d_qkvg = back(p, qkvd, dgt, dd, zbt)

        parts = d_bias.reshape(HEADS, rows, count_rows, width).transpose(1, 0, 2, 3)
        parts = lax.all_to_all(parts, "row", 0, 0, tiled=True)
        mine = jnp.sum(parts.astype(f32), 0).astype(bf16)
        d_pbias = lax.dot_general(
            mine, zbt, (((1, 2), (0, 2)), ((), ())), preferred_element_type=f32
        )

        blocks = jnp.concatenate(
            [split(jnp.concatenate([d_qkvg, d_out, d_in], 1)), split(d_down.T)], 1
        ).astype(bf16)
        blocks = jnp.pad(blocks, ((0, 0), (0, -sizes % 128)))
        own = lax.all_to_all(blocks.reshape(devices, -1, 128), both, 0, 0, tiled=True)
        own = jnp.sum(own.astype(f32), 0)
        grads = gathered(own.astype(bf16), both, devices, all_masks)
        grads = jnp.take(grads, places(me, devices, all_masks), axis=0)
        grads = grads.reshape(devices, -1).astype(f32)
        own = own.reshape(-1)
        wide_g = own[:wide_size].reshape(wide.shape)
        down_g = own[wide_size:sizes].reshape(down.shape)
        wide_all = joined(grads[:, :wide_size], *wide.shape)
        down_all = joined(grads[:, wide_size:sizes], *down.shape)

        few = jnp.concatenate(
            [
                d_head[:BINS] + d_head[BINS:],
                d_pbias,
                jnp.broadcast_to(jnp.sum(loss), (4, CZ)),
            ],
            0,
        )
        few = summed(few, both, devices, all_masks)
        small_grad = jnp.concatenate([few[BINS : BINS + HEADS], few[:BINS]], 0).T
        loss_sum = few[BINS + HEADS, 0]

        stats = jnp.concatenate([wide_rows, wide_cols, down_rows, down_cols])
        stats = gathered(
            jnp.pad(stats, (0, -stat_size % 128)).reshape(-1, 128), both, devices, all_masks
        )
        stats = jnp.take(stats, places(me, devices, all_masks), axis=0).reshape(crops, rows, -1)
        ends = [0, wide_rows.size]
        for part in (wide_cols, down_rows, down_cols):
            ends.append(ends[-1] + part.size)
        wide_rows_all = stats[0, :, ends[0] : ends[1]].reshape(-1)
        wide_cols_all = stats[:, 0, ends[1] : ends[2]].reshape(-1)
        down_rows_all = stats[0, :, ends[2] : ends[3]].reshape(-1)
        down_cols_all = stats[:, 0, ends[3] : ends[4]].reshape(-1)

        wide_w = wide_full.astype(f32)
        small_w = rounded(small)
        through = wide_all * wide_w
        behind = small_grad * small_w
        gain_grad = (
            jnp.stack(
                [
                    jnp.sum(through[:, : 4 * CZ], 1) + jnp.sum(behind[:, :HEADS], 1),
                    jnp.sum(through[:, 5 * CZ :], 1),
                    jnp.sum(behind[:, HEADS:], 1),
                ]
            )
            / gains
        )

        wide_r_new, wide_c_new, wide_new = factored(
            wide_all,
            wide_rows_all,
            wide_cols_all,
            wide_g,
            wide,
            row_index * wide.shape[0],
            crop_index * wide.shape[1],
        )
        down_r_new, down_c_new, down_new = factored(
            down_all,
            down_rows_all,
            down_cols_all,
            down_g,
            down,
            row_index * down.shape[0],
            crop_index * down.shape[1],
        )
        gain_s, gain_n = plain(gains, gain_grad, gain_second, 0.3)
        small_s, small_n = plain(small, small_grad, small_second, 0.03)
        return (
            loss_sum,
            pair_count,
            wide_g,
            wide_r_new,
            wide_c_new,
            wide_new,
            down_g,
            down_r_new,
            down_c_new,
            down_new,
            gain_grad,
            gain_s,
            gain_n,
            small_grad,
            small_s,
            small_n,
        )

    return body


def solution(mesh):
    return jax.shard_map(
        build(mesh.shape["crop"], mesh.shape["row"]),
        mesh=mesh,
        in_specs=(
            P("crop", "row", None, None),
            P("crop"),
            P("crop", "row", None),
            P("crop", "row", None),
            P("row", "crop"),
            P("row"),
            P("crop"),
            P("row", "crop"),
            P("row"),
            P("crop"),
            P(),
            P(),
            P(),
            P(),
        ),
        out_specs=(
            P(),
            P(),
            P("row", "crop"),
            P("row"),
            P("crop"),
            P("row", "crop"),
            P("row", "crop"),
            P("row"),
            P("crop"),
            P("row", "crop"),
            P(),
            P(),
            P(),
            P(),
            P(),
            P(),
        ),
        check_vma=False,
    )
```

```python
import math
from functools import partial

import jax
import jax.numpy as jnp
from jax import lax
from jax.experimental import pallas as pl
from jax.experimental.pallas import tpu as pltpu
from jax.sharding import PartitionSpec as P

CZ = 128
HEADS = 4
HEAD_DIM = 32
FF = 512
BINS = 64
WIDE = 5 * CZ + FF

DECAY = 1.0 - 10.0 ** (-0.8)
TINY = 1e-30
LOG2E = math.log2(math.e)
ROOT = 1.0 / math.sqrt(HEAD_DIM)
BLK = 256
SAFE = 40.0

GATE_BLOCK, OUT_BLOCK, IN_BLOCK, DOWN_BLOCK, HEAD_BLOCK, BLOCKS = 0, 1, 2, 6, 10, 12

f32 = jnp.float32
bf16 = jnp.bfloat16


def dot(a, b):
    return lax.dot_general(a, b, (((1,), (0,)), ((), ())), preferred_element_type=f32)


def dot_nt(a, b):
    return lax.dot_general(a, b, (((1,), (1,)), ((), ())), preferred_element_type=f32)


def rounded(v):
    return v.astype(bf16).astype(f32)


def halves(v):
    high = v.astype(bf16)
    return high, (v - high.astype(f32)).astype(bf16)


def normed(x):
    centre = x - jnp.sum(x, 0, keepdims=True) * (1.0 / CZ)
    var = jnp.sum(centre * centre, 0, keepdims=True) * (1.0 / CZ)
    inv = lax.rsqrt(var + 1e-05)
    return centre * inv, inv


def normed_back(d, xhat, inv):
    one = jnp.sum(d, 0, keepdims=True) * (1.0 / CZ)
    two = jnp.sum(d * xhat, 0, keepdims=True) * (1.0 / CZ)
    return inv * (d - one - xhat * two)


def sigmoid(x):
    return 0.5 * jnp.tanh(0.5 * x) + 0.5


def wider(column, x):
    return jnp.concatenate([column] * (x.shape[1] // 128), 1)


def lanes(ref):
    return jnp.concatenate([ref[g] for g in range(ref.shape[0])], 1)


def spread(ref, x):
    width = ref.shape[2]
    for g in range(ref.shape[0]):
        ref[g] = x[:, g * width : (g + 1) * width]


def columns_of(gains_ref, which, scratch):
    scratch[...] = jnp.broadcast_to(gains_ref[...].T[:, which : which + 1], (CZ, CZ))


def place(source, me, masks):
    apart = source ^ me
    where = 0
    for t, mask in enumerate(masks):
        where = where + ((apart >> (mask.bit_length() - 1)) & 1) * (1 << t)
    return where


def front_kernel(
    pair_ref,
    gains_ref,
    small_ref,
    wide_ref,
    down_ref,
    stats_ref,
    zt_ref,
    zbt_ref,
    bias_ref,
    pack_ref,
    gain,
    wb,
    part,
    pack,
):
    rows, width, _ = pair_ref.shape
    step = pl.program_id(0)

    @pl.when(step == 0)
    def _():
        columns_of(gains_ref, 0, gain)
        wb[...] = small_ref[:16].astype(bf16)
        lines, cols = wide_ref.shape
        span = down_ref.shape[1]
        pack[...] = jnp.zeros_like(pack)
        pack[:lines, :cols] = wide_ref[...]
        for at in range(FF // CZ):
            pack[:lines, cols + at * span : cols + (at + 1) * span] = down_ref[
                at * lines : (at + 1) * lines, :
            ]
        after = cols + (FF // CZ) * span
        stats = stats_ref[...]
        upper = rounded(stats)
        pack[0:1, after : after + stats.shape[1]] = upper
        pack[1:2, after : after + stats.shape[1]] = stats - upper
        pack_ref[...] = pack[...].astype(bf16)

    x = pair_ref[...].astype(f32).reshape(rows * width, CZ).T
    spread(zt_ref, x.astype(bf16))
    xhat, _ = normed(x)
    zb = (xhat * wider(gain[...], x)).astype(bf16)
    spread(zbt_ref, zb)
    bias = dot(wb[...], zb)
    for g in range(rows):
        for h in range(HEADS):
            part[h, pl.ds(step * rows + g, 1), :] = bias[h : h + 1, g * width : (g + 1) * width]

    @pl.when(step == pl.num_programs(0) - 1)
    def _():
        bias_ref[...] = part[...].astype(bf16)


def project_kernel(
    crops,
    rows,
    masks,
    info_ref,
    packs_ref,
    zbt_ref,
    qkv_ref,
    gate_ref,
    kvn_ref,
    norm_ref,
    wide_ref,
    down_ref,
    wide_s,
    down_s,
    wqt,
):
    lines, cols, span = CZ // rows, WIDE // crops, CZ // crops

    @pl.when(pl.program_id(0) == 0)
    def _():
        me = info_ref[1] * rows + info_ref[0]
        for c in range(crops):
            for r in range(rows):
                block = packs_ref[place(c * rows + r, me, masks)].astype(f32)[:lines]
                wide_s[r * lines : (r + 1) * lines, c * cols : (c + 1) * cols] = block[:, :cols]
                for part in range(FF // CZ):
                    at = (r * (FF // CZ) + part) * lines
                    down_s[at : at + lines, c * span : (c + 1) * span] = block[
                        :, cols + part * span : cols + (part + 1) * span
                    ]
        wide_ref[...] = wide_s[...].astype(bf16)
        down_ref[...] = down_s[...].astype(bf16)
        wqt[...] = wide_s[:, : 4 * CZ].T.astype(bf16)

    proj = dot(wqt[...], lanes(zbt_ref))
    qkv = proj[: 3 * CZ].astype(bf16)
    spread(qkv_ref, qkv)
    spread(gate_ref, sigmoid(proj[3 * CZ :]))
    q = qkv[:CZ].astype(f32)
    k = qkv[CZ : 2 * CZ].astype(f32)
    kvn_ref[...] = qkv[CZ:].T.reshape(kvn_ref.shape)
    norm_ref[...] = jnp.concatenate(
        [
            jnp.sum((x * x)[h * HEAD_DIM : (h + 1) * HEAD_DIM], 0, keepdims=True)
            for x in (q, k)
            for h in range(HEADS)
        ],
        0,
    )


def attend_kernel(
    masks,
    info_ref,
    norm_ref,
    bias_ref,
    q_ref,
    kn_ref,
    v_ref,
    p_ref,
    o_ref,
    r_ref,
    biast,
    nat,
    qbd,
    kk,
    bound,
):
    group, _, width = q_ref.shape
    shards, _, rows, _ = bias_ref.shape
    step = pl.program_id(0)

    @pl.when(step == 0)
    def _():
        top = 0.0
        key = lax.broadcasted_iota(jnp.int32, (1, width), 1)
        kb = jnp.where(key < info_ref[2], 0.0, -1000000000.0 * LOG2E)
        for h in range(HEADS):
            for s in range(shards):
                nat[s * rows : (s + 1) * rows, :] = bias_ref[place(s, info_ref[0], masks), h].astype(f32)
            top = jnp.maximum(top, jnp.max(jnp.abs(nat[...])))
            biast[:, h * width : (h + 1) * width] = (nat[...] * LOG2E + kb).T
        bound[0] = top * LOG2E
        qbd[...] = jnp.zeros_like(qbd)
        r_ref[...] = jnp.zeros_like(r_ref)

    def attend(shift):
        for g in range(group):
            high, low = halves(q_ref[g].astype(f32) * (LOG2E * ROOT))
            for h in range(HEADS):
                a, b = h * HEAD_DIM, (h + 1) * HEAD_DIM
                qbd[g, a:b, h * width : (h + 1) * width] = high[a:b]
                qbd[g, CZ + a : CZ + b, h * width : (h + 1) * width] = low[a:b]
            kk[g, :, :CZ] = kn_ref[g]
            kk[g, :, CZ:] = kn_ref[g]
            sums = []
            for c in range(0, HEADS * width, BLK):
                s = dot(kk[g], qbd[g, :, c : c + BLK]) + biast[:, c : c + BLK]
                if shift:
                    s = s - jnp.max(s, 0, keepdims=True)
                e = jnp.exp2(s)
                sums.append(jnp.sum(e, 0, keepdims=True))
                p_ref[g, :, c : c + BLK] = e.astype(bf16)
            r = 1.0 / jnp.concatenate(sums, 1)
            for h in range(HEADS):
                a, b = h * HEAD_DIM, (h + 1) * HEAD_DIM
                mine = r[:, h * width : (h + 1) * width]
                r_ref[g, h : h + 1] = mine
                o_ref[g, a:b] = dot(v_ref[g, a:b], p_ref[g, :, h * width : (h + 1) * width]) * mine

    norms = jnp.max(norm_ref[...], 1, keepdims=True)
    reach = jnp.max(jnp.sqrt(norms[:HEADS] * norms[HEADS:])) * (1.01 * LOG2E * ROOT)
    safe = reach + bound[0] < SAFE

    @pl.when(safe)
    def _():
        attend(False)

    @pl.when(jnp.logical_not(safe))
    def _():
        attend(True)


def middle_kernel(
    info_ref,
    wide_ref,
    down_ref,
    head_ref,
    gains_ref,
    zt_ref,
    zbt_ref,
    o_ref,
    gate_ref,
    r_ref,
    tgt_ref,
    nbr_ref,
    do_ref,
    nd_ref,
    grads_ref,
    scalars_ref,
    acc,
    sums,
    g1,
    g2,
    wot,
    wint,
    wdownt,
    wht,
    wo2,
    wdown2,
    wh2,
):
    step = pl.program_id(0)

    @pl.when(step == 0)
    def _():
        wo = wide_ref[:, 4 * CZ : 5 * CZ]
        wot[...] = wo.T
        wint[...] = wide_ref[:, 5 * CZ :].T
        wdownt[...] = down_ref[...].T
        head = head_ref[...][HEADS:]
        wht[...] = head.astype(bf16)
        head = head.T.astype(bf16)
        wo2[...] = jnp.concatenate([wo, wo], 1)
        wdown2[...] = jnp.concatenate([down_ref[...], down_ref[...]], 1)
        wh2[...] = jnp.concatenate([head, head], 1)
        acc[...] = jnp.zeros_like(acc)
        columns_of(gains_ref, 1, g1)
        columns_of(gains_ref, 2, g2)
        sums[...] = jnp.zeros_like(sums)

    o = lanes(o_ref)
    gate = lanes(gate_ref)
    gain1 = wider(g1[...], o)
    gain2 = wider(g2[...], o)

    def add(block, grad):
        for c in range(0, grad.shape[1], CZ):
            acc[block + c // CZ] += grad[:, c : c + CZ]

    og = (o * gate).astype(bf16)
    z1 = lanes(zt_ref).astype(f32) + dot(wot[...], og)
    xhat1, inv1 = normed(z1)
    zb2 = (xhat1 * gain1).astype(bf16)
    hidden, slopes = [], []
    for f in range(0, FF, CZ):
        hid = dot(wint[f : f + CZ], zb2)
        sg = sigmoid(hid)
        act = hid * sg
        hidden.append(act.astype(bf16))
        slopes.append(sg + act * (1.0 - sg))
    a = jnp.concatenate(hidden, 0)
    z2 = z1 + dot(wdownt[...], a)
    xhat2, inv2 = normed(z2)
    zb3 = (xhat2 * gain2).astype(bf16)
    logits = dot(wht[...], zb3)
    top = jnp.max(logits, 0, keepdims=True)
    ex = jnp.exp(logits - top)
    total = jnp.sum(ex, 0, keepdims=True)
    group, _, width = o_ref.shape
    first = step * group
    target = jnp.concatenate([tgt_ref[0, pl.ds(first + g, 1), :] for g in range(group)], 1)
    hot = lax.broadcasted_iota(jnp.int32, logits.shape, 0) == target
    picked = jnp.sum(jnp.where(hot, logits, 0.0), 0, keepdims=True)
    column = lax.broadcasted_iota(jnp.int32, (1, width), 1)
    length = info_ref[2]
    mask = jnp.concatenate(
        [
            jnp.where(
                (nbr_ref[0, pl.ds(first + g, 1), :] > 0)
                & (column < jnp.where(info_ref[0] * info_ref[3] + first + g < length, length, 0)),
                1.0,
                0.0,
            )
            for g in range(group)
        ],
        1,
    )
    sums[0:1] += (jnp.log(total) + top - picked) * mask
    sums[1:2] += mask

    dl = ex * (mask / total) - jnp.where(hot, mask, 0.0)
    dl2 = jnp.concatenate(halves(dl), 0)
    add(HEAD_BLOCK, dot_nt(dl2, zb3))
    dzb3 = rounded(dot(wh2[...], dl2))
    dz2 = normed_back(dzb3 * gain2, xhat2, inv2)
    high2, low2 = halves(dz2)
    both2 = jnp.concatenate([high2, low2], 0)
    dh = jnp.concatenate(
        [
            (dot(wdown2[f : f + CZ], both2) * slopes[f // CZ]).astype(bf16)
            for f in range(0, FF, CZ)
        ],
        0,
    )
    add(DOWN_BLOCK, dot_nt(high2, a))
    dzb2 = rounded(dot(wide_ref[:, 5 * CZ :], dh))
    add(IN_BLOCK, dot_nt(zb2, dh))
    dz1 = dz2 + normed_back(dzb2 * gain1, xhat1, inv1)
    high1, low1 = halves(dz1)
    add(OUT_BLOCK, dot_nt(og, high1))
    dog = rounded(dot(wo2[...], jnp.concatenate([high1, low1], 0)))
    do = dog * gate
    doo = do * o
    add(GATE_BLOCK, dot_nt(lanes(zbt_ref), (doo * (1.0 - gate)).astype(bf16)))
    r = lanes(r_ref)
    parts, minus = [], []
    for h in range(HEADS):
        x, y = h * HEAD_DIM, (h + 1) * HEAD_DIM
        mine = r[h : h + 1]
        parts.append((do[x:y] * mine).astype(bf16))
        less = -jnp.sum(doo[x:y], 0, keepdims=True) * mine
        upper = rounded(less)
        minus.append(
            jnp.concatenate([upper, less - upper, jnp.zeros((14, less.shape[1]), f32)], 0)
        )
    spread(do_ref, jnp.concatenate(parts, 0))
    spread(nd_ref, jnp.concatenate(minus, 0).astype(bf16))

    @pl.when(step == pl.num_programs(0) - 1)
    def _():
        for block in range(BLOCKS):
            grads_ref[block] = acc[block].astype(bf16)
        both = jnp.sum(sums[...], 1, keepdims=True)
        lane = lax.broadcasted_iota(jnp.int32, scalars_ref.shape, 1)
        out = jnp.zeros(scalars_ref.shape, f32)
        for part in range(3):
            upper = rounded(both)
            for which in range(2):
                out = jnp.where(lane == 2 * part + which, upper[which : which + 1], out)
            both = both - upper
        scalars_ref[...] = out.astype(bf16)


def score_kernel(p_ref, vn_ref, do_ref, nd_ref, dbias_ref, acc, dobd, vv):
    group, _, width = do_ref.shape
    step = pl.program_id(0)

    @pl.when(step == 0)
    def _():
        acc[...] = jnp.zeros_like(acc)
        prepare(dobd, vv)

    for g in range(group):
        score_operands(g, vn_ref, do_ref, nd_ref, dobd, vv)
        for c in range(0, HEADS * width, BLK):
            acc[:, c : c + BLK] += dot(vv[g], dobd[g, :, c : c + BLK]) * p_ref[
                g, :, c : c + BLK
            ].astype(f32)

    @pl.when(step == pl.num_programs(0) - 1)
    def _():
        owners, _, lines, _ = dbias_ref.shape
        for h in range(HEADS):
            mine = acc[:, h * width : (h + 1) * width].T
            for r in range(owners):
                dbias_ref[r, h] = mine[r * lines : (r + 1) * lines].astype(bf16)


def prepare(dobd, vv):
    dobd[...] = jnp.zeros_like(dobd)
    vv[...] = jnp.ones_like(vv)


def score_operands(g, vn_ref, do_ref, nd_ref, dobd, vv):
    width = do_ref.shape[2]
    vv[g, :, :CZ] = vn_ref[g]
    for h in range(HEADS):
        a, b = h * HEAD_DIM, (h + 1) * HEAD_DIM
        at = slice(h * width, (h + 1) * width)
        dobd[g, a:b, at] = do_ref[g, a:b]
        dobd[g, CZ : CZ + 16, at] = nd_ref[g, 16 * h : 16 * (h + 1)]


def back_kernel(
    p_ref, q_ref, k_ref, vn_ref, do_ref, nd_ref, zbt_ref, dwq_ref, dobd, dst, vv, dproj
):
    group, _, width = do_ref.shape

    @pl.when(pl.program_id(0) == 0)
    def _():
        dwq_ref[...] = jnp.zeros_like(dwq_ref)
        prepare(dobd, vv)

    for g in range(group):
        score_operands(g, vn_ref, do_ref, nd_ref, dobd, vv)
        for c in range(0, HEADS * width, BLK):
            ds = dot(vv[g], dobd[g, :, c : c + BLK]) * p_ref[g, :, c : c + BLK].astype(f32)
            dst[g, :, c : c + BLK] = ds.astype(bf16)
        at = slice(g * width, (g + 1) * width)
        for h in range(HEADS):
            a, b = h * HEAD_DIM, (h + 1) * HEAD_DIM
            mine = dst[g, :, h * width : (h + 1) * width]
            dproj[a:b, at] = (dot(k_ref[g, a:b], mine) * ROOT).astype(bf16)
            dproj[CZ + a : CZ + b, at] = (dot_nt(q_ref[g, a:b], mine) * ROOT).astype(bf16)
            dproj[2 * CZ + a : 2 * CZ + b, at] = dot_nt(
                do_ref[g, a:b], p_ref[g, :, h * width : (h + 1) * width]
            ).astype(bf16)
    grad = dot_nt(lanes(zbt_ref), dproj[...])
    for block in range(3):
        dwq_ref[block] += grad[:, block * CZ : (block + 1) * CZ]


def factored(grad_ref, rows, cols, weight_ref, crop, row_start, scratch, outs):
    grad_out, rows_out, cols_out, new_out = outs
    lines, span = weight_ref.shape
    grad = grad_ref[...]
    count, columns = grad.shape
    sq = grad * grad
    rows_new = DECAY * rows + (1.0 - DECAY) * (jnp.sum(sq, 1, keepdims=True) / columns + TINY)
    cols_new = DECAY * cols + (1.0 - DECAY) * (jnp.sum(sq, 0, keepdims=True) / count + TINY)
    mean = jnp.sum(rows_new, 0, keepdims=True) / count
    rows_factor = mean / rows_new
    cols_factor = 1.0 / cols_new
    size = jnp.sum(jnp.sum(sq * rows_factor * cols_factor, 1, keepdims=True), 0, keepdims=True)
    clip = jnp.maximum(0.1, jnp.sqrt(size / (count * columns)))
    scratch[...] = rows_factor
    mine = grad_ref[pl.ds(row_start, lines), :]
    update = mine * lax.rsqrt((1.0 / scratch[pl.ds(row_start, lines), :]) * (1.0 / cols_factor))
    update = weight_step(update, clip)
    scratch[...] = rows_new
    own_rows = jnp.broadcast_to(scratch[pl.ds(row_start, lines), :], (lines, CZ))
    rows_out[...] = own_rows.T[:1]

    def own(x):
        part = x[:, :span]
        for c in range(1, columns // span):
            part = jnp.where(crop == c, x[:, c * span : (c + 1) * span], part)
        return part

    grad_out[...] = own(mine)
    cols_out[...] = own(cols_new)
    new_out[...] = weight_ref[...] - own(update)


def weight_step(update, clip):
    return update * (0.03 / clip)


def plain(weight, grad, second, rate, outs):
    second_new = DECAY * second + (1.0 - DECAY) * (grad * grad + TINY)
    update = grad * lax.rsqrt(second_new)
    square = jnp.sum(jnp.sum(update * update, 1, keepdims=True), 0, keepdims=True)
    clip = jnp.maximum(1.0, jnp.sqrt(square / (grad.shape[0] * grad.shape[1])))
    outs[0][...] = grad
    outs[1][...] = second_new
    outs[2][...] = weight - rate * update / clip


def finish_kernel(
    info_ref,
    late_ref,
    early_ref,
    full_ref,
    wide_rows_ref,
    wide_cols_ref,
    down_rows_ref,
    down_cols_ref,
    wide_ref,
    down_ref,
    gains_ref,
    gain_second_ref,
    small_ref,
    small_second_ref,
    *refs,
):
    outs, (flat, wide_s, down_s, wide_c, down_c) = refs[:14], refs[14:]
    devices, lines, _ = early_ref.shape
    lines -= 16
    tail = jnp.zeros((1, CZ), f32)
    for d in range(devices):
        block = early_ref[d].astype(f32)
        flat[d * lines : (d + 1) * lines, :] = block[:lines]
        tail += block[lines : lines + 1]
    scale = 1.0 / (tail[:, 1:2] + tail[:, 3:4] + tail[:, 5:6])

    def early(block):
        return flat[block * CZ : (block + 1) * CZ, :] * scale

    for block in range(3):
        wide_s[:, block * CZ : (block + 1) * CZ] = (
            late_ref[block * CZ : (block + 1) * CZ, :] * scale
        )
    for block in range(GATE_BLOCK, DOWN_BLOCK):
        wide_s[:, (3 + block) * CZ : (4 + block) * CZ] = early(block)
    for block in range(DOWN_BLOCK, HEAD_BLOCK):
        down_s[(block - DOWN_BLOCK) * CZ : (block - DOWN_BLOCK + 1) * CZ, :] = early(block).T
    head = early(HEAD_BLOCK)
    pbias = late_ref[3 * CZ : 3 * CZ + 16, :] * scale
    small_grad = jnp.concatenate([pbias[:HEADS], head[:BINS] + head[BINS:]], 0)
    small = small_ref[...]
    plain(small, small_grad, small_second_ref[...], 0.03, outs[11:])

    through = wide_s[...] * full_ref[...].astype(f32)
    behind = small_grad * rounded(small)
    lane = lax.broadcasted_iota(jnp.int32, (CZ, CZ), 1)
    table = jnp.where(
        lane == 0,
        jnp.sum(through[:, : 4 * CZ], 1, keepdims=True),
        jnp.sum(through[:, 5 * CZ :], 1, keepdims=True),
    ).T
    table = jnp.concatenate(
        [
            table[:1] + jnp.sum(behind[:HEADS], 0, keepdims=True),
            table[1:2],
            jnp.sum(behind[HEADS:], 0, keepdims=True),
        ],
        0,
    )
    gains = gains_ref[...]
    plain(gains, table / gains, gain_second_ref[...], 0.3, outs[8:11])

    row, crop = info_ref[0], info_ref[1]
    factored(
        wide_s,
        wide_rows_ref[...],
        wide_cols_ref[...],
        wide_ref,
        crop,
        row * wide_ref.shape[0],
        wide_c,
        outs[:4],
    )
    factored(
        down_s,
        down_rows_ref[...],
        down_cols_ref[...],
        down_ref,
        crop,
        row * down_ref.shape[0],
        down_c,
        outs[4:8],
    )


def whole(shape):
    return pl.BlockSpec(shape, lambda i: (0,) * len(shape))


def rows_of(group, lines, columns, line=0, column=0):
    return pl.BlockSpec((group, lines, columns), lambda i: (i, line, column))


def of(shape, dtype):
    return jax.ShapeDtypeStruct(shape, dtype)


SMEM = pl.BlockSpec(memory_space=pltpu.SMEM)


def call(kernel, name, micros, grid, in_specs, outs, scratch, args):
    return pl.pallas_call(
        kernel,
        grid=(grid,),
        in_specs=in_specs,
        out_specs=[o[0] for o in outs],
        out_shape=[of(o[1], o[2]) for o in outs],
        scratch_shapes=scratch,
        compiler_params=pltpu.CompilerParams(vmem_limit_bytes=56 * 1024 * 1024),
        cost_estimate=pl.CostEstimate(
            flops=int(micros * 8e8), bytes_accessed=1 << 20, transcendentals=0
        ),
        name=name,
    )(*args)


def group_of(count, most):
    return next(g for g in range(most, 0, -1) if count % g == 0)


def front(pair, gains, small, wide, down, stats):
    count, width = pair.shape[0], pair.shape[1]
    columns = wide.shape[1] + (FF // CZ) * down.shape[1] + CZ
    g = group_of(count, 4)
    return call(
        front_kernel,
        "front",
        6,
        count // g,
        [rows_of(g, width, CZ)] + [whole(x.shape) for x in (gains, small, wide, down, stats)],
        [
            (rows_of(g, CZ, width), (count, CZ, width), bf16),
            (rows_of(g, CZ, width), (count, CZ, width), bf16),
            (whole((HEADS, count, width)), (HEADS, count, width), bf16),
            (whole((8, columns)), (8, columns), bf16),
        ],
        [
            pltpu.VMEM((CZ, CZ), f32),
            pltpu.VMEM((16, CZ), bf16),
            pltpu.VMEM((HEADS, count, width), f32),
            pltpu.VMEM((8, columns), f32),
        ],
        (pair, gains, small, wide, down, stats),
    )


def project(crops, rows, masks, info, packs, zbt):
    count, _, width = zbt.shape
    g = group_of(count, 4)
    return call(
        partial(project_kernel, crops, rows, masks),
        "project",
        8,
        count // g,
        [SMEM, whole(packs.shape), rows_of(g, CZ, width)],
        [
            (rows_of(g, 3 * CZ, width), (count, 3 * CZ, width), bf16),
            (rows_of(g, CZ, width), (count, CZ, width), f32),
            (rows_of(g, width, 2 * CZ), (count, width, 2 * CZ), bf16),
            (pl.BlockSpec((8, g * width), lambda i: (0, i)), (8, count * width), f32),
            (whole((CZ, WIDE)), (CZ, WIDE), bf16),
            (whole((FF, CZ)), (FF, CZ), bf16),
        ],
        [pltpu.VMEM((CZ, WIDE), f32), pltpu.VMEM((FF, CZ), f32), pltpu.VMEM((4 * CZ, CZ), bf16)],
        (info, packs, zbt),
    )


ATTEND_ROWS = 4
MIDDLE_ROWS = 4
SCORE_ROWS = 3
BACK_ROWS = 3


def attend(masks, info, norms, bias, kvn, qkv):
    count, _, width = qkv.shape
    g = group_of(count, ATTEND_ROWS)
    return call(
        partial(attend_kernel, masks),
        "attend",
        25,
        count // g,
        [
            SMEM,
            pl.BlockSpec((8, g * width), lambda i: (0, i)),
            whole(bias.shape),
            rows_of(g, CZ, width),
            rows_of(g, width, CZ),
            rows_of(g, CZ, width, 2),
        ],
        [
            (rows_of(g, width, HEADS * width), (count, width, HEADS * width), bf16),
            (rows_of(g, CZ, width), (count, CZ, width), f32),
            (rows_of(g, 8, width), (count, 8, width), f32),
        ],
        [
            pltpu.VMEM((width, HEADS * width), f32),
            pltpu.VMEM((width, width), f32),
            pltpu.VMEM((g, 2 * CZ, HEADS * width), bf16),
            pltpu.VMEM((g, width, 2 * CZ), bf16),
            pltpu.SMEM((1,), f32),
        ],
        (info, norms, bias, qkv, kvn, qkv),
    )


def middle(info, wide, down, small, gains, zt, zbt, o, gate, r, tgt, nbr):
    count, _, width = zt.shape
    g = group_of(count, MIDDLE_ROWS)
    return call(
        middle_kernel,
        "middle",
        30,
        count // g,
        [
            SMEM,
            whole((CZ, WIDE)),
            whole((FF, CZ)),
            whole(small.shape),
            whole(gains.shape),
            rows_of(g, CZ, width),
            rows_of(g, CZ, width),
            rows_of(g, CZ, width),
            rows_of(g, CZ, width),
            rows_of(g, 8, width),
            whole(tgt.shape),
            whole(nbr.shape),
        ],
        [
            (rows_of(g, CZ, width), (count, CZ, width), bf16),
            (rows_of(g, 16 * HEADS, width), (count, 16 * HEADS, width), bf16),
            (whole((BLOCKS, CZ, CZ)), (BLOCKS, CZ, CZ), bf16),
            (whole((16, CZ)), (16, CZ), bf16),
        ],
        [
            pltpu.VMEM((BLOCKS, CZ, CZ), f32),
            pltpu.VMEM((2, g * width), f32),
            pltpu.VMEM((CZ, CZ), f32),
            pltpu.VMEM((CZ, CZ), f32),
            pltpu.VMEM((CZ, CZ), bf16),
            pltpu.VMEM((FF, CZ), bf16),
            pltpu.VMEM((CZ, FF), bf16),
            pltpu.VMEM((BINS, CZ), bf16),
            pltpu.VMEM((CZ, 2 * CZ), bf16),
            pltpu.VMEM((FF, 2 * CZ), bf16),
            pltpu.VMEM((CZ, 2 * BINS), bf16),
        ],
        (info, wide, down, small, gains, zt, zbt, o, gate, r, tgt, nbr),
    )


def score(p, kvn, do, nd):
    count, _, width = do.shape
    g = group_of(count, SCORE_ROWS)
    shape = (width // count, HEADS, count, width)
    return call(
        score_kernel,
        "score",
        17,
        count // g,
        [
            rows_of(g, width, HEADS * width),
            rows_of(g, width, CZ, 0, 1),
            rows_of(g, CZ, width),
            rows_of(g, 16 * HEADS, width),
        ],
        [(whole(shape), shape, bf16)],
        [
            pltpu.VMEM((width, HEADS * width), f32),
            pltpu.VMEM((g, 2 * CZ, HEADS * width), bf16),
            pltpu.VMEM((g, width, 2 * CZ), bf16),
        ],
        (p, kvn, do, nd),
    )[0]


def back(p, qkv, kvn, do, nd, zbt):
    count, _, width = zbt.shape
    g = group_of(count, BACK_ROWS)
    return call(
        back_kernel,
        "back",
        38,
        count // g,
        [
            rows_of(g, width, HEADS * width),
            rows_of(g, CZ, width),
            rows_of(g, CZ, width, 1),
            rows_of(g, width, CZ, 0, 1),
            rows_of(g, CZ, width),
            rows_of(g, 16 * HEADS, width),
            rows_of(g, CZ, width),
        ],
        [(whole((3, CZ, CZ)), (3, CZ, CZ), f32)],
        [
            pltpu.VMEM((g, 2 * CZ, HEADS * width), bf16),
            pltpu.VMEM((g, width, HEADS * width), bf16),
            pltpu.VMEM((g, width, 2 * CZ), bf16),
            pltpu.VMEM((3 * CZ, g * width), bf16),
        ],
        (p, qkv, qkv, kvn, do, nd, zbt),
    )[0]


def finish(*args):
    wide, down, gains, small = args[8], args[9], args[10], args[12]
    shapes = []
    for weight in (wide, down):
        shapes += [weight.shape, (1, weight.shape[0]), (1, weight.shape[1]), weight.shape]
    shapes += [gains.shape] * 3 + [small.shape] * 3
    return call(
        finish_kernel,
        "finish",
        4,
        1,
        [SMEM] + [whole(x.shape) for x in args[1:]],
        [(whole(shape), shape, f32) for shape in shapes],
        [
            pltpu.VMEM((BLOCKS * CZ, CZ), f32),
            pltpu.VMEM((CZ, WIDE), f32),
            pltpu.VMEM((FF, CZ), f32),
            pltpu.VMEM((CZ, 1), f32),
            pltpu.VMEM((FF, 1), f32),
        ],
        args,
    )


def bits(n):
    return [1 << t for t in reversed(range(n.bit_length() - 1))]


def swap(x, axes, size, mask):
    return lax.ppermute(x, axes, [(i, i ^ mask) for i in range(size)])


def gathered(x, axes, size, masks):
    x = x[None]
    for mask in masks:
        x = jnp.concatenate([x, swap(x, axes, size, mask)], 0)
    return x


def places(me, size, masks):
    apart = jnp.arange(size, dtype=jnp.int32) ^ me
    place = jnp.zeros((size,), jnp.int32)
    for t, mask in enumerate(masks):
        place = place + jnp.where((apart & mask) != 0, 1 << t, 0)
    return place


def exact_halves(v):
    high = lax.reduce_precision(v, 8, 7)
    return high.astype(bf16), (v - high).astype(bf16)


def build(crops, rows):
    both = ("crop", "row")
    devices = crops * rows
    row_masks = bits(rows)
    all_masks = row_masks[:-1] + [m * rows for m in bits(crops)] + row_masks[-1:]

    def total(x, core):
        half = x.shape[0] // 2
        keep = lax.dynamic_slice_in_dim(x, core * half, half)
        give = lax.dynamic_slice_in_dim(x, (1 - core) * half, half)
        keep = keep + swap(give, both, devices, 1)
        for mask in all_masks[:-1]:
            keep = keep + swap(keep, both, devices, mask)
        other = swap(keep, both, devices, 1)
        first = core == 0
        return jnp.concatenate([jnp.where(first, keep, other), jnp.where(first, other, keep)], 0)

    def body(
        pair,
        crop_len,
        targets,
        neighbours,
        wide,
        wide_rows,
        wide_cols,
        down,
        down_rows,
        down_cols,
        gains,
        gain_second,
        small,
        small_second,
    ):
        row_index = lax.axis_index("row")
        crop_index = lax.axis_index("crop")
        count_rows, width = pair.shape[1], pair.shape[2]
        info = jnp.stack([row_index, crop_index, crop_len[0], jnp.int32(count_rows)])

        lines, cols = wide.shape
        cols_stat = jnp.concatenate([wide_cols, down_cols])
        cols_stat = jnp.pad(cols_stat, (0, -cols_stat.size % rows))
        share = cols_stat.size // rows
        stats = jnp.concatenate(
            [
                wide_rows,
                down_rows,
                lax.dynamic_slice_in_dim(cols_stat, row_index * share, share),
            ]
        )
        small_t = small.T
        zt, zbt, bias_part, pack = front(pair[0], gains, small_t, wide, down, stats[None, :])
        packs = gathered(pack, both, devices, all_masks)
        bias = gathered(bias_part, "row", rows, row_masks[:-1])
        qkv, gate, kvn, norms, wide_full, down_full = project(
            crops, rows, all_masks, info, packs, zbt
        )
        bias, norms = lax.optimization_barrier((bias, norms))
        bias = jnp.concatenate([bias, swap(bias, "row", rows, row_masks[-1])], 0)
        if count_rows % 8:
            bias = jnp.take(bias, places(row_index, rows, row_masks), axis=0)
            bias = bias.transpose(1, 0, 2, 3).reshape(1, HEADS, width, width)
        bias_masks = [] if count_rows % 8 else row_masks
        p, o, r = attend(bias_masks, info, norms, bias, kvn, qkv)
        do, nd, early, scalars = middle(
            info,
            wide_full,
            down_full,
            small_t,
            gains,
            zt,
            zbt,
            o,
            gate,
            r,
            targets,
            neighbours,
        )

        early = lax.all_to_all(early.reshape(devices, -1, CZ), both, 0, 0, tiled=True)
        d_bias = score(p, kvn, do, nd)
        early, d_bias = lax.optimization_barrier((early, d_bias))
        early = jnp.sum(early.astype(f32), 0).astype(bf16)
        early = jnp.concatenate([early, scalars], 0)
        early = jnp.broadcast_to(early[None], (devices, *early.shape))
        early, d_bias, do = lax.optimization_barrier((early, d_bias, do))
        early = lax.all_to_all(early, both, 0, 0, tiled=True)
        scalars = jnp.sum(early[:, -16, :6].astype(f32), 0).reshape(3, 2)
        loss_sum, pair_count = jnp.sum(scalars[:, 0]), jnp.sum(scalars[:, 1])

        d_bias = lax.all_to_all(d_bias, "row", 0, 0, tiled=True)
        d_qkv = back(p, qkv, kvn, do, nd, zbt)
        d_bias = jnp.sum(d_bias.astype(f32), 0).astype(bf16)
        d_pbias = lax.dot_general(
            d_bias, zbt, (((1, 2), (0, 2)), ((), ())), preferred_element_type=f32
        )
        late = total(
            jnp.concatenate(
                [d_qkv.reshape(3 * CZ, CZ), jnp.pad(d_pbias, ((0, 16 - HEADS), (0, 0)))], 0
            ),
            row_index & 1,
        )

        after = cols + (FF // CZ) * down.shape[1]
        extras = jnp.sum(packs[:, :2, after : after + stats.size].astype(f32), 1)
        extras = jnp.take(
            extras, places(crop_index * rows + row_index, devices, all_masks), axis=0
        )
        wide_rows_all = extras[:rows, :lines].reshape(-1)
        down_rows_all = extras[:rows, lines : lines + down_rows.size].reshape(-1)
        cols_all = extras[:, lines + down_rows.size :].reshape(crops, -1)
        wide_cols_all = cols_all[:, :cols].reshape(-1)
        down_cols_all = cols_all[:, cols : cols + down_cols.size].reshape(-1)

        (
            wide_g,
            wide_r_new,
            wide_c_new,
            wide_new,
            down_g,
            down_r_new,
            down_c_new,
            down_new,
            gain_grad,
            gain_s,
            gain_n,
            small_grad,
            small_s,
            small_n,
        ) = finish(
            info,
            late,
            early,
            wide_full,
            wide_rows_all[:, None],
            wide_cols_all[None, :],
            down_rows_all[:, None],
            down_cols_all[None, :],
            wide,
            down,
            gains,
            gain_second,
            small_t,
            small_second.T,
        )
        return (
            loss_sum,
            pair_count,
            wide_g,
            wide_r_new.reshape(-1),
            wide_c_new.reshape(-1),
            wide_new,
            down_g,
            down_r_new.reshape(-1),
            down_c_new.reshape(-1),
            down_new,
            gain_grad,
            gain_s,
            gain_n,
            small_grad.T,
            small_s.T,
            small_n.T,
        )

    return body


def solution(mesh):
    return jax.shard_map(
        build(mesh.shape["crop"], mesh.shape["row"]),
        mesh=mesh,
        in_specs=(
            P("crop", "row", None, None),
            P("crop"),
            P("crop", "row", None),
            P("crop", "row", None),
            P("row", "crop"),
            P("row"),
            P("crop"),
            P("row", "crop"),
            P("row"),
            P("crop"),
            P(),
            P(),
            P(),
            P(),
        ),
        out_specs=(
            P(),
            P(),
            P("row", "crop"),
            P("row"),
            P("crop"),
            P("row", "crop"),
            P("row", "crop"),
            P("row"),
            P("crop"),
            P("row", "crop"),
            P(),
            P(),
            P(),
            P(),
            P(),
            P(),
        ),
        check_vma=False,
    )
```

```python
import math
from functools import partial

import jax
import jax.numpy as jnp
from jax import lax
from jax.experimental import pallas as pl
from jax.experimental.pallas import tpu as pltpu
from jax.sharding import PartitionSpec as P

CZ = 128
HEADS = 4
HEAD_DIM = 32
FF = 512
BINS = 64
WIDE = 5 * CZ + FF

DECAY = 1.0 - 10.0 ** (-0.8)
TINY = 1e-30
LOG2E = math.log2(math.e)
ROOT = 1.0 / math.sqrt(HEAD_DIM)
BLK = 256
SAFE = 40.0
STATS = 256

GATE_BLOCK, OUT_BLOCK, IN_BLOCK, DOWN_BLOCK, HEAD_BLOCK, BLOCKS = 0, 1, 2, 6, 10, 12

f32 = jnp.float32
bf16 = jnp.bfloat16


def dot(a, b):
    return lax.dot_general(a, b, (((1,), (0,)), ((), ())), preferred_element_type=f32)


def dot_nt(a, b):
    return lax.dot_general(a, b, (((1,), (1,)), ((), ())), preferred_element_type=f32)


def rounded(v):
    return v.astype(bf16).astype(f32)


def halves(v):
    high = v.astype(bf16)
    return high, (v - high.astype(f32)).astype(bf16)


def normed(x):
    centre = x - jnp.sum(x, 0, keepdims=True) * (1.0 / CZ)
    var = jnp.sum(centre * centre, 0, keepdims=True) * (1.0 / CZ)
    inv = lax.rsqrt(var + 1e-05)
    return centre * inv, inv


def normed_back(d, xhat, inv):
    one = jnp.sum(d, 0, keepdims=True) * (1.0 / CZ)
    two = jnp.sum(d * xhat, 0, keepdims=True) * (1.0 / CZ)
    return inv * (d - one - xhat * two)


def sigmoid(x):
    return 0.5 * jnp.tanh(0.5 * x) + 0.5


def wider(column, x):
    return jnp.concatenate([column] * (x.shape[1] // 128), 1)


def lanes(ref):
    return jnp.concatenate([ref[g] for g in range(ref.shape[0])], 1)


def spread(ref, x):
    width = ref.shape[2]
    for g in range(ref.shape[0]):
        ref[g] = x[:, g * width : (g + 1) * width]


def columns_of(gains_ref, which, scratch):
    scratch[...] = jnp.broadcast_to(gains_ref[...].T[:, which : which + 1], (CZ, CZ))


def place(source, me, masks):
    apart = source ^ me
    where = 0
    for t, mask in enumerate(masks):
        where = where + ((apart >> (mask.bit_length() - 1)) & 1) * (1 << t)
    return where


def pack_kernel(
    wide_ref, down_ref, wide_rows_ref, down_rows_ref, wide_cols_ref, down_cols_ref, pack_ref, pack
):
    lines, cols = wide_ref.shape
    span = down_ref.shape[1]
    pack[...] = jnp.zeros_like(pack)
    for at, ref in ((0, wide_rows_ref), (lines, down_rows_ref)):
        some = ref[...].reshape(1, -1)
        upper = rounded(some)
        pack[0:1, at : at + some.shape[1]] = upper
        pack[1:2, at : at + some.shape[1]] = some - upper
    stats = jnp.concatenate(
        [wide_cols_ref[...].reshape(1, -1), down_cols_ref[...].reshape(1, -1)], 1
    )
    for part in range(-(-stats.shape[1] // STATS)):
        some = stats[:, part * STATS : (part + 1) * STATS]
        upper = rounded(some)
        pack[2 + part : 3 + part, : some.shape[1]] = upper
        pack[5 + part : 6 + part, : some.shape[1]] = some - upper
    pack[:lines, STATS : STATS + cols] = wide_ref[...]
    for part in range(FF // CZ):
        at = STATS + cols + part * span
        pack[:lines, at : at + span] = down_ref[part * lines : (part + 1) * lines, :]
    for peer in range(pack_ref.shape[0]):
        pack_ref[peer] = pack[...].astype(bf16)


def front_kernel(
    pair_ref, gains_ref, small_ref, zt_ref, zbt_ref, bias_ref, gain, wb, part
):
    rows, width, _ = pair_ref.shape
    step = pl.program_id(0)

    @pl.when(step == 0)
    def _():
        columns_of(gains_ref, 0, gain)
        wb[...] = small_ref[:16].astype(bf16)

    x = pair_ref[...].astype(f32).reshape(rows * width, CZ).T
    spread(zt_ref, x.astype(bf16))
    xhat, _ = normed(x)
    zb = (xhat * wider(gain[...], x)).astype(bf16)
    spread(zbt_ref, zb)
    bias = dot(wb[...], zb)
    for g in range(rows):
        for h in range(HEADS):
            part[h, pl.ds(step * rows + g, 1), :] = bias[h : h + 1, g * width : (g + 1) * width]

    @pl.when(step == pl.num_programs(0) - 1)
    def _():
        bias_ref[...] = part[...].astype(bf16)


def pick(info_ref, mine_ref, other_ref, crop, row, rows):
    chip = crop * (rows // 2) + row // 2
    side = info_ref[0] & 1
    return jnp.where(
        side == row % 2, mine_ref[chip].astype(f32), other_ref[chip].astype(f32)
    )


def project_kernel(
    crops,
    rows,
    info_ref,
    mine_ref,
    other_ref,
    zbt_ref,
    qkv_ref,
    vn_ref,
    norm_ref,
    wide_ref,
    down_ref,
    done_ref,
    wide_s,
    down_s,
    wqt,
):
    lines, cols, span = CZ // rows, WIDE // crops, CZ // crops

    @pl.when(pl.program_id(0) == 0)
    def _():
        for c in range(crops):
            for r in range(rows):
                block = pick(info_ref, mine_ref, other_ref, c, r, rows)[:lines]
                wide_s[r * lines : (r + 1) * lines, c * cols : (c + 1) * cols] = block[
                    :, STATS : STATS + cols
                ]
                for part in range(FF // CZ):
                    at = (r * (FF // CZ) + part) * lines
                    left = STATS + cols + part * span
                    down_s[at : at + lines, c * span : (c + 1) * span] = block[:, left : left + span]
        wide_ref[...] = wide_s[...].astype(bf16)
        down_ref[...] = down_s[...].astype(bf16)
        wqt[...] = wide_s[:, : 3 * CZ].T.astype(bf16)
        done_ref[...] = jnp.zeros_like(done_ref)

    qkv = dot(wqt[...], lanes(zbt_ref)).astype(bf16)
    spread(qkv_ref, qkv)
    q = qkv[:CZ].astype(f32)
    k = qkv[CZ : 2 * CZ].astype(f32)
    vn_ref[...] = qkv[2 * CZ :].T.reshape(vn_ref.shape)
    norm_ref[...] = jnp.concatenate(
        [
            jnp.sum((x * x)[h * HEAD_DIM : (h + 1) * HEAD_DIM], 0, keepdims=True)
            for x in (q, k)
            for h in range(HEADS)
        ],
        0,
    )


def attend_kernel(
    masks,
    info_ref,
    norm_ref,
    bias_ref,
    other_bias_ref,
    q_ref,
    k_ref,
    v_ref,
    p_ref,
    o_ref,
    r_ref,
    biast,
    nat,
    qbd,
    kk,
    bound,
):
    group, _, width = q_ref.shape
    rows = bias_ref.shape[2]
    shards = width // rows
    step = pl.program_id(0)

    @pl.when(step == 0)
    def _():
        top = 0.0
        key = lax.broadcasted_iota(jnp.int32, (1, width), 1)
        kb = jnp.where(key < info_ref[2], 0.0, -1000000000.0 * LOG2E)
        for h in range(HEADS):
            for s in range(shards):
                at = place(s, info_ref[0], masks[:-1])
                block = bias_ref[at, h].astype(f32)
                if shards > 1:
                    here = (info_ref[0] & 1) == s % 2
                    block = jnp.where(here, block, other_bias_ref[at, h].astype(f32))
                nat[s * rows : (s + 1) * rows, :] = block
            top = jnp.maximum(top, jnp.max(jnp.abs(nat[...])))
            biast[:, h * width : (h + 1) * width] = (nat[...] * LOG2E + kb).T
        bound[0] = top * LOG2E
        qbd[...] = jnp.zeros_like(qbd)
        r_ref[...] = jnp.zeros_like(r_ref)

    def attend(shift):
        for g in range(group):
            high, low = halves(q_ref[g].astype(f32) * (LOG2E * ROOT))
            for h in range(HEADS):
                a, b = h * HEAD_DIM, (h + 1) * HEAD_DIM
                qbd[g, a:b, h * width : (h + 1) * width] = high[a:b]
                qbd[g, CZ + a : CZ + b, h * width : (h + 1) * width] = low[a:b]
            kn = k_ref[g].T
            kk[g, :, :CZ] = kn
            kk[g, :, CZ:] = kn
            sums = []
            for c in range(0, HEADS * width, BLK):
                s = dot(kk[g], qbd[g, :, c : c + BLK]) + biast[:, c : c + BLK]
                if shift:
                    s = s - jnp.max(s, 0, keepdims=True)
                e = jnp.exp2(s)
                sums.append(jnp.sum(e, 0, keepdims=True))
                p_ref[g, :, c : c + BLK] = e.astype(bf16)
            r = 1.0 / jnp.concatenate(sums, 1)
            for h in range(HEADS):
                a, b = h * HEAD_DIM, (h + 1) * HEAD_DIM
                mine = r[:, h * width : (h + 1) * width]
                r_ref[g, h : h + 1] = mine
                o_ref[g, a:b] = dot(v_ref[g, a:b], p_ref[g, :, h * width : (h + 1) * width]) * mine

    norms = jnp.max(norm_ref[...], 1, keepdims=True)
    reach = jnp.max(jnp.sqrt(norms[:HEADS] * norms[HEADS:])) * (1.01 * LOG2E * ROOT)
    safe = reach + bound[0] < SAFE

    @pl.when(safe)
    def _():
        attend(False)

    @pl.when(jnp.logical_not(safe))
    def _():
        attend(True)


def middle_kernel(
    info_ref,
    wide_ref,
    down_ref,
    head_ref,
    gains_ref,
    zt_ref,
    zbt_ref,
    o_ref,
    r_ref,
    tgt_ref,
    nbr_ref,
    do_ref,
    nd_ref,
    grads_ref,
    scalars_ref,
    acc,
    sums,
    g1,
    g2,
    wgt,
    wot,
    wint,
    wdownt,
    wht,
    wo2,
    wdown2,
    wh2,
):
    step = pl.program_id(0)

    @pl.when(step == 0)
    def _():
        wo = wide_ref[:, 4 * CZ : 5 * CZ]
        wot[...] = wo.T
        wgt[...] = wide_ref[:, 3 * CZ : 4 * CZ].T
        wint[...] = wide_ref[:, 5 * CZ :].T * 0.5
        wdownt[...] = down_ref[...].T
        head = head_ref[...][HEADS:]
        wht[...] = head.astype(bf16)
        head = head.T.astype(bf16)
        wo2[...] = jnp.concatenate([wo, wo], 1)
        wdown2[...] = jnp.concatenate([down_ref[...], down_ref[...]], 1) * 0.5
        wh2[...] = jnp.concatenate([head, head], 1)
        acc[...] = jnp.zeros_like(acc)
        columns_of(gains_ref, 1, g1)
        columns_of(gains_ref, 2, g2)
        sums[...] = jnp.zeros_like(sums)

    group, _, width = o_ref.shape
    first = step * group

    def add(block, grad):
        for c in range(0, grad.shape[1], CZ):
            acc[block + c // CZ] += grad[:, c : c + CZ]

    def stages(low, high):
        spots = [divmod(block * 128, width) for block in range(low, high)]

        def mine(ref):
            return jnp.concatenate([ref[g, :, at : at + 128] for g, at in spots], 1)

        def line(ref):
            return jnp.concatenate(
                [ref[0, pl.ds(first + g, 1), :][:, at : at + 128] for g, at in spots], 1
            )

        def out(ref, x):
            for n, (g, at) in enumerate(spots):
                ref[g, :, at : at + 128] = x[:, n * 128 : (n + 1) * 128]

        o = mine(o_ref)
        zb = mine(zbt_ref)
        gate = sigmoid(dot(wgt[...], zb))
        gain1 = wider(g1[...], o)
        gain2 = wider(g2[...], o)
        og = (o * gate).astype(bf16)
        z1 = mine(zt_ref).astype(f32) + dot(wot[...], og)
        yield
        xhat1, inv1 = normed(z1)
        zb2 = (xhat1 * gain1).astype(bf16)
        yield
        hidden, slopes = [], []
        for f in range(0, FF, CZ):
            hid = dot(wint[f : f + CZ], zb2)
            t = jnp.tanh(hid)
            sg = 1.0 + t
            act = hid * sg
            hidden.append(act.astype(bf16))
            slopes.append(sg + act * (1.0 - t))
            yield
        a = jnp.concatenate(hidden, 0)
        z2 = z1 + dot(wdownt[...], a)
        yield
        xhat2, inv2 = normed(z2)
        zb3 = (xhat2 * gain2).astype(bf16)
        logits = dot(wht[...], zb3)
        yield
        top = jnp.max(logits, 0, keepdims=True)
        ex = jnp.exp(logits - top)
        total = jnp.sum(ex, 0, keepdims=True)
        hot = lax.broadcasted_iota(jnp.int32, logits.shape, 0) == line(tgt_ref)
        picked = jnp.sum(jnp.where(hot, logits, 0.0), 0, keepdims=True)
        column = lax.broadcasted_iota(jnp.int32, (1, 128), 1)
        length = info_ref[2]
        valid = jnp.concatenate(
            [
                column + at < jnp.where(info_ref[0] * info_ref[3] + first + g < length, length, 0)
                for g, at in spots
            ],
            1,
        )
        mask = jnp.where((line(nbr_ref) > 0) & valid, 1.0, 0.0)
        at = slice(0, mask.shape[1])
        sums[0:1, at] += (jnp.log(total) + top - picked) * mask
        sums[1:2, at] += mask
        dl = ex * (mask / total) - jnp.where(hot, mask, 0.0)
        dl2 = jnp.concatenate(halves(dl), 0)
        yield
        add(HEAD_BLOCK, dot_nt(dl2, zb3))
        dzb3 = rounded(dot(wh2[...], dl2))
        yield
        dz2 = normed_back(dzb3 * gain2, xhat2, inv2)
        high2, low2 = halves(dz2)
        both2 = jnp.concatenate([high2, low2], 0)
        yield
        dh = []
        for f in range(0, FF, CZ):
            dh.append((dot(wdown2[f : f + CZ], both2) * slopes[f // CZ]).astype(bf16))
            yield
        dh = jnp.concatenate(dh, 0)
        add(DOWN_BLOCK, dot_nt(high2, a))
        yield
        dzb2 = rounded(dot(wide_ref[:, 5 * CZ :], dh))
        yield
        add(IN_BLOCK, dot_nt(zb2, dh))
        dz1 = dz2 + normed_back(dzb2 * gain1, xhat1, inv1)
        high1, low1 = halves(dz1)
        yield
        add(OUT_BLOCK, dot_nt(og, high1))
        dog = rounded(dot(wo2[...], jnp.concatenate([high1, low1], 0)))
        yield
        do = dog * gate
        doo = do * o
        add(GATE_BLOCK, dot_nt(zb, (doo * (1.0 - gate)).astype(bf16)))
        yield
        r = mine(r_ref)
        parts, minus = [], []
        for h in range(HEADS):
            x, y = h * HEAD_DIM, (h + 1) * HEAD_DIM
            share = r[h : h + 1]
            parts.append((do[x:y] * share).astype(bf16))
            less = -jnp.sum(doo[x:y], 0, keepdims=True) * share
            upper = rounded(less)
            minus.append(
                jnp.concatenate([upper, less - upper, jnp.zeros((14, less.shape[1]), f32)], 0)
            )
        out(do_ref, jnp.concatenate(parts, 0))
        out(nd_ref, jnp.concatenate(minus, 0).astype(bf16))

    blocks = group * width // 128
    running = [
        stages(low, min(low + MIDDLE_PART, blocks)) for low in range(0, blocks, MIDDLE_PART)
    ]
    turn = 0
    waiting = list(enumerate(running))
    while waiting:
        for item in list(waiting):
            if turn >= item[0] * MIDDLE_LAG and next(item[1], item) is item:
                waiting.remove(item)
        turn += 1

    @pl.when(step == pl.num_programs(0) - 1)
    def _():
        for block in range(BLOCKS):
            grads_ref[block] = acc[block].astype(bf16)
        both = jnp.sum(sums[...], 1, keepdims=True)
        lane = lax.broadcasted_iota(jnp.int32, scalars_ref.shape, 1)
        out = jnp.zeros(scalars_ref.shape, f32)
        for part in range(3):
            upper = rounded(both)
            for which in range(2):
                out = jnp.where(lane == 2 * part + which, upper[which : which + 1], out)
            both = both - upper
        scalars_ref[...] = out.astype(bf16)


def score_kernel(info_ref, p_ref, vn_ref, do_ref, nd_ref, keep_ref, give_ref, acc, dobd, vv, nat):
    group, _, width = do_ref.shape
    step = pl.program_id(0)

    @pl.when(step == 0)
    def _():
        acc[...] = jnp.zeros_like(acc)
        prepare(dobd, vv)

    for g in range(group):
        score_operands(g, vn_ref, do_ref, nd_ref, dobd, vv)
        for c in range(0, HEADS * width, BLK):
            acc[:, c : c + BLK] += dot(vv[g], dobd[g, :, c : c + BLK]) * p_ref[
                g, :, c : c + BLK
            ].astype(f32)

    @pl.when(step == pl.num_programs(0) - 1)
    def _():
        chips, tall, _ = keep_ref.shape
        lines = width // (2 * chips)
        first = (info_ref[0] & 1) == 0
        for h in range(HEADS):
            nat[h] = acc[:, h * width : (h + 1) * width].T
        for chip in range(chips):
            sides = [
                jnp.concatenate(
                    [
                        nat[h, (2 * chip + side) * lines : (2 * chip + side + 1) * lines, c : c + CZ]
                        for c in range(0, width, CZ)
                        for h in range(HEADS)
                    ],
                    0,
                )
                for side in range(2)
            ]
            keep_ref[chip] = jnp.where(first, sides[0], sides[1]).astype(bf16)
            give_ref[chip] = jnp.where(first, sides[1], sides[0]).astype(bf16)


def prepare(dobd, vv):
    dobd[...] = jnp.zeros_like(dobd)
    vv[...] = jnp.ones_like(vv)


def score_operands(g, vn_ref, do_ref, nd_ref, dobd, vv):
    width = do_ref.shape[2]
    vv[g, :, :CZ] = vn_ref[g]
    for h in range(HEADS):
        a, b = h * HEAD_DIM, (h + 1) * HEAD_DIM
        at = slice(h * width, (h + 1) * width)
        dobd[g, a:b, at] = do_ref[g, a:b]
        dobd[g, CZ : CZ + 16, at] = nd_ref[g, 16 * h : 16 * (h + 1)]


def back_kernel(
    p_ref, q_ref, k_ref, vn_ref, do_ref, nd_ref, zbt_ref, dwq_ref, dobd, dst, vv, dproj
):
    group, _, width = do_ref.shape

    @pl.when(pl.program_id(0) == 0)
    def _():
        dwq_ref[...] = jnp.zeros_like(dwq_ref)
        prepare(dobd, vv)

    for g in range(group):
        score_operands(g, vn_ref, do_ref, nd_ref, dobd, vv)
        for c in range(0, HEADS * width, BLK):
            ds = dot(vv[g], dobd[g, :, c : c + BLK]) * p_ref[g, :, c : c + BLK].astype(f32)
            dst[g, :, c : c + BLK] = ds.astype(bf16)
        at = slice(g * width, (g + 1) * width)
        for h in range(HEADS):
            a, b = h * HEAD_DIM, (h + 1) * HEAD_DIM
            mine = dst[g, :, h * width : (h + 1) * width]
            dproj[a:b, at] = (dot(k_ref[g, a:b], mine) * ROOT).astype(bf16)
            dproj[CZ + a : CZ + b, at] = (dot_nt(q_ref[g, a:b], mine) * ROOT).astype(bf16)
            dproj[2 * CZ + a : 2 * CZ + b, at] = dot_nt(
                do_ref[g, a:b], p_ref[g, :, h * width : (h + 1) * width]
            ).astype(bf16)
    grad = dot_nt(lanes(zbt_ref), dproj[...])
    for block in range(3):
        dwq_ref[block] += grad[:, block * CZ : (block + 1) * CZ]


def factored(grad_ref, rows, cols, weight_ref, crop, row_start, scratch, outs):
    grad_out, rows_out, cols_out, new_out = outs
    lines, span = weight_ref.shape
    grad = grad_ref[...]
    count, columns = grad.shape
    sq = grad * grad
    rows_new = DECAY * rows + (1.0 - DECAY) * (jnp.sum(sq, 1, keepdims=True) / columns + TINY)
    cols_new = DECAY * cols + (1.0 - DECAY) * (jnp.sum(sq, 0, keepdims=True) / count + TINY)
    mean = jnp.sum(rows_new, 0, keepdims=True) / count
    rows_factor = mean / rows_new
    cols_factor = 1.0 / cols_new
    size = jnp.sum(jnp.sum(sq * rows_factor * cols_factor, 1, keepdims=True), 0, keepdims=True)
    clip = jnp.maximum(0.1, jnp.sqrt(size / (count * columns)))
    scratch[...] = rows_factor
    mine = grad_ref[pl.ds(row_start, lines), :]
    update = mine * lax.rsqrt((1.0 / scratch[pl.ds(row_start, lines), :]) * (1.0 / cols_factor))
    update = weight_step(update, clip)
    scratch[...] = rows_new
    own_rows = jnp.broadcast_to(scratch[pl.ds(row_start, lines), :], (lines, CZ))
    rows_out[...] = own_rows.T[0]

    def own(x):
        part = x[:, :span]
        for c in range(1, columns // span):
            part = jnp.where(crop == c, x[:, c * span : (c + 1) * span], part)
        return part

    grad_out[...] = own(mine)
    cols_out[...] = own(cols_new)[0]
    new_out[...] = weight_ref[...] - own(update)


def weight_step(update, clip):
    return update * (0.03 / clip)


def plain(weight, grad, second, rate, outs):
    second_new = DECAY * second + (1.0 - DECAY) * (grad * grad + TINY)
    update = grad * lax.rsqrt(second_new)
    square = jnp.sum(jnp.sum(update * update, 1, keepdims=True), 0, keepdims=True)
    clip = jnp.maximum(1.0, jnp.sqrt(square / (grad.shape[0] * grad.shape[1])))
    outs[0][...] = grad
    outs[1][...] = second_new
    outs[2][...] = weight - rate * update / clip


def finish_kernel(
    crops,
    rows,
    info_ref,
    keep_ref,
    other_ref,
    spread_ref,
    packs_ref,
    other_packs_ref,
    full_ref,
    wide_ref,
    down_ref,
    gains_ref,
    gain_second_ref,
    small_ref,
    small_second_ref,
    *refs,
):
    outs, (flat, late_ref, wide_s, down_s, wide_c, down_c, table, wide_cols, down_cols) = (
        refs[:14],
        refs[14:],
    )
    row, crop = info_ref[0], info_ref[1]
    side = row & 1
    half = keep_ref.shape[0]
    mine, other = keep_ref[...], other_ref[...]
    late_ref[:half, :] = jnp.where(side == 0, mine, other)
    late_ref[half:, :] = jnp.where(side == 0, other, mine)

    lines = BLOCKS * CZ // (crops * rows)
    height = lines + 16
    tail = jnp.zeros((1, CZ), f32)
    for c in range(crops):
        for r in range(rows):
            at = (c * rows + r) * lines
            which = ((r % 2) ^ side) + 2 * (c ^ crop)
            start = spread_ref.shape[1] - 2 * crops * height
            block = jnp.zeros((height, CZ), f32)
            for p in range(2 * crops):
                some = spread_ref[r // 2, start + p * height : start + (p + 1) * height]
                block = jnp.where(which == p, some.astype(f32), block)
            flat[at : at + lines, :] = block[:lines]
            tail += block[lines : lines + 1]
    scale = 1.0 / (tail[:, 1:2] + tail[:, 3:4] + tail[:, 5:6])

    def early(block):
        return flat[block * CZ : (block + 1) * CZ, :] * scale

    for block in range(3):
        wide_s[:, block * CZ : (block + 1) * CZ] = (
            late_ref[block * CZ : (block + 1) * CZ, :] * scale
        )
    for block in range(GATE_BLOCK, DOWN_BLOCK):
        wide_s[:, (3 + block) * CZ : (4 + block) * CZ] = early(block)
    for block in range(DOWN_BLOCK, HEAD_BLOCK):
        down_s[(block - DOWN_BLOCK) * CZ : (block - DOWN_BLOCK + 1) * CZ, :] = early(block).T
    head = early(HEAD_BLOCK)
    pbias = late_ref[3 * CZ : 3 * CZ + 16, :] * scale
    small_grad = jnp.concatenate([pbias[:HEADS], head[:BINS] + head[BINS:]], 0)
    small = small_ref[...]
    plain(small, small_grad, small_second_ref[...], 0.03, outs[11:])

    through = wide_s[...] * full_ref[...].astype(f32)
    behind = small_grad * rounded(small)
    lane = lax.broadcasted_iota(jnp.int32, (CZ, CZ), 1)
    gain_grad = jnp.where(
        lane == 0,
        jnp.sum(through[:, : 4 * CZ], 1, keepdims=True),
        jnp.sum(through[:, 5 * CZ :], 1, keepdims=True),
    ).T
    gain_grad = jnp.concatenate(
        [
            gain_grad[:1] + jnp.sum(behind[:HEADS], 0, keepdims=True),
            gain_grad[1:2],
            jnp.sum(behind[HEADS:], 0, keepdims=True),
        ],
        0,
    )
    gains = gains_ref[...]
    plain(gains, gain_grad / gains, gain_second_ref[...], 0.3, outs[8:11])

    per, down_per = CZ // rows, FF // rows
    for r in range(rows):
        block = pick(info_ref, packs_ref, other_packs_ref, 0, r, rows)
        table[r : r + 1, :] = block[0:1, :CZ] + block[1:2, :CZ]

    def column(size, start):
        tall = jnp.broadcast_to(table[...][:, None, :], (rows, size, CZ)).reshape(rows * size, CZ)
        lane = lax.broadcasted_iota(jnp.int32, tall.shape, 1)
        line = lax.broadcasted_iota(jnp.int32, tall.shape, 0)
        return jnp.sum(jnp.where(lane == start + line % size, tall, 0.0), 1, keepdims=True)

    cols, span = WIDE // crops, CZ // crops
    for c in range(crops):
        block = pick(info_ref, packs_ref, other_packs_ref, c, 0, rows)[:, :STATS]
        block = block[2:5] + block[5:8]
        stats = jnp.concatenate([block[part : part + 1] for part in range(3)], 1)
        wide_cols[:, c * cols : (c + 1) * cols] = stats[:, :cols]
        down_cols[:, c * span : (c + 1) * span] = stats[:, cols : cols + span]
    factored(
        wide_s,
        column(per, 0),
        wide_cols[...],
        wide_ref,
        crop,
        row * wide_ref.shape[0],
        wide_c,
        outs[:4],
    )
    factored(
        down_s,
        column(down_per, per),
        down_cols[...],
        down_ref,
        crop,
        row * down_ref.shape[0],
        down_c,
        outs[4:8],
    )


def late_kernel(info_ref, spread_ref, dqkv_ref, zbt_ref, keep_ref, give_ref, dbias, acc, stack):
    group, _, width = zbt_ref.shape
    tall = dbias.shape[0]
    lines = tall // (HEADS * (width // CZ))
    step = pl.program_id(0)

    @pl.when(step == 0)
    def _():
        total = spread_ref[0, :tall].astype(f32)
        for chip in range(1, spread_ref.shape[0]):
            total += spread_ref[chip, :tall].astype(f32)
        dbias[...] = rounded(total)
        acc[...] = jnp.zeros_like(acc)

    some = jnp.concatenate(
        [
            dbias[pl.ds(c * HEADS * lines + step * group + g, HEADS, stride=lines), :]
            for g in range(group)
            for c in range(width // CZ)
        ],
        1,
    )
    some = jnp.concatenate([some, jnp.zeros((16 - HEADS, some.shape[1]), f32)], 0)
    acc[...] += dot_nt(lanes(zbt_ref), some.astype(bf16))

    @pl.when(step == pl.num_programs(0) - 1)
    def _():
        for block in range(3):
            stack[block * CZ : (block + 1) * CZ, :] = dqkv_ref[block]
        stack[3 * CZ :, :] = acc[...].T
        half = keep_ref.shape[0]
        first = (info_ref[0] & 1) == 0
        one, two = stack[:half, :], stack[half:, :]
        keep_ref[...] = jnp.where(first, one, two)
        give_ref[...] = jnp.where(first, two, one)


def whole(shape):
    return pl.BlockSpec(shape, lambda i: (0,) * len(shape))


def rows_of(group, lines, columns, line=0, column=0):
    return pl.BlockSpec((group, lines, columns), lambda i: (i, line, column))


def of(shape, dtype):
    return jax.ShapeDtypeStruct(shape, dtype)


SMEM = pl.BlockSpec(memory_space=pltpu.SMEM)


def call(kernel, name, micros, grid, in_specs, outs, scratch, args):
    return pl.pallas_call(
        kernel,
        grid=(grid,),
        in_specs=in_specs,
        out_specs=[o[0] for o in outs],
        out_shape=[of(o[1], o[2]) for o in outs],
        scratch_shapes=scratch,
        compiler_params=pltpu.CompilerParams(vmem_limit_bytes=56 * 1024 * 1024),
        cost_estimate=pl.CostEstimate(
            flops=int(micros * 8e8), bytes_accessed=1 << 20, transcendentals=0
        ),
        name=name,
    )(*args)


def group_of(count, most):
    return next(g for g in range(most, 0, -1) if count % g == 0)


def pack_weights(peers, wide, down, *stats):
    args = (wide, down, *stats)
    shape = (peers, 8, STATS + wide.shape[1] + (FF // CZ) * down.shape[1])
    return call(
        pack_kernel,
        "pack",
        1,
        1,
        [whole(x.shape) for x in args],
        [(whole(shape), shape, bf16)],
        [pltpu.VMEM(shape[1:], f32)],
        args,
    )[0]


def front(pair, gains, small):
    count, width = pair.shape[0], pair.shape[1]
    g = group_of(count, FRONT_ROWS)
    return call(
        front_kernel,
        "front",
        6,
        count // g,
        [rows_of(g, width, CZ), whole(gains.shape), whole(small.shape)],
        [
            (rows_of(g, CZ, width), (count, CZ, width), bf16),
            (rows_of(g, CZ, width), (count, CZ, width), bf16),
            (whole((HEADS, count, width)), (HEADS, count, width), bf16),
        ],
        [
            pltpu.VMEM((CZ, CZ), f32),
            pltpu.VMEM((16, CZ), bf16),
            pltpu.VMEM((HEADS, count, width), f32),
        ],
        (pair, gains, small),
    )


def project(crops, rows, info, mine, other, zbt):
    count, _, width = zbt.shape
    g = group_of(count, 6)
    return call(
        partial(project_kernel, crops, rows),
        "project",
        40,
        count // g,
        [SMEM, whole(mine.shape), whole(other.shape), rows_of(g, CZ, width)],
        [
            (rows_of(g, 3 * CZ, width), (count, 3 * CZ, width), bf16),
            (rows_of(g, width, CZ), (count, width, CZ), bf16),
            (pl.BlockSpec((8, g * width), lambda i: (0, i)), (8, count * width), f32),
            (whole((CZ, WIDE)), (CZ, WIDE), bf16),
            (whole((FF, CZ)), (FF, CZ), bf16),
            (whole((1, 1)), (1, 1), f32),
        ],
        [pltpu.VMEM((CZ, WIDE), f32), pltpu.VMEM((FF, CZ), f32), pltpu.VMEM((3 * CZ, CZ), bf16)],
        (info, mine, other, zbt),
    )


FRONT_ROWS = 12
ATTEND_ROWS = 4
MIDDLE_ROWS = 8
MIDDLE_PART = 2
MIDDLE_LAG = 1
SCORE_ROWS = 6
BACK_ROWS = 3


def attend(masks, info, norms, bias, other_bias, qkv):
    count, _, width = qkv.shape
    g = group_of(count, ATTEND_ROWS)
    return call(
        partial(attend_kernel, masks),
        "attend",
        25,
        count // g,
        [
            SMEM,
            pl.BlockSpec((8, g * width), lambda i: (0, i)),
            whole(bias.shape),
            whole(bias.shape),
            rows_of(g, CZ, width),
            rows_of(g, CZ, width, 1),
            rows_of(g, CZ, width, 2),
        ],
        [
            (rows_of(g, width, HEADS * width), (count, width, HEADS * width), bf16),
            (rows_of(g, CZ, width), (count, CZ, width), f32),
            (rows_of(g, 8, width), (count, 8, width), f32),
        ],
        [
            pltpu.VMEM((width, HEADS * width), f32),
            pltpu.VMEM((width, width), f32),
            pltpu.VMEM((g, 2 * CZ, HEADS * width), bf16),
            pltpu.VMEM((g, width, 2 * CZ), bf16),
            pltpu.SMEM((1,), f32),
        ],
        (info, norms, bias, other_bias, qkv, qkv, qkv),
    )


def middle(info, wide, down, small, gains, zt, zbt, o, r, tgt, nbr):
    count, _, width = zt.shape
    g = group_of(count, MIDDLE_ROWS)
    return call(
        middle_kernel,
        "middle",
        30,
        count // g,
        [
            SMEM,
            whole((CZ, WIDE)),
            whole((FF, CZ)),
            whole(small.shape),
            whole(gains.shape),
            rows_of(g, CZ, width),
            rows_of(g, CZ, width),
            rows_of(g, CZ, width),
            rows_of(g, 8, width),
            whole(tgt.shape),
            whole(nbr.shape),
        ],
        [
            (rows_of(g, CZ, width), (count, CZ, width), bf16),
            (rows_of(g, 16 * HEADS, width), (count, 16 * HEADS, width), bf16),
            (whole((BLOCKS, CZ, CZ)), (BLOCKS, CZ, CZ), bf16),
            (whole((16, CZ)), (16, CZ), bf16),
        ],
        [
            pltpu.VMEM((BLOCKS, CZ, CZ), f32),
            pltpu.VMEM((2, 128 * MIDDLE_PART), f32),
            pltpu.VMEM((CZ, CZ), f32),
            pltpu.VMEM((CZ, CZ), f32),
            pltpu.VMEM((CZ, CZ), bf16),
            pltpu.VMEM((CZ, CZ), bf16),
            pltpu.VMEM((FF, CZ), bf16),
            pltpu.VMEM((CZ, FF), bf16),
            pltpu.VMEM((BINS, CZ), bf16),
            pltpu.VMEM((CZ, 2 * CZ), bf16),
            pltpu.VMEM((FF, 2 * CZ), bf16),
            pltpu.VMEM((CZ, 2 * BINS), bf16),
        ],
        (info, wide, down, small, gains, zt, zbt, o, r, tgt, nbr),
    )


def score(info, p, vn, do, nd):
    count, _, width = do.shape
    g = group_of(count, SCORE_ROWS)
    shape = (width // count // 2, HEADS * count * (width // CZ), CZ)
    return call(
        score_kernel,
        "score",
        17,
        count // g,
        [
            SMEM,
            rows_of(g, width, HEADS * width),
            rows_of(g, width, CZ),
            rows_of(g, CZ, width),
            rows_of(g, 16 * HEADS, width),
        ],
        [(whole(shape), shape, bf16)] * 2,
        [
            pltpu.VMEM((width, HEADS * width), f32),
            pltpu.VMEM((g, 2 * CZ, HEADS * width), bf16),
            pltpu.VMEM((g, width, 2 * CZ), bf16),
            pltpu.VMEM((HEADS, width, width), f32),
        ],
        (info, p, vn, do, nd),
    )


def late_sums(info, spread_out, d_qkv, zbt):
    count, _, width = zbt.shape
    g = group_of(count, 8)
    half = (3 * CZ + 16) // 2
    return call(
        late_kernel,
        "late",
        3,
        count // g,
        [SMEM, whole(spread_out.shape), whole(d_qkv.shape), rows_of(g, CZ, width)],
        [(whole((half, CZ)), (half, CZ), f32)] * 2,
        [
            pltpu.VMEM((HEADS * count * (width // CZ), CZ), f32),
            pltpu.VMEM((CZ, 16), f32),
            pltpu.VMEM((2 * half, CZ), f32),
        ],
        (info, spread_out, d_qkv, zbt),
    )


def back(p, qkv, vn, do, nd, zbt):
    count, _, width = zbt.shape
    g = group_of(count, BACK_ROWS)
    return call(
        back_kernel,
        "back",
        38,
        count // g,
        [
            rows_of(g, width, HEADS * width),
            rows_of(g, CZ, width),
            rows_of(g, CZ, width, 1),
            rows_of(g, width, CZ),
            rows_of(g, CZ, width),
            rows_of(g, 16 * HEADS, width),
            rows_of(g, CZ, width),
        ],
        [(whole((3, CZ, CZ)), (3, CZ, CZ), f32)],
        [
            pltpu.VMEM((g, 2 * CZ, HEADS * width), bf16),
            pltpu.VMEM((g, width, HEADS * width), bf16),
            pltpu.VMEM((g, width, 2 * CZ), bf16),
            pltpu.VMEM((3 * CZ, g * width), bf16),
        ],
        (p, qkv, qkv, vn, do, nd, zbt),
    )[0]


def finish(crops, rows, *args):
    wide, down, gains, small = args[7], args[8], args[9], args[11]
    shapes = []
    for weight in (wide, down):
        shapes += [weight.shape, weight.shape[:1], weight.shape[1:], weight.shape]
    shapes += [gains.shape] * 3 + [small.shape] * 3
    return call(
        partial(finish_kernel, crops, rows),
        "finish",
        4,
        1,
        [SMEM] + [whole(x.shape) for x in args[1:]],
        [(whole(shape), shape, f32) for shape in shapes],
        [
            pltpu.VMEM((BLOCKS * CZ, CZ), f32),
            pltpu.VMEM((3 * CZ + 16, CZ), f32),
            pltpu.VMEM((CZ, WIDE), f32),
            pltpu.VMEM((FF, CZ), f32),
            pltpu.VMEM((CZ, 1), f32),
            pltpu.VMEM((FF, 1), f32),
            pltpu.VMEM((rows, CZ), f32),
            pltpu.VMEM((1, WIDE), f32),
            pltpu.VMEM((1, CZ), f32),
        ],
        args,
    )


def bits(n):
    return [1 << t for t in reversed(range(n.bit_length() - 1))]


def swap(x, axes, size, mask):
    return lax.ppermute(x, axes, [(i, i ^ mask) for i in range(size)])


def gathered(x, axes, size, masks):
    x = x[None]
    for mask in masks:
        x = jnp.concatenate([x, swap(x, axes, size, mask)], 0)
    return x


def places(me, size, masks):
    apart = jnp.arange(size, dtype=jnp.int32) ^ me
    place = jnp.zeros((size,), jnp.int32)
    for t, mask in enumerate(masks):
        place = place + jnp.where((apart & mask) != 0, 1 << t, 0)
    return place


def build(crops, rows):
    both = ("crop", "row")
    devices = crops * rows
    row_masks = bits(rows)
    all_masks = row_masks[:-1] + [m * rows for m in bits(crops)] + row_masks[-1:]

    sides = [[2 * chip + side for chip in range(devices // 2)] for side in range(2)]
    row_sides = [[2 * chip + side for chip in range(rows // 2)] for side in range(2)]

    def body(
        pair,
        crop_len,
        targets,
        neighbours,
        wide,
        wide_rows,
        wide_cols,
        down,
        down_rows,
        down_cols,
        gains,
        gain_second,
        small,
        small_second,
    ):
        row_index = lax.axis_index("row")
        crop_index = lax.axis_index("crop")
        count_rows, width = pair.shape[1], pair.shape[2]
        info = jnp.stack([row_index, crop_index, crop_len[0], jnp.int32(count_rows)])

        pack = pack_weights(
            devices // 2, wide, down, wide_rows, down_rows, wide_cols, down_cols
        )
        small_t = small.T
        packs = lax.all_to_all(pack, both, 0, 0, axis_index_groups=sides, tiled=True)
        zt, zbt, bias_part = front(pair[0], gains, small_t)
        bias = gathered(bias_part, "row", rows, row_masks[:-1])
        other_packs = swap(packs, both, devices, 1)
        qkv, vn, norms, wide_full, down_full, done = project(
            crops, rows, info, packs, other_packs, zbt
        )
        bias = bias + done.astype(bf16)[..., None, None]
        other_bias = swap(bias, "row", rows, row_masks[-1])
        if count_rows % 8:
            bias = jnp.concatenate([bias, other_bias], 0)
            bias = jnp.take(bias, places(row_index, rows, row_masks), axis=0)
            bias = bias.transpose(1, 0, 2, 3).reshape(1, HEADS, width, width)
            other_bias = bias
        bias_masks = [] if count_rows % 8 else row_masks
        p, o, r = attend(bias_masks, info, norms, bias, other_bias, qkv)
        do, nd, early, scalars = middle(
            info,
            wide_full,
            down_full,
            small_t,
            gains,
            zt,
            zbt,
            o,
            r,
            targets,
            neighbours,
        )

        early = lax.all_to_all(early.reshape(devices, -1, CZ), both, 0, 0, tiled=True)
        keep, give = score(info, p, vn, do, nd)
        early, keep, give = lax.optimization_barrier((early, keep, give))
        got = swap(give, both, devices, 1)
        early = jnp.concatenate([jnp.sum(early.astype(f32), 0).astype(bf16), scalars], 0)
        early_lines = early.shape[0]
        early = gathered(early, both, devices, [1] + [m * rows for m in bits(crops)])
        early = early.reshape(-1, CZ)
        early = jnp.broadcast_to(early[None], (rows // 2, *early.shape))
        parcel = jnp.concatenate([(keep.astype(f32) + got.astype(f32)).astype(bf16), early], 1)
        parcel, do = lax.optimization_barrier((parcel, do))
        parcel = lax.all_to_all(parcel, "row", 0, 0, axis_index_groups=row_sides, tiled=True)
        d_qkv = back(p, qkv, vn, do, nd, zbt)

        keep, give = late_sums(info, parcel, d_qkv, zbt)
        keep = keep + swap(give, both, devices, 1)
        for mask in all_masks[:-1]:
            keep = keep + swap(keep, both, devices, mask)
        other = swap(keep, both, devices, 1)
        scalars = parcel[:, -2 * crops * early_lines :].reshape(rows // 2, 2 * crops, -1, CZ)
        scalars = jnp.sum(scalars[:, :, -16, :6].astype(f32), (0, 1)).reshape(3, 2)
        loss_sum, pair_count = jnp.sum(scalars[:, 0]), jnp.sum(scalars[:, 1])
        (
            wide_g,
            wide_r_new,
            wide_c_new,
            wide_new,
            down_g,
            down_r_new,
            down_c_new,
            down_new,
            gain_grad,
            gain_s,
            gain_n,
            small_grad,
            small_s,
            small_n,
        ) = finish(
            crops,
            rows,
            info,
            keep,
            other,
            parcel,
            packs,
            other_packs,
            wide_full,
            wide,
            down,
            gains,
            gain_second,
            small_t,
            small_second.T,
        )
        return (
            loss_sum,
            pair_count,
            wide_g,
            wide_r_new,
            wide_c_new,
            wide_new,
            down_g,
            down_r_new,
            down_c_new,
            down_new,
            gain_grad,
            gain_s,
            gain_n,
            small_grad.T,
            small_s.T,
            small_n.T,
        )

    return body


def solution(mesh):
    return jax.shard_map(
        build(mesh.shape["crop"], mesh.shape["row"]),
        mesh=mesh,
        in_specs=(
            P("crop", "row", None, None),
            P("crop"),
            P("crop", "row", None),
            P("crop", "row", None),
            P("row", "crop"),
            P("row"),
            P("crop"),
            P("row", "crop"),
            P("row"),
            P("crop"),
            P(),
            P(),
            P(),
            P(),
        ),
        out_specs=(
            P(),
            P(),
            P("row", "crop"),
            P("row"),
            P("crop"),
            P("row", "crop"),
            P("row", "crop"),
            P("row"),
            P("crop"),
            P("row", "crop"),
            P(),
            P(),
            P(),
            P(),
            P(),
            P(),
        ),
        check_vma=False,
    )
```

```python
import math
from functools import partial

import jax
import jax.numpy as jnp
from jax import lax
from jax.experimental import pallas as pl
from jax.experimental.pallas import tpu as pltpu
from jax.sharding import PartitionSpec as P

CZ = 128
HEADS = 4
HEAD_DIM = 32
FF = 512
BINS = 64
WIDE = 5 * CZ + FF

DECAY = 1.0 - 10.0 ** (-0.8)
TINY = 1e-30
LOG2E = math.log2(math.e)
ROOT = 1.0 / math.sqrt(HEAD_DIM)
BLK = 256
SAFE = 40.0
STATS = 256

GATE_BLOCK, OUT_BLOCK, IN_BLOCK, DOWN_BLOCK, HEAD_BLOCK, BLOCKS = 0, 1, 2, 6, 10, 12

f32 = jnp.float32
bf16 = jnp.bfloat16


def dot(a, b):
    return lax.dot_general(a, b, (((1,), (0,)), ((), ())), preferred_element_type=f32)


def dot_nt(a, b):
    return lax.dot_general(a, b, (((1,), (1,)), ((), ())), preferred_element_type=f32)


def rounded(v):
    return v.astype(bf16).astype(f32)


def halves(v):
    high = v.astype(bf16)
    return high, (v - high.astype(f32)).astype(bf16)


def normed(x):
    centre = x - jnp.sum(x, 0, keepdims=True) * (1.0 / CZ)
    var = jnp.sum(centre * centre, 0, keepdims=True) * (1.0 / CZ)
    inv = lax.rsqrt(var + 1e-05)
    return centre * inv, inv


def normed_back(d, xhat, inv):
    one = jnp.sum(d, 0, keepdims=True) * (1.0 / CZ)
    two = jnp.sum(d * xhat, 0, keepdims=True) * (1.0 / CZ)
    return inv * (d - one - xhat * two)


def sigmoid(x):
    return 0.5 * jnp.tanh(0.5 * x) + 0.5


def wider(column, x):
    return jnp.concatenate([column] * (x.shape[1] // 128), 1)


def lanes(ref):
    return jnp.concatenate([ref[g] for g in range(ref.shape[0])], 1)


def spread(ref, x):
    width = ref.shape[2]
    for g in range(ref.shape[0]):
        ref[g] = x[:, g * width : (g + 1) * width]


def columns_of(gains_ref, which, scratch):
    scratch[...] = jnp.broadcast_to(gains_ref[...].T[:, which : which + 1], (CZ, CZ))


def place(source, me, masks):
    apart = source ^ me
    where = 0
    for t, mask in enumerate(masks):
        where = where + ((apart >> (mask.bit_length() - 1)) & 1) * (1 << t)
    return where


def pack_kernel(
    wide_ref, down_ref, wide_rows_ref, down_rows_ref, wide_cols_ref, down_cols_ref, pack_ref, pack
):
    lines, cols = wide_ref.shape
    span = down_ref.shape[1]
    pack[...] = jnp.zeros_like(pack)
    for at, ref in ((0, wide_rows_ref), (lines, down_rows_ref)):
        some = ref[...].reshape(1, -1)
        upper = rounded(some)
        pack[0:1, at : at + some.shape[1]] = upper
        pack[1:2, at : at + some.shape[1]] = some - upper
    stats = jnp.concatenate(
        [wide_cols_ref[...].reshape(1, -1), down_cols_ref[...].reshape(1, -1)], 1
    )
    for part in range(-(-stats.shape[1] // STATS)):
        some = stats[:, part * STATS : (part + 1) * STATS]
        upper = rounded(some)
        pack[2 + part : 3 + part, : some.shape[1]] = upper
        pack[5 + part : 6 + part, : some.shape[1]] = some - upper
    pack[:lines, STATS : STATS + cols] = wide_ref[...]
    for part in range(FF // CZ):
        at = STATS + cols + part * span
        pack[:lines, at : at + span] = down_ref[part * lines : (part + 1) * lines, :]
    for peer in range(pack_ref.shape[0]):
        pack_ref[peer] = pack[...].astype(bf16)


def front_kernel(
    pair_ref, gains_ref, small_ref, zt_ref, zbt_ref, bias_ref, gain, wb, part
):
    rows, width, _ = pair_ref.shape
    step = pl.program_id(0)

    @pl.when(step == 0)
    def _():
        columns_of(gains_ref, 0, gain)
        wb[...] = small_ref[:16].astype(bf16)

    x = pair_ref[...].astype(f32).reshape(rows * width, CZ).T
    spread(zt_ref, x.astype(bf16))
    xhat, _ = normed(x)
    zb = (xhat * wider(gain[...], x)).astype(bf16)
    spread(zbt_ref, zb)
    bias = dot(wb[...], zb)
    for g in range(rows):
        for h in range(HEADS):
            part[h, pl.ds(step * rows + g, 1), :] = bias[h : h + 1, g * width : (g + 1) * width]

    @pl.when(step == pl.num_programs(0) - 1)
    def _():
        bias_ref[...] = part[...].astype(bf16)


def pick(info_ref, mine_ref, other_ref, crop, row, rows):
    chip = crop * (rows // 2) + row // 2
    side = info_ref[0] & 1
    return jnp.where(
        side == row % 2, mine_ref[chip].astype(f32), other_ref[chip].astype(f32)
    )


def project_kernel(
    crops,
    rows,
    info_ref,
    mine_ref,
    other_ref,
    zbt_ref,
    qkv_ref,
    vn_ref,
    norm_ref,
    wide_ref,
    down_ref,
    done_ref,
    wide_s,
    down_s,
    wqt,
):
    lines, cols, span = CZ // rows, WIDE // crops, CZ // crops

    @pl.when(pl.program_id(0) == 0)
    def _():
        for c in range(crops):
            for r in range(rows):
                block = pick(info_ref, mine_ref, other_ref, c, r, rows)[:lines]
                wide_s[r * lines : (r + 1) * lines, c * cols : (c + 1) * cols] = block[
                    :, STATS : STATS + cols
                ]
                for part in range(FF // CZ):
                    at = (r * (FF // CZ) + part) * lines
                    left = STATS + cols + part * span
                    down_s[at : at + lines, c * span : (c + 1) * span] = block[:, left : left + span]
        wide_ref[...] = wide_s[...].astype(bf16)
        down_ref[...] = down_s[...].astype(bf16)
        wqt[...] = wide_s[:, : 3 * CZ].T.astype(bf16)
        done_ref[...] = jnp.zeros_like(done_ref)

    qkv = dot(wqt[...], lanes(zbt_ref)).astype(bf16)
    spread(qkv_ref, qkv)
    q = qkv[:CZ].astype(f32)
    k = qkv[CZ : 2 * CZ].astype(f32)
    vn_ref[...] = qkv[2 * CZ :].T.reshape(vn_ref.shape)
    norm_ref[...] = jnp.concatenate(
        [
            jnp.sum((x * x)[h * HEAD_DIM : (h + 1) * HEAD_DIM], 0, keepdims=True)
            for x in (q, k)
            for h in range(HEADS)
        ],
        0,
    )


def attend_kernel(
    masks,
    info_ref,
    norm_ref,
    bias_ref,
    other_bias_ref,
    q_ref,
    k_ref,
    v_ref,
    p_ref,
    o_ref,
    r_ref,
    biast,
    nat,
    qbd,
    kk,
    bound,
):
    group, _, width = q_ref.shape
    rows = bias_ref.shape[2]
    shards = width // rows
    step = pl.program_id(0)

    @pl.when(step == 0)
    def _():
        top = 0.0
        key = lax.broadcasted_iota(jnp.int32, (1, width), 1)
        kb = jnp.where(key < info_ref[2], 0.0, -1000000000.0 * LOG2E)
        for h in range(HEADS):
            for s in range(shards):
                at = place(s, info_ref[0], masks[:-1])
                block = bias_ref[at, h].astype(f32)
                if shards > 1:
                    here = (info_ref[0] & 1) == s % 2
                    block = jnp.where(here, block, other_bias_ref[at, h].astype(f32))
                nat[s * rows : (s + 1) * rows, :] = block
            top = jnp.maximum(top, jnp.max(jnp.abs(nat[...])))
            biast[:, h * width : (h + 1) * width] = (nat[...] * LOG2E + kb).T
        bound[0] = top * LOG2E
        qbd[...] = jnp.zeros_like(qbd)
        r_ref[...] = jnp.zeros_like(r_ref)

    def attend(shift):
        for g in range(group):
            high, low = halves(q_ref[g].astype(f32) * (LOG2E * ROOT))
            for h in range(HEADS):
                a, b = h * HEAD_DIM, (h + 1) * HEAD_DIM
                qbd[g, a:b, h * width : (h + 1) * width] = high[a:b]
                qbd[g, CZ + a : CZ + b, h * width : (h + 1) * width] = low[a:b]
            kn = k_ref[g].T
            kk[g, :, :CZ] = kn
            kk[g, :, CZ:] = kn
            sums = []
            for c in range(0, HEADS * width, BLK):
                s = dot(kk[g], qbd[g, :, c : c + BLK]) + biast[:, c : c + BLK]
                if shift:
                    s = s - jnp.max(s, 0, keepdims=True)
                e = jnp.exp2(s)
                sums.append(jnp.sum(e, 0, keepdims=True))
                p_ref[g, :, c : c + BLK] = e.astype(bf16)
            r = 1.0 / jnp.concatenate(sums, 1)
            for h in range(HEADS):
                a, b = h * HEAD_DIM, (h + 1) * HEAD_DIM
                mine = r[:, h * width : (h + 1) * width]
                r_ref[g, h : h + 1] = mine
                o_ref[g, a:b] = dot(v_ref[g, a:b], p_ref[g, :, h * width : (h + 1) * width]) * mine

    norms = jnp.max(norm_ref[...], 1, keepdims=True)
    reach = jnp.max(jnp.sqrt(norms[:HEADS] * norms[HEADS:])) * (1.01 * LOG2E * ROOT)
    safe = reach + bound[0] < SAFE

    @pl.when(safe)
    def _():
        attend(False)

    @pl.when(jnp.logical_not(safe))
    def _():
        attend(True)


def middle_kernel(
    info_ref,
    wide_ref,
    down_ref,
    head_ref,
    gains_ref,
    zt_ref,
    zbt_ref,
    o_ref,
    r_ref,
    tgt_ref,
    nbr_ref,
    do_ref,
    nd_ref,
    grads_ref,
    scalars_ref,
    acc,
    sums,
    g1,
    g2,
    wgt,
    wot,
    wint,
    wdownt,
    wht,
    wo2,
    wdown2,
    wh2,
):
    step = pl.program_id(0)

    @pl.when(step == 0)
    def _():
        wo = wide_ref[:, 4 * CZ : 5 * CZ]
        wot[...] = wo.T
        wgt[...] = wide_ref[:, 3 * CZ : 4 * CZ].T
        wint[...] = wide_ref[:, 5 * CZ :].T * 0.5
        wdownt[...] = down_ref[...].T
        head = head_ref[...][HEADS:]
        wht[...] = head.astype(bf16)
        head = head.T.astype(bf16)
        wo2[...] = jnp.concatenate([wo, wo], 1)
        wdown2[...] = jnp.concatenate([down_ref[...], down_ref[...]], 1) * 0.5
        wh2[...] = jnp.concatenate([head, head], 1)
        acc[...] = jnp.zeros_like(acc)
        columns_of(gains_ref, 1, g1)
        columns_of(gains_ref, 2, g2)
        sums[...] = jnp.zeros_like(sums)

    group, _, width = o_ref.shape
    first = step * group

    def add(block, grad):
        for c in range(0, grad.shape[1], CZ):
            acc[block + c // CZ] += grad[:, c : c + CZ]

    def stages(low, high):
        spots = [divmod(block * 128, width) for block in range(low, high)]

        def mine(ref):
            return jnp.concatenate([ref[g, :, at : at + 128] for g, at in spots], 1)

        def line(ref):
            return jnp.concatenate(
                [ref[0, pl.ds(first + g, 1), :][:, at : at + 128] for g, at in spots], 1
            )

        def out(ref, x):
            for n, (g, at) in enumerate(spots):
                ref[g, :, at : at + 128] = x[:, n * 128 : (n + 1) * 128]

        o = mine(o_ref)
        zb = mine(zbt_ref)
        gate = sigmoid(dot(wgt[...], zb))
        gain1 = wider(g1[...], o)
        gain2 = wider(g2[...], o)
        og = (o * gate).astype(bf16)
        z1 = mine(zt_ref).astype(f32) + dot(wot[...], og)
        yield
        xhat1, inv1 = normed(z1)
        zb2 = (xhat1 * gain1).astype(bf16)
        yield
        hidden, slopes = [], []
        for f in range(0, FF, CZ):
            hid = dot(wint[f : f + CZ], zb2)
            t = jnp.tanh(hid)
            sg = 1.0 + t
            act = hid * sg
            hidden.append(act.astype(bf16))
            slopes.append(sg + act * (1.0 - t))
            yield
        a = jnp.concatenate(hidden, 0)
        z2 = z1 + dot(wdownt[...], a)
        yield
        xhat2, inv2 = normed(z2)
        zb3 = (xhat2 * gain2).astype(bf16)
        logits = dot(wht[...], zb3)
        yield
        top = jnp.max(logits, 0, keepdims=True)
        ex = jnp.exp(logits - top)
        total = jnp.sum(ex, 0, keepdims=True)
        hot = lax.broadcasted_iota(jnp.int32, logits.shape, 0) == line(tgt_ref)
        picked = jnp.sum(jnp.where(hot, logits, 0.0), 0, keepdims=True)
        column = lax.broadcasted_iota(jnp.int32, (1, 128), 1)
        length = info_ref[2]
        valid = jnp.concatenate(
            [
                column + at < jnp.where(info_ref[0] * info_ref[3] + first + g < length, length, 0)
                for g, at in spots
            ],
            1,
        )
        mask = jnp.where((line(nbr_ref) > 0) & valid, 1.0, 0.0)
        at = slice(0, mask.shape[1])
        sums[0:1, at] += (jnp.log(total) + top - picked) * mask
        sums[1:2, at] += mask
        dl = ex * (mask / total) - jnp.where(hot, mask, 0.0)
        dl2 = jnp.concatenate(halves(dl), 0)
        yield
        add(HEAD_BLOCK, dot_nt(dl2, zb3))
        dzb3 = rounded(dot(wh2[...], dl2))
        yield
        dz2 = normed_back(dzb3 * gain2, xhat2, inv2)
        high2, low2 = halves(dz2)
        both2 = jnp.concatenate([high2, low2], 0)
        yield
        dh = []
        for f in range(0, FF, CZ):
            dh.append((dot(wdown2[f : f + CZ], both2) * slopes[f // CZ]).astype(bf16))
            yield
        dh = jnp.concatenate(dh, 0)
        add(DOWN_BLOCK, dot_nt(high2, a))
        yield
        dzb2 = rounded(dot(wide_ref[:, 5 * CZ :], dh))
        yield
        add(IN_BLOCK, dot_nt(zb2, dh))
        dz1 = dz2 + normed_back(dzb2 * gain1, xhat1, inv1)
        high1, low1 = halves(dz1)
        yield
        add(OUT_BLOCK, dot_nt(og, high1))
        dog = rounded(dot(wo2[...], jnp.concatenate([high1, low1], 0)))
        yield
        do = dog * gate
        doo = do * o
        add(GATE_BLOCK, dot_nt(zb, (doo * (1.0 - gate)).astype(bf16)))
        yield
        r = mine(r_ref)
        parts, minus = [], []
        for h in range(HEADS):
            x, y = h * HEAD_DIM, (h + 1) * HEAD_DIM
            share = r[h : h + 1]
            parts.append((do[x:y] * share).astype(bf16))
            less = -jnp.sum(doo[x:y], 0, keepdims=True) * share
            upper = rounded(less)
            minus.append(
                jnp.concatenate([upper, less - upper, jnp.zeros((14, less.shape[1]), f32)], 0)
            )
        out(do_ref, jnp.concatenate(parts, 0))
        out(nd_ref, jnp.concatenate(minus, 0).astype(bf16))

    blocks = group * width // 128
    running = [
        stages(low, min(low + MIDDLE_PART, blocks)) for low in range(0, blocks, MIDDLE_PART)
    ]
    turn = 0
    waiting = list(enumerate(running))
    while waiting:
        for item in list(waiting):
            if turn >= item[0] * MIDDLE_LAG and next(item[1], item) is item:
                waiting.remove(item)
        turn += 1

    @pl.when(step == pl.num_programs(0) - 1)
    def _():
        for block in range(BLOCKS):
            grads_ref[block] = acc[block].astype(bf16)
        both = jnp.sum(sums[...], 1, keepdims=True)
        lane = lax.broadcasted_iota(jnp.int32, scalars_ref.shape, 1)
        out = jnp.zeros(scalars_ref.shape, f32)
        for part in range(3):
            upper = rounded(both)
            for which in range(2):
                out = jnp.where(lane == 2 * part + which, upper[which : which + 1], out)
            both = both - upper
        scalars_ref[...] = out.astype(bf16)


def score_kernel(info_ref, p_ref, vn_ref, do_ref, nd_ref, keep_ref, give_ref, acc, dobd, vv, nat):
    group, _, width = do_ref.shape
    step = pl.program_id(0)

    @pl.when(step == 0)
    def _():
        acc[...] = jnp.zeros_like(acc)
        prepare(dobd, vv)

    for g in range(group):
        score_operands(g, vn_ref, do_ref, nd_ref, dobd, vv)
        for c in range(0, HEADS * width, BLK):
            acc[:, c : c + BLK] += dot(vv[g], dobd[g, :, c : c + BLK]) * p_ref[
                g, :, c : c + BLK
            ].astype(f32)

    @pl.when(step == pl.num_programs(0) - 1)
    def _():
        chips, tall, _ = keep_ref.shape
        lines = width // (2 * chips)
        first = (info_ref[0] & 1) == 0
        for h in range(HEADS):
            nat[h] = acc[:, h * width : (h + 1) * width].T
        for chip in range(chips):
            sides = [
                jnp.concatenate(
                    [
                        nat[h, (2 * chip + side) * lines : (2 * chip + side + 1) * lines, c : c + CZ]
                        for c in range(0, width, CZ)
                        for h in range(HEADS)
                    ],
                    0,
                )
                for side in range(2)
            ]
            keep_ref[chip] = jnp.where(first, sides[0], sides[1]).astype(bf16)
            give_ref[chip] = jnp.where(first, sides[1], sides[0]).astype(bf16)


def prepare(dobd, vv):
    dobd[...] = jnp.zeros_like(dobd)
    vv[...] = jnp.ones_like(vv)


def score_operands(g, vn_ref, do_ref, nd_ref, dobd, vv):
    width = do_ref.shape[2]
    vv[g, :, :CZ] = vn_ref[g]
    for h in range(HEADS):
        a, b = h * HEAD_DIM, (h + 1) * HEAD_DIM
        at = slice(h * width, (h + 1) * width)
        dobd[g, a:b, at] = do_ref[g, a:b]
        dobd[g, CZ : CZ + 16, at] = nd_ref[g, 16 * h : 16 * (h + 1)]


def back_kernel(
    info_ref,
    p_ref,
    q_ref,
    k_ref,
    vn_ref,
    do_ref,
    nd_ref,
    zbt_ref,
    keep_ref,
    give_ref,
    dwq,
    dobd,
    dst,
    vv,
    dproj,
):
    group, _, width = do_ref.shape
    step = pl.program_id(0)

    @pl.when(step == 0)
    def _():
        dwq[...] = jnp.zeros_like(dwq)
        prepare(dobd, vv)

    for g in range(group):
        score_operands(g, vn_ref, do_ref, nd_ref, dobd, vv)
        for c in range(0, HEADS * width, BLK):
            ds = dot(vv[g], dobd[g, :, c : c + BLK]) * p_ref[g, :, c : c + BLK].astype(f32)
            dst[g, :, c : c + BLK] = ds.astype(bf16)
        at = slice(g * width, (g + 1) * width)
        for h in range(HEADS):
            a, b = h * HEAD_DIM, (h + 1) * HEAD_DIM
            mine = dst[g, :, h * width : (h + 1) * width]
            dproj[a:b, at] = (dot(k_ref[g, a:b], mine) * ROOT).astype(bf16)
            dproj[CZ + a : CZ + b, at] = (dot_nt(q_ref[g, a:b], mine) * ROOT).astype(bf16)
            dproj[2 * CZ + a : 2 * CZ + b, at] = dot_nt(
                do_ref[g, a:b], p_ref[g, :, h * width : (h + 1) * width]
            ).astype(bf16)
    grad = dot_nt(lanes(zbt_ref), dproj[...])
    for block in range(3):
        dwq[block * CZ : (block + 1) * CZ, :] += grad[:, block * CZ : (block + 1) * CZ]

    @pl.when(step == pl.num_programs(0) - 1)
    def _():
        half = keep_ref.shape[0]
        first = (info_ref[0] & 1) == 0
        one, two = dwq[:half, :], dwq[half:, :]
        keep_ref[...] = jnp.where(first, one, two)
        give_ref[...] = jnp.where(first, two, one)


def factored(grad_ref, rows, cols, weight_ref, crop, row_start, scratch, outs):
    grad_out, rows_out, cols_out, new_out = outs
    lines, span = weight_ref.shape
    grad = grad_ref[...]
    count, columns = grad.shape
    sq = grad * grad
    rows_new = DECAY * rows + (1.0 - DECAY) * (jnp.sum(sq, 1, keepdims=True) / columns + TINY)
    cols_new = DECAY * cols + (1.0 - DECAY) * (jnp.sum(sq, 0, keepdims=True) / count + TINY)
    mean = jnp.sum(rows_new, 0, keepdims=True) / count
    rows_factor = mean / rows_new
    cols_factor = 1.0 / cols_new
    size = jnp.sum(jnp.sum(sq * rows_factor * cols_factor, 1, keepdims=True), 0, keepdims=True)
    clip = jnp.maximum(0.1, jnp.sqrt(size / (count * columns)))
    scratch[...] = rows_factor
    mine = grad_ref[pl.ds(row_start, lines), :]
    update = mine * lax.rsqrt((1.0 / scratch[pl.ds(row_start, lines), :]) * (1.0 / cols_factor))
    update = weight_step(update, clip)
    scratch[...] = rows_new
    own_rows = jnp.broadcast_to(scratch[pl.ds(row_start, lines), :], (lines, CZ))
    rows_out[...] = own_rows.T[0]

    def own(x):
        part = x[:, :span]
        for c in range(1, columns // span):
            part = jnp.where(crop == c, x[:, c * span : (c + 1) * span], part)
        return part

    grad_out[...] = own(mine)
    cols_out[...] = own(cols_new)[0]
    new_out[...] = weight_ref[...] - own(update)


def weight_step(update, clip):
    return update * (0.03 / clip)


def plain(weight, grad, second, rate, outs):
    second_new = DECAY * second + (1.0 - DECAY) * (grad * grad + TINY)
    update = grad * lax.rsqrt(second_new)
    square = jnp.sum(jnp.sum(update * update, 1, keepdims=True), 0, keepdims=True)
    clip = jnp.maximum(1.0, jnp.sqrt(square / (grad.shape[0] * grad.shape[1])))
    outs[0][...] = grad
    outs[1][...] = second_new
    outs[2][...] = weight - rate * update / clip


def finish_kernel(
    crops,
    rows,
    info_ref,
    keep_ref,
    other_ref,
    spread_ref,
    across_ref,
    packs_ref,
    other_packs_ref,
    full_ref,
    wide_ref,
    down_ref,
    gains_ref,
    gain_second_ref,
    small_ref,
    small_second_ref,
    *refs,
):
    outs, (flat, late_ref, wide_s, down_s, wide_c, down_c, table, wide_cols, down_cols) = (
        refs[:14],
        refs[14:],
    )
    row, crop = info_ref[0], info_ref[1]
    side = row & 1
    half = 3 * CZ // 2
    mine, other = keep_ref[...], other_ref[...]
    late_ref[:half, :] = jnp.where(side == 0, mine[:half], other[:half])
    late_ref[half:, :] = jnp.where(side == 0, other[:half], mine[:half])
    pbias = mine[half:] + other[half:]

    lines = BLOCKS * CZ // (crops * rows)
    height = lines + 16
    start = spread_ref.shape[1] - 2 * height
    tail = jnp.zeros((1, CZ), f32)
    for c in range(crops):
        for r in range(rows):
            at = (c * rows + r) * lines
            which = (r % 2) ^ side
            block = jnp.zeros((height, CZ), f32)
            for p in range(2):
                part = slice(start + p * height, start + (p + 1) * height)
                here = spread_ref[r // 2, part].astype(f32)
                there = across_ref[r // 2, p * height : (p + 1) * height].astype(f32)
                block = jnp.where(which == p, jnp.where(c == crop, here, there), block)
            flat[at : at + lines, :] = block[:lines]
            tail += block[lines : lines + 1]
    scale = 1.0 / (tail[:, 1:2] + tail[:, 3:4] + tail[:, 5:6])

    def early(block):
        return flat[block * CZ : (block + 1) * CZ, :] * scale

    for block in range(3):
        wide_s[:, block * CZ : (block + 1) * CZ] = (
            late_ref[block * CZ : (block + 1) * CZ, :] * scale
        )
    for block in range(GATE_BLOCK, DOWN_BLOCK):
        wide_s[:, (3 + block) * CZ : (4 + block) * CZ] = early(block)
    for block in range(DOWN_BLOCK, HEAD_BLOCK):
        down_s[(block - DOWN_BLOCK) * CZ : (block - DOWN_BLOCK + 1) * CZ, :] = early(block).T
    head = early(HEAD_BLOCK)
    pbias = pbias[:HEADS] * scale
    small_grad = jnp.concatenate([pbias, head[:BINS] + head[BINS:]], 0)
    small = small_ref[...]
    plain(small, small_grad, small_second_ref[...], 0.03, outs[11:])

    through = wide_s[...] * full_ref[...].astype(f32)
    behind = small_grad * rounded(small)
    lane = lax.broadcasted_iota(jnp.int32, (CZ, CZ), 1)
    gain_grad = jnp.where(
        lane == 0,
        jnp.sum(through[:, : 4 * CZ], 1, keepdims=True),
        jnp.sum(through[:, 5 * CZ :], 1, keepdims=True),
    ).T
    gain_grad = jnp.concatenate(
        [
            gain_grad[:1] + jnp.sum(behind[:HEADS], 0, keepdims=True),
            gain_grad[1:2],
            jnp.sum(behind[HEADS:], 0, keepdims=True),
        ],
        0,
    )
    gains = gains_ref[...]
    plain(gains, gain_grad / gains, gain_second_ref[...], 0.3, outs[8:11])

    per, down_per = CZ // rows, FF // rows
    for r in range(rows):
        block = pick(info_ref, packs_ref, other_packs_ref, 0, r, rows)
        table[r : r + 1, :] = block[0:1, :CZ] + block[1:2, :CZ]

    def column(size, start):
        tall = jnp.broadcast_to(table[...][:, None, :], (rows, size, CZ)).reshape(rows * size, CZ)
        lane = lax.broadcasted_iota(jnp.int32, tall.shape, 1)
        line = lax.broadcasted_iota(jnp.int32, tall.shape, 0)
        return jnp.sum(jnp.where(lane == start + line % size, tall, 0.0), 1, keepdims=True)

    cols, span = WIDE // crops, CZ // crops
    for c in range(crops):
        block = pick(info_ref, packs_ref, other_packs_ref, c, 0, rows)[:, :STATS]
        block = block[2:5] + block[5:8]
        stats = jnp.concatenate([block[part : part + 1] for part in range(3)], 1)
        wide_cols[:, c * cols : (c + 1) * cols] = stats[:, :cols]
        down_cols[:, c * span : (c + 1) * span] = stats[:, cols : cols + span]
    factored(
        wide_s,
        column(per, 0),
        wide_cols[...],
        wide_ref,
        crop,
        row * wide_ref.shape[0],
        wide_c,
        outs[:4],
    )
    factored(
        down_s,
        column(down_per, per),
        down_cols[...],
        down_ref,
        crop,
        row * down_ref.shape[0],
        down_c,
        outs[4:8],
    )


def late_kernel(spread_ref, keep_ref, got_ref, zbt_ref, out_ref, send_ref, dbias, acc):
    group, _, width = zbt_ref.shape
    tall = dbias.shape[0]
    lines = tall // (HEADS * (width // CZ))
    step = pl.program_id(0)

    @pl.when(step == 0)
    def _():
        total = spread_ref[0, :tall].astype(f32)
        for chip in range(1, spread_ref.shape[0]):
            total += spread_ref[chip, :tall].astype(f32)
        dbias[...] = rounded(total)
        acc[...] = jnp.zeros_like(acc)

    some = jnp.concatenate(
        [
            dbias[pl.ds(c * HEADS * lines + step * group + g, HEADS, stride=lines), :]
            for g in range(group)
            for c in range(width // CZ)
        ],
        1,
    )
    some = jnp.concatenate([some, jnp.zeros((16 - HEADS, some.shape[1]), f32)], 0)
    acc[...] += dot_nt(lanes(zbt_ref), some.astype(bf16))

    @pl.when(step == pl.num_programs(0) - 1)
    def _():
        half = keep_ref.shape[0]
        for at, x in ((0, keep_ref[...] + got_ref[...]), (half, acc[...].T[:8])):
            out_ref[at : at + x.shape[0], :] = rounded(x)
        send_ref[...] = out_ref[...].astype(bf16)


def whole(shape):
    return pl.BlockSpec(shape, lambda i: (0,) * len(shape))


def rows_of(group, lines, columns, line=0, column=0):
    return pl.BlockSpec((group, lines, columns), lambda i: (i, line, column))


def of(shape, dtype):
    return jax.ShapeDtypeStruct(shape, dtype)


SMEM = pl.BlockSpec(memory_space=pltpu.SMEM)


def call(kernel, name, micros, grid, in_specs, outs, scratch, args, mebibytes=52):
    return pl.pallas_call(
        kernel,
        grid=(grid,),
        in_specs=in_specs,
        out_specs=[o[0] for o in outs],
        out_shape=[of(o[1], o[2]) for o in outs],
        scratch_shapes=scratch,
        compiler_params=pltpu.CompilerParams(vmem_limit_bytes=mebibytes << 20),
        cost_estimate=pl.CostEstimate(
            flops=int(micros * 8e8), bytes_accessed=1 << 20, transcendentals=0
        ),
        name=name,
    )(*args)


def group_of(count, most):
    return next(g for g in range(most, 0, -1) if count % g == 0)


def pack_weights(peers, wide, down, *stats):
    args = (wide, down, *stats)
    shape = (peers, 8, STATS + wide.shape[1] + (FF // CZ) * down.shape[1])
    return call(
        pack_kernel,
        "pack",
        1,
        1,
        [whole(x.shape) for x in args],
        [(whole(shape), shape, bf16)],
        [pltpu.VMEM(shape[1:], f32)],
        args,
        60,
    )[0]


def front(pair, gains, small):
    count, width = pair.shape[0], pair.shape[1]
    g = group_of(count, FRONT_ROWS)
    return call(
        front_kernel,
        "front",
        6,
        count // g,
        [rows_of(g, width, CZ), whole(gains.shape), whole(small.shape)],
        [
            (rows_of(g, CZ, width), (count, CZ, width), bf16),
            (rows_of(g, CZ, width), (count, CZ, width), bf16),
            (whole((HEADS, count, width)), (HEADS, count, width), bf16),
        ],
        [
            pltpu.VMEM((CZ, CZ), f32),
            pltpu.VMEM((16, CZ), bf16),
            pltpu.VMEM((HEADS, count, width), f32),
        ],
        (pair, gains, small),
    )


def project(crops, rows, info, mine, other, zbt):
    count, _, width = zbt.shape
    g = group_of(count, 6)
    return call(
        partial(project_kernel, crops, rows),
        "project",
        40,
        count // g,
        [SMEM, whole(mine.shape), whole(other.shape), rows_of(g, CZ, width)],
        [
            (rows_of(g, 3 * CZ, width), (count, 3 * CZ, width), bf16),
            (rows_of(g, width, CZ), (count, width, CZ), bf16),
            (pl.BlockSpec((8, g * width), lambda i: (0, i)), (8, count * width), f32),
            (whole((CZ, WIDE)), (CZ, WIDE), bf16),
            (whole((FF, CZ)), (FF, CZ), bf16),
            (whole((1, 1)), (1, 1), f32),
        ],
        [pltpu.VMEM((CZ, WIDE), f32), pltpu.VMEM((FF, CZ), f32), pltpu.VMEM((3 * CZ, CZ), bf16)],
        (info, mine, other, zbt),
    )


FRONT_ROWS = 12
ATTEND_ROWS = 4
MIDDLE_ROWS = 8
MIDDLE_PART = 2
MIDDLE_LAG = 1
SCORE_ROWS = 6
BACK_ROWS = 3
LATE_ROWS = 12


def attend(masks, info, norms, bias, other_bias, qkv):
    count, _, width = qkv.shape
    g = group_of(count, ATTEND_ROWS)
    return call(
        partial(attend_kernel, masks),
        "attend",
        25,
        count // g,
        [
            SMEM,
            pl.BlockSpec((8, g * width), lambda i: (0, i)),
            whole(bias.shape),
            whole(bias.shape),
            rows_of(g, CZ, width),
            rows_of(g, CZ, width, 1),
            rows_of(g, CZ, width, 2),
        ],
        [
            (rows_of(g, width, HEADS * width), (count, width, HEADS * width), bf16),
            (rows_of(g, CZ, width), (count, CZ, width), f32),
            (rows_of(g, 8, width), (count, 8, width), f32),
        ],
        [
            pltpu.VMEM((width, HEADS * width), f32),
            pltpu.VMEM((width, width), f32),
            pltpu.VMEM((g, 2 * CZ, HEADS * width), bf16),
            pltpu.VMEM((g, width, 2 * CZ), bf16),
            pltpu.SMEM((1,), f32),
        ],
        (info, norms, bias, other_bias, qkv, qkv, qkv),
    )


def middle(info, wide, down, small, gains, zt, zbt, o, r, tgt, nbr):
    count, _, width = zt.shape
    g = group_of(count, MIDDLE_ROWS)
    return call(
        middle_kernel,
        "middle",
        30,
        count // g,
        [
            SMEM,
            whole((CZ, WIDE)),
            whole((FF, CZ)),
            whole(small.shape),
            whole(gains.shape),
            rows_of(g, CZ, width),
            rows_of(g, CZ, width),
            rows_of(g, CZ, width),
            rows_of(g, 8, width),
            whole(tgt.shape),
            whole(nbr.shape),
        ],
        [
            (rows_of(g, CZ, width), (count, CZ, width), bf16),
            (rows_of(g, 16 * HEADS, width), (count, 16 * HEADS, width), bf16),
            (whole((BLOCKS, CZ, CZ)), (BLOCKS, CZ, CZ), bf16),
            (whole((16, CZ)), (16, CZ), bf16),
        ],
        [
            pltpu.VMEM((BLOCKS, CZ, CZ), f32),
            pltpu.VMEM((2, 128 * MIDDLE_PART), f32),
            pltpu.VMEM((CZ, CZ), f32),
            pltpu.VMEM((CZ, CZ), f32),
            pltpu.VMEM((CZ, CZ), bf16),
            pltpu.VMEM((CZ, CZ), bf16),
            pltpu.VMEM((FF, CZ), bf16),
            pltpu.VMEM((CZ, FF), bf16),
            pltpu.VMEM((BINS, CZ), bf16),
            pltpu.VMEM((CZ, 2 * CZ), bf16),
            pltpu.VMEM((FF, 2 * CZ), bf16),
            pltpu.VMEM((CZ, 2 * BINS), bf16),
        ],
        (info, wide, down, small, gains, zt, zbt, o, r, tgt, nbr),
    )


def score(info, p, vn, do, nd):
    count, _, width = do.shape
    g = group_of(count, SCORE_ROWS)
    shape = (width // count // 2, HEADS * count * (width // CZ), CZ)
    return call(
        score_kernel,
        "score",
        17,
        count // g,
        [
            SMEM,
            rows_of(g, width, HEADS * width),
            rows_of(g, width, CZ),
            rows_of(g, CZ, width),
            rows_of(g, 16 * HEADS, width),
        ],
        [(whole(shape), shape, bf16)] * 2,
        [
            pltpu.VMEM((width, HEADS * width), f32),
            pltpu.VMEM((g, 2 * CZ, HEADS * width), bf16),
            pltpu.VMEM((g, width, 2 * CZ), bf16),
            pltpu.VMEM((HEADS, width, width), f32),
        ],
        (info, p, vn, do, nd),
    )


def late_sums(parcel, keep, got, zbt):
    count, _, width = zbt.shape
    shape = (keep.shape[0] + 8, CZ)
    g = group_of(count, LATE_ROWS)
    tall = HEADS * count * (width // CZ)
    return call(
        late_kernel,
        "late",
        3,
        count // g,
        [
            whole((parcel.shape[0], tall if tall % 16 == 0 else parcel.shape[1], CZ)),
            whole(keep.shape),
            whole(keep.shape),
            rows_of(g, CZ, width),
        ],
        [(whole(shape), shape, f32), (whole(shape), shape, bf16)],
        [pltpu.VMEM((tall, CZ), f32), pltpu.VMEM((CZ, 16), f32)],
        (parcel, keep, got, zbt),
    )


def back(info, p, qkv, vn, do, nd, zbt):
    count, _, width = zbt.shape
    half = 3 * CZ // 2
    g = group_of(count, BACK_ROWS)
    return call(
        back_kernel,
        "back",
        38,
        count // g,
        [
            SMEM,
            rows_of(g, width, HEADS * width),
            rows_of(g, CZ, width),
            rows_of(g, CZ, width, 1),
            rows_of(g, width, CZ),
            rows_of(g, CZ, width),
            rows_of(g, 16 * HEADS, width),
            rows_of(g, CZ, width),
        ],
        [(whole((half, CZ)), (half, CZ), f32)] * 2,
        [
            pltpu.VMEM((3 * CZ, CZ), f32),
            pltpu.VMEM((g, 2 * CZ, HEADS * width), bf16),
            pltpu.VMEM((g, width, HEADS * width), bf16),
            pltpu.VMEM((g, width, 2 * CZ), bf16),
            pltpu.VMEM((3 * CZ, g * width), bf16),
        ],
        (info, p, qkv, qkv, vn, do, nd, zbt),
    )


def finish(crops, rows, *args):
    wide, down, gains, small = args[8], args[9], args[10], args[12]
    shapes = []
    for weight in (wide, down):
        shapes += [weight.shape, weight.shape[:1], weight.shape[1:], weight.shape]
    shapes += [gains.shape] * 3 + [small.shape] * 3
    return call(
        partial(finish_kernel, crops, rows),
        "finish",
        4,
        1,
        [SMEM] + [whole(x.shape) for x in args[1:]],
        [(whole(shape), shape, f32) for shape in shapes],
        [
            pltpu.VMEM((BLOCKS * CZ, CZ), f32),
            pltpu.VMEM((3 * CZ, CZ), f32),
            pltpu.VMEM((CZ, WIDE), f32),
            pltpu.VMEM((FF, CZ), f32),
            pltpu.VMEM((CZ, 1), f32),
            pltpu.VMEM((FF, 1), f32),
            pltpu.VMEM((rows, CZ), f32),
            pltpu.VMEM((1, WIDE), f32),
            pltpu.VMEM((1, CZ), f32),
        ],
        args,
    )


def bits(n):
    return [1 << t for t in reversed(range(n.bit_length() - 1))]


def swap(x, axes, size, mask):
    return lax.ppermute(x, axes, [(i, i ^ mask) for i in range(size)])


def gathered(x, axes, size, masks):
    x = x[None]
    for mask in masks:
        x = jnp.concatenate([x, swap(x, axes, size, mask)], 0)
    return x


def places(me, size, masks):
    apart = jnp.arange(size, dtype=jnp.int32) ^ me
    place = jnp.zeros((size,), jnp.int32)
    for t, mask in enumerate(masks):
        place = place + jnp.where((apart & mask) != 0, 1 << t, 0)
    return place


def build(crops, rows):
    both = ("crop", "row")
    devices = crops * rows
    row_masks = bits(rows)
    all_masks = row_masks[:-1] + [m * rows for m in bits(crops)] + row_masks[-1:]

    sides = [[2 * chip + side for chip in range(devices // 2)] for side in range(2)]
    row_sides = [[2 * chip + side for chip in range(rows // 2)] for side in range(2)]

    def body(
        pair,
        crop_len,
        targets,
        neighbours,
        wide,
        wide_rows,
        wide_cols,
        down,
        down_rows,
        down_cols,
        gains,
        gain_second,
        small,
        small_second,
    ):
        row_index = lax.axis_index("row")
        crop_index = lax.axis_index("crop")
        count_rows, width = pair.shape[1], pair.shape[2]
        info = jnp.stack([row_index, crop_index, crop_len[0], jnp.int32(count_rows)])

        pack = pack_weights(
            devices // 2, wide, down, wide_rows, down_rows, wide_cols, down_cols
        )
        small_t = small.T
        packs = lax.all_to_all(pack, both, 0, 0, axis_index_groups=sides, tiled=True)
        zt, zbt, bias_part = front(pair[0], gains, small_t)
        bias = gathered(bias_part, "row", rows, row_masks[:-1])
        other_packs = swap(packs, both, devices, 1)
        qkv, vn, norms, wide_full, down_full, done = project(
            crops, rows, info, packs, other_packs, zbt
        )
        bias = bias + done.astype(bf16)[..., None, None]
        other_bias = swap(bias, "row", rows, row_masks[-1])
        if count_rows % 8:
            bias = jnp.concatenate([bias, other_bias], 0)
            bias = jnp.take(bias, places(row_index, rows, row_masks), axis=0)
            bias = bias.transpose(1, 0, 2, 3).reshape(1, HEADS, width, width)
            other_bias = bias
        bias_masks = [] if count_rows % 8 else row_masks
        p, o, r = attend(bias_masks, info, norms, bias, other_bias, qkv)
        do, nd, early, scalars = middle(
            info,
            wide_full,
            down_full,
            small_t,
            gains,
            zt,
            zbt,
            o,
            r,
            targets,
            neighbours,
        )

        early = lax.all_to_all(early.reshape(devices, -1, CZ), both, 0, 0, tiled=True)
        keep, give = score(info, p, vn, do, nd)
        early, keep, give = lax.optimization_barrier((early, keep, give))
        got = swap(give, both, devices, 1)
        early = jnp.concatenate([jnp.sum(early.astype(f32), 0).astype(bf16), scalars], 0)
        early_lines = early.shape[0]
        early = gathered(early, both, devices, [1])
        early = early.reshape(-1, CZ)
        early = jnp.broadcast_to(early[None], (rows // 2, *early.shape))
        parcel = jnp.concatenate([(keep.astype(f32) + got.astype(f32)).astype(bf16), early], 1)
        parcel, do = lax.optimization_barrier((parcel, do))
        parcel = lax.all_to_all(parcel, "row", 0, 0, axis_index_groups=row_sides, tiled=True)
        keep, give = back(info, p, qkv, vn, do, nd, zbt)
        got = swap(give, both, devices, 1)
        across = swap(parcel[:, -2 * early_lines :], both, devices, rows)
        keep, send = late_sums(parcel, keep, got, zbt)
        for n, mask in enumerate(all_masks[:-1]):
            if n == 0:
                keep = keep + swap(send, both, devices, mask).astype(f32)
            else:
                if n == len(all_masks) - 2:
                    keep = keep + across[0, -16:-15].astype(f32) * 0.0
                keep = keep + swap(keep, both, devices, mask)
        other = swap(keep, both, devices, 1)
        scalars = jnp.stack([parcel[:, -2 * early_lines :], across])
        scalars = scalars.reshape(crops, rows, -1, CZ)[:, :, -16, :6]
        scalars = jnp.sum(scalars.astype(f32), (0, 1)).reshape(3, 2)
        loss_sum, pair_count = jnp.sum(scalars[:, 0]), jnp.sum(scalars[:, 1])
        (
            wide_g,
            wide_r_new,
            wide_c_new,
            wide_new,
            down_g,
            down_r_new,
            down_c_new,
            down_new,
            gain_grad,
            gain_s,
            gain_n,
            small_grad,
            small_s,
            small_n,
        ) = finish(
            crops,
            rows,
            info,
            keep,
            other,
            parcel,
            across,
            packs,
            other_packs,
            wide_full,
            wide,
            down,
            gains,
            gain_second,
            small_t,
            small_second.T,
        )
        return (
            loss_sum,
            pair_count,
            wide_g,
            wide_r_new,
            wide_c_new,
            wide_new,
            down_g,
            down_r_new,
            down_c_new,
            down_new,
            gain_grad,
            gain_s,
            gain_n,
            small_grad.T,
            small_s.T,
            small_n.T,
        )

    return body


def solution(mesh):
    return jax.shard_map(
        build(mesh.shape["crop"], mesh.shape["row"]),
        mesh=mesh,
        in_specs=(
            P("crop", "row", None, None),
            P("crop"),
            P("crop", "row", None),
            P("crop", "row", None),
            P("row", "crop"),
            P("row"),
            P("crop"),
            P("row", "crop"),
            P("row"),
            P("crop"),
            P(),
            P(),
            P(),
            P(),
        ),
        out_specs=(
            P(),
            P(),
            P("row", "crop"),
            P("row"),
            P("crop"),
            P("row", "crop"),
            P("row", "crop"),
            P("row"),
            P("crop"),
            P("row", "crop"),
            P(),
            P(),
            P(),
            P(),
            P(),
            P(),
        ),
        check_vma=False,
    )
```

```python
import math
from functools import partial

import jax
import jax.numpy as jnp
from jax import lax
from jax.experimental import pallas as pl
from jax.experimental.pallas import tpu as pltpu
from jax.sharding import PartitionSpec as P

CZ = 128
HEADS = 4
HEAD_DIM = 32
FF = 512
BINS = 64
WIDE = 5 * CZ + FF

DECAY = 1.0 - 10.0 ** (-0.8)
TINY = 1e-30
LOG2E = math.log2(math.e)
ROOT = 1.0 / math.sqrt(HEAD_DIM)
BLK = 256
SAFE = 40.0
STATS = 256

GATE_BLOCK, OUT_BLOCK, IN_BLOCK, DOWN_BLOCK, HEAD_BLOCK, BLOCKS = 0, 1, 2, 6, 10, 12

f32 = jnp.float32
bf16 = jnp.bfloat16


def dot(a, b):
    return lax.dot_general(a, b, (((1,), (0,)), ((), ())), preferred_element_type=f32)


def dot_nt(a, b):
    return lax.dot_general(a, b, (((1,), (1,)), ((), ())), preferred_element_type=f32)


def rounded(v):
    return v.astype(bf16).astype(f32)


def halves(v):
    high = v.astype(bf16)
    return high, (v - high.astype(f32)).astype(bf16)


def normed(x):
    centre = x - jnp.sum(x, 0, keepdims=True) * (1.0 / CZ)
    var = jnp.sum(centre * centre, 0, keepdims=True) * (1.0 / CZ)
    inv = lax.rsqrt(var + 1e-05)
    return centre * inv, inv


def normed_back(d, xhat, inv):
    one = jnp.sum(d, 0, keepdims=True) * (1.0 / CZ)
    two = jnp.sum(d * xhat, 0, keepdims=True) * (1.0 / CZ)
    return inv * (d - one - xhat * two)


def sigmoid(x):
    return 0.5 * jnp.tanh(0.5 * x) + 0.5


def wider(column, x):
    return jnp.concatenate([column] * (x.shape[1] // 128), 1)


def lanes(ref):
    return jnp.concatenate([ref[g] for g in range(ref.shape[0])], 1)


def spread(ref, x):
    width = ref.shape[2]
    for g in range(ref.shape[0]):
        ref[g] = x[:, g * width : (g + 1) * width]


def columns_of(gains_ref, which, scratch):
    scratch[...] = jnp.broadcast_to(gains_ref[...].T[:, which : which + 1], (CZ, CZ))


def place(source, me, masks):
    apart = source ^ me
    where = 0
    for t, mask in enumerate(masks):
        where = where + ((apart >> (mask.bit_length() - 1)) & 1) * (1 << t)
    return where


def pack_kernel(
    wide_ref, down_ref, wide_rows_ref, down_rows_ref, wide_cols_ref, down_cols_ref, pack_ref, pack
):
    lines, cols = wide_ref.shape
    span = down_ref.shape[1]
    pack[...] = jnp.zeros_like(pack)
    for at, ref in ((0, wide_rows_ref), (lines, down_rows_ref)):
        some = ref[...].reshape(1, -1)
        upper = rounded(some)
        pack[0:1, at : at + some.shape[1]] = upper
        pack[1:2, at : at + some.shape[1]] = some - upper
    stats = jnp.concatenate(
        [wide_cols_ref[...].reshape(1, -1), down_cols_ref[...].reshape(1, -1)], 1
    )
    for part in range(-(-stats.shape[1] // STATS)):
        some = stats[:, part * STATS : (part + 1) * STATS]
        upper = rounded(some)
        pack[2 + part : 3 + part, : some.shape[1]] = upper
        pack[5 + part : 6 + part, : some.shape[1]] = some - upper
    pack[:lines, STATS : STATS + cols] = wide_ref[...]
    for part in range(FF // CZ):
        at = STATS + cols + part * span
        pack[:lines, at : at + span] = down_ref[part * lines : (part + 1) * lines, :]
    for peer in range(pack_ref.shape[0]):
        pack_ref[peer] = pack[...].astype(bf16)


def front_kernel(
    pair_ref, gains_ref, small_ref, zt_ref, zbt_ref, bias_ref, gain, wb, part
):
    rows, width, _ = pair_ref.shape
    step = pl.program_id(0)

    @pl.when(step == 0)
    def _():
        columns_of(gains_ref, 0, gain)
        wb[...] = small_ref[:16].astype(bf16)

    x = pair_ref[...].astype(f32).reshape(rows * width, CZ).T
    spread(zt_ref, x.astype(bf16))
    xhat, _ = normed(x)
    zb = (xhat * wider(gain[...], x)).astype(bf16)
    spread(zbt_ref, zb)
    bias = dot(wb[...], zb)
    for g in range(rows):
        for h in range(HEADS):
            part[h, pl.ds(step * rows + g, 1), :] = bias[h : h + 1, g * width : (g + 1) * width]

    @pl.when(step == pl.num_programs(0) - 1)
    def _():
        bias_ref[...] = part[...].astype(bf16)


def pick(info_ref, mine_ref, other_ref, crop, row, rows):
    chip = crop * (rows // 2) + row // 2
    side = info_ref[0] & 1
    return jnp.where(
        side == row % 2, mine_ref[chip].astype(f32), other_ref[chip].astype(f32)
    )


def project_kernel(
    crops,
    rows,
    info_ref,
    mine_ref,
    other_ref,
    zbt_ref,
    qkv_ref,
    vn_ref,
    norm_ref,
    wide_ref,
    down_ref,
    done_ref,
    wide_s,
    down_s,
    wqt,
):
    lines, cols, span = CZ // rows, WIDE // crops, CZ // crops

    @pl.when(pl.program_id(0) == 0)
    def _():
        for c in range(crops):
            for r in range(rows):
                block = pick(info_ref, mine_ref, other_ref, c, r, rows)[:lines]
                wide_s[r * lines : (r + 1) * lines, c * cols : (c + 1) * cols] = block[
                    :, STATS : STATS + cols
                ]
                for part in range(FF // CZ):
                    at = (r * (FF // CZ) + part) * lines
                    left = STATS + cols + part * span
                    down_s[at : at + lines, c * span : (c + 1) * span] = block[:, left : left + span]
        wide_ref[...] = wide_s[...].astype(bf16)
        down_ref[...] = down_s[...].astype(bf16)
        wqt[...] = wide_s[:, : 3 * CZ].T.astype(bf16)
        done_ref[...] = jnp.zeros_like(done_ref)

    qkv = dot(wqt[...], lanes(zbt_ref)).astype(bf16)
    spread(qkv_ref, qkv)
    q = qkv[:CZ].astype(f32)
    k = qkv[CZ : 2 * CZ].astype(f32)
    vn_ref[...] = qkv[2 * CZ :].T.reshape(vn_ref.shape)
    norm_ref[...] = jnp.concatenate(
        [
            jnp.sum((x * x)[h * HEAD_DIM : (h + 1) * HEAD_DIM], 0, keepdims=True)
            for x in (q, k)
            for h in range(HEADS)
        ],
        0,
    )


def attend_kernel(
    masks,
    info_ref,
    norm_ref,
    bias_ref,
    other_bias_ref,
    q_ref,
    k_ref,
    v_ref,
    p_ref,
    o_ref,
    r_ref,
    biast,
    nat,
    qbd,
    kk,
    bound,
):
    group, _, width = q_ref.shape
    rows = bias_ref.shape[2]
    shards = width // rows
    step = pl.program_id(0)

    @pl.when(step == 0)
    def _():
        top = 0.0
        key = lax.broadcasted_iota(jnp.int32, (1, width), 1)
        kb = jnp.where(key < info_ref[2], 0.0, -1000000000.0 * LOG2E)
        for h in range(HEADS):
            for s in range(shards):
                at = place(s, info_ref[0], masks[:-1])
                block = bias_ref[at, h].astype(f32)
                if shards > 1:
                    here = (info_ref[0] & 1) == s % 2
                    block = jnp.where(here, block, other_bias_ref[at, h].astype(f32))
                nat[s * rows : (s + 1) * rows, :] = block
            top = jnp.maximum(top, jnp.max(jnp.abs(nat[...])))
            biast[:, h * width : (h + 1) * width] = (nat[...] * LOG2E + kb).T
        bound[0] = top * LOG2E
        qbd[...] = jnp.zeros_like(qbd)
        r_ref[...] = jnp.zeros_like(r_ref)

    def attend(shift):
        for g in range(group):
            high, low = halves(q_ref[g].astype(f32) * (LOG2E * ROOT))
            for h in range(HEADS):
                a, b = h * HEAD_DIM, (h + 1) * HEAD_DIM
                qbd[g, a:b, h * width : (h + 1) * width] = high[a:b]
                qbd[g, CZ + a : CZ + b, h * width : (h + 1) * width] = low[a:b]
            kn = k_ref[g].T
            kk[g, :, :CZ] = kn
            kk[g, :, CZ:] = kn
            sums = []
            for c in range(0, HEADS * width, BLK):
                s = dot(kk[g], qbd[g, :, c : c + BLK]) + biast[:, c : c + BLK]
                if shift:
                    s = s - jnp.max(s, 0, keepdims=True)
                e = jnp.exp2(s)
                sums.append(jnp.sum(e, 0, keepdims=True))
                p_ref[g, :, c : c + BLK] = e.astype(bf16)
            r = 1.0 / jnp.concatenate(sums, 1)
            for h in range(HEADS):
                a, b = h * HEAD_DIM, (h + 1) * HEAD_DIM
                mine = r[:, h * width : (h + 1) * width]
                r_ref[g, h : h + 1] = mine
                o_ref[g, a:b] = dot(v_ref[g, a:b], p_ref[g, :, h * width : (h + 1) * width]) * mine

    norms = jnp.max(norm_ref[...], 1, keepdims=True)
    reach = jnp.max(jnp.sqrt(norms[:HEADS] * norms[HEADS:])) * (1.01 * LOG2E * ROOT)
    safe = reach + bound[0] < SAFE

    @pl.when(safe)
    def _():
        attend(False)

    @pl.when(jnp.logical_not(safe))
    def _():
        attend(True)


def middle_kernel(
    info_ref,
    wide_ref,
    down_ref,
    head_ref,
    gains_ref,
    zt_ref,
    zbt_ref,
    o_ref,
    r_ref,
    tgt_ref,
    nbr_ref,
    do_ref,
    nd_ref,
    grads_ref,
    scalars_ref,
    acc,
    sums,
    g1,
    g2,
    wgt,
    wot,
    wint,
    wdownt,
    wht,
    wo2,
    wdown2,
    wh2,
):
    step = pl.program_id(0)

    @pl.when(step == 0)
    def _():
        wo = wide_ref[:, 4 * CZ : 5 * CZ]
        wot[...] = wo.T
        wgt[...] = wide_ref[:, 3 * CZ : 4 * CZ].T
        wint[...] = wide_ref[:, 5 * CZ :].T * 0.5
        wdownt[...] = down_ref[...].T
        head = head_ref[...][HEADS:]
        wht[...] = head.astype(bf16)
        head = head.T.astype(bf16)
        wo2[...] = jnp.concatenate([wo, wo], 1)
        wdown2[...] = jnp.concatenate([down_ref[...], down_ref[...]], 1) * 0.5
        wh2[...] = jnp.concatenate([head, head], 1)
        acc[...] = jnp.zeros_like(acc)
        columns_of(gains_ref, 1, g1)
        columns_of(gains_ref, 2, g2)
        sums[...] = jnp.zeros_like(sums)

    group, _, width = o_ref.shape
    first = step * group

    def add(block, grad):
        for c in range(0, grad.shape[1], CZ):
            acc[block + c // CZ] += grad[:, c : c + CZ]

    def stages(low, high):
        spots = [divmod(block * 128, width) for block in range(low, high)]

        def mine(ref):
            return jnp.concatenate([ref[g, :, at : at + 128] for g, at in spots], 1)

        def line(ref):
            return jnp.concatenate(
                [ref[0, pl.ds(first + g, 1), :][:, at : at + 128] for g, at in spots], 1
            )

        def out(ref, x):
            for n, (g, at) in enumerate(spots):
                ref[g, :, at : at + 128] = x[:, n * 128 : (n + 1) * 128]

        o = mine(o_ref)
        zb = mine(zbt_ref)
        gate = sigmoid(dot(wgt[...], zb))
        gain1 = wider(g1[...], o)
        gain2 = wider(g2[...], o)
        og = (o * gate).astype(bf16)
        z1 = mine(zt_ref).astype(f32) + dot(wot[...], og)
        yield
        xhat1, inv1 = normed(z1)
        zb2 = (xhat1 * gain1).astype(bf16)
        yield
        hidden, slopes = [], []
        for f in range(0, FF, CZ):
            hid = dot(wint[f : f + CZ], zb2)
            t = jnp.tanh(hid)
            sg = 1.0 + t
            act = hid * sg
            hidden.append(act.astype(bf16))
            slopes.append(sg + act * (1.0 - t))
            yield
        a = jnp.concatenate(hidden, 0)
        z2 = z1 + dot(wdownt[...], a)
        yield
        xhat2, inv2 = normed(z2)
        zb3 = (xhat2 * gain2).astype(bf16)
        logits = dot(wht[...], zb3)
        yield
        top = jnp.max(logits, 0, keepdims=True)
        ex = jnp.exp(logits - top)
        total = jnp.sum(ex, 0, keepdims=True)
        hot = lax.broadcasted_iota(jnp.int32, logits.shape, 0) == line(tgt_ref)
        picked = jnp.sum(jnp.where(hot, logits, 0.0), 0, keepdims=True)
        column = lax.broadcasted_iota(jnp.int32, (1, 128), 1)
        length = info_ref[2]
        valid = jnp.concatenate(
            [
                column + at < jnp.where(info_ref[0] * info_ref[3] + first + g < length, length, 0)
                for g, at in spots
            ],
            1,
        )
        mask = jnp.where((line(nbr_ref) > 0) & valid, 1.0, 0.0)
        at = slice(0, mask.shape[1])
        sums[0:1, at] += (jnp.log(total) + top - picked) * mask
        sums[1:2, at] += mask
        dl = ex * (mask / total) - jnp.where(hot, mask, 0.0)
        dl2 = jnp.concatenate(halves(dl), 0)
        yield
        add(HEAD_BLOCK, dot_nt(dl2, zb3))
        dzb3 = rounded(dot(wh2[...], dl2))
        yield
        dz2 = normed_back(dzb3 * gain2, xhat2, inv2)
        high2, low2 = halves(dz2)
        both2 = jnp.concatenate([high2, low2], 0)
        yield
        dh = []
        for f in range(0, FF, CZ):
            dh.append((dot(wdown2[f : f + CZ], both2) * slopes[f // CZ]).astype(bf16))
            yield
        dh = jnp.concatenate(dh, 0)
        add(DOWN_BLOCK, dot_nt(high2, a))
        yield
        dzb2 = rounded(dot(wide_ref[:, 5 * CZ :], dh))
        yield
        add(IN_BLOCK, dot_nt(zb2, dh))
        dz1 = dz2 + normed_back(dzb2 * gain1, xhat1, inv1)
        high1, low1 = halves(dz1)
        yield
        add(OUT_BLOCK, dot_nt(og, high1))
        dog = rounded(dot(wo2[...], jnp.concatenate([high1, low1], 0)))
        yield
        do = dog * gate
        doo = do * o
        add(GATE_BLOCK, dot_nt(zb, (doo * (1.0 - gate)).astype(bf16)))
        yield
        r = mine(r_ref)
        parts, minus = [], []
        for h in range(HEADS):
            x, y = h * HEAD_DIM, (h + 1) * HEAD_DIM
            share = r[h : h + 1]
            parts.append((do[x:y] * share).astype(bf16))
            minus.append(-jnp.sum(doo[x:y], 0, keepdims=True) * share)
        out(do_ref, jnp.concatenate(parts, 0))
        out(nd_ref, jnp.concatenate(minus + minus, 0))

    blocks = group * width // 128
    running = [
        stages(low, min(low + MIDDLE_PART, blocks)) for low in range(0, blocks, MIDDLE_PART)
    ]
    turn = 0
    waiting = list(enumerate(running))
    while waiting:
        for item in list(waiting):
            if turn >= item[0] * MIDDLE_LAG and next(item[1], item) is item:
                waiting.remove(item)
        turn += 1

    @pl.when(step == pl.num_programs(0) - 1)
    def _():
        for block in range(BLOCKS):
            grads_ref[block] = acc[block].astype(bf16)
        both = jnp.sum(sums[...], 1, keepdims=True)
        lane = lax.broadcasted_iota(jnp.int32, scalars_ref.shape, 1)
        out = jnp.zeros(scalars_ref.shape, f32)
        for part in range(3):
            upper = rounded(both)
            for which in range(2):
                out = jnp.where(lane == 2 * part + which, upper[which : which + 1], out)
            both = both - upper
        scalars_ref[...] = out.astype(bf16)


def score_kernel(info_ref, p_ref, vn_ref, do_ref, nd_ref, keep_ref, give_ref, acc, dobd, vv, nat):
    group, _, width = do_ref.shape
    step = pl.program_id(0)

    @pl.when(step == 0)
    def _():
        acc[...] = jnp.zeros_like(acc)
        prepare(dobd, vv)

    for g in range(group):
        score_operands(g, vn_ref, do_ref, nd_ref, dobd, vv)
        for c in range(0, HEADS * width, BLK):
            acc[:, c : c + BLK] += dot(vv[g], dobd[g, :, c : c + BLK]) * p_ref[
                g, :, c : c + BLK
            ].astype(f32)

    @pl.when(step == pl.num_programs(0) - 1)
    def _():
        chips, tall, _ = keep_ref.shape
        lines = width // (2 * chips)
        first = (info_ref[0] & 1) == 0
        for h in range(HEADS):
            nat[h] = acc[:, h * width : (h + 1) * width].T
        for chip in range(chips):
            sides = [
                jnp.concatenate(
                    [
                        nat[h, (2 * chip + side) * lines : (2 * chip + side + 1) * lines, c : c + CZ]
                        for c in range(0, width, CZ)
                        for h in range(HEADS)
                    ],
                    0,
                )
                for side in range(2)
            ]
            keep_ref[chip] = jnp.where(first, sides[0], sides[1]).astype(bf16)
            give_ref[chip] = jnp.where(first, sides[1], sides[0]).astype(bf16)


def prepare(dobd, vv):
    dobd[...] = jnp.zeros_like(dobd)
    vv[...] = jnp.ones_like(vv)


def score_operands(g, vn_ref, do_ref, nd_ref, dobd, vv):
    width = do_ref.shape[2]
    vv[g, :, :CZ] = vn_ref[g]
    for h in range(HEADS):
        a, b = h * HEAD_DIM, (h + 1) * HEAD_DIM
        at = slice(h * width, (h + 1) * width)
        dobd[g, a:b, at] = do_ref[g, a:b]
        minus = nd_ref[g, h : h + 1]
        upper = rounded(minus)
        dobd[g, CZ : CZ + 16, at] = jnp.concatenate(
            [upper, minus - upper, jnp.zeros((14, width), f32)], 0
        ).astype(bf16)


def back_kernel(
    info_ref,
    p_ref,
    q_ref,
    k_ref,
    vn_ref,
    do_ref,
    nd_ref,
    zbt_ref,
    keep_ref,
    give_ref,
    dwq,
    dobd,
    dst,
    vv,
    dproj,
):
    group, _, width = do_ref.shape
    step = pl.program_id(0)

    @pl.when(step == 0)
    def _():
        dwq[...] = jnp.zeros_like(dwq)
        prepare(dobd, vv)

    for g in range(group):
        score_operands(g, vn_ref, do_ref, nd_ref, dobd, vv)
        for c in range(0, HEADS * width, BLK):
            ds = dot(vv[g], dobd[g, :, c : c + BLK]) * p_ref[g, :, c : c + BLK].astype(f32)
            dst[g, :, c : c + BLK] = ds.astype(bf16)
        at = slice(g * width, (g + 1) * width)
        for h in range(HEADS):
            a, b = h * HEAD_DIM, (h + 1) * HEAD_DIM
            mine = dst[g, :, h * width : (h + 1) * width]
            dproj[a:b, at] = (dot(k_ref[g, a:b], mine) * ROOT).astype(bf16)
            dproj[CZ + a : CZ + b, at] = (dot_nt(q_ref[g, a:b], mine) * ROOT).astype(bf16)
            dproj[2 * CZ + a : 2 * CZ + b, at] = dot_nt(
                do_ref[g, a:b], p_ref[g, :, h * width : (h + 1) * width]
            ).astype(bf16)
    grad = dot_nt(lanes(zbt_ref), dproj[...])
    for block in range(3):
        dwq[block * CZ : (block + 1) * CZ, :] += grad[:, block * CZ : (block + 1) * CZ]

    @pl.when(step == pl.num_programs(0) - 1)
    def _():
        half = keep_ref.shape[0]
        first = (info_ref[0] & 1) == 0
        one, two = dwq[:half, :], dwq[half:, :]
        keep_ref[...] = jnp.where(first, one, two)
        give_ref[...] = jnp.where(first, two, one)


def factored(grad_ref, rows, cols, weight_ref, crop, row_start, scratch, outs):
    grad_out, rows_out, cols_out, new_out = outs
    lines, span = weight_ref.shape
    grad = grad_ref[...]
    count, columns = grad.shape
    sq = grad * grad
    rows_new = DECAY * rows + (1.0 - DECAY) * (jnp.sum(sq, 1, keepdims=True) / columns + TINY)
    cols_new = DECAY * cols + (1.0 - DECAY) * (jnp.sum(sq, 0, keepdims=True) / count + TINY)
    mean = jnp.sum(rows_new, 0, keepdims=True) / count
    rows_factor = mean / rows_new
    cols_factor = 1.0 / cols_new
    size = jnp.sum(jnp.sum(sq * rows_factor * cols_factor, 1, keepdims=True), 0, keepdims=True)
    clip = jnp.maximum(0.1, jnp.sqrt(size / (count * columns)))
    scratch[...] = rows_factor
    mine = grad_ref[pl.ds(row_start, lines), :]
    update = mine * lax.rsqrt((1.0 / scratch[pl.ds(row_start, lines), :]) * (1.0 / cols_factor))
    update = weight_step(update, clip)
    scratch[...] = rows_new
    own_rows = jnp.broadcast_to(scratch[pl.ds(row_start, lines), :], (lines, CZ))
    rows_out[...] = own_rows.T[0]

    def own(x):
        part = x[:, :span]
        for c in range(1, columns // span):
            part = jnp.where(crop == c, x[:, c * span : (c + 1) * span], part)
        return part

    grad_out[...] = own(mine)
    cols_out[...] = own(cols_new)[0]
    new_out[...] = weight_ref[...] - own(update)


def weight_step(update, clip):
    return update * (0.03 / clip)


def plain(weight, grad, second, rate, outs):
    second_new = DECAY * second + (1.0 - DECAY) * (grad * grad + TINY)
    update = grad * lax.rsqrt(second_new)
    square = jnp.sum(jnp.sum(update * update, 1, keepdims=True), 0, keepdims=True)
    clip = jnp.maximum(1.0, jnp.sqrt(square / (grad.shape[0] * grad.shape[1])))
    outs[0][...] = grad
    outs[1][...] = second_new
    outs[2][...] = weight - rate * update / clip


def finish_kernel(
    crops,
    rows,
    info_ref,
    keep_ref,
    other_ref,
    spread_ref,
    across_ref,
    packs_ref,
    other_packs_ref,
    full_ref,
    wide_ref,
    down_ref,
    gains_ref,
    gain_second_ref,
    small_ref,
    small_second_ref,
    *refs,
):
    outs, (flat, late_ref, wide_s, down_s, wide_c, down_c, table, wide_cols, down_cols) = (
        refs[:14],
        refs[14:],
    )
    row, crop = info_ref[0], info_ref[1]
    side = row & 1
    half = 3 * CZ // 2
    mine, other = keep_ref[...], other_ref[...]
    late_ref[:half, :] = jnp.where(side == 0, mine[:half], other[:half])
    late_ref[half:, :] = jnp.where(side == 0, other[:half], mine[:half])
    pbias = mine[half:] + other[half:]

    lines = BLOCKS * CZ // (crops * rows)
    height = lines + 16
    tail = jnp.zeros((1, CZ), f32)
    for c in range(crops):
        for r in range(rows):
            at = (c * rows + r) * lines
            which = (r % 2) ^ side
            block = jnp.zeros((height, CZ), f32)
            for p in range(2):
                part = slice(p * height, (p + 1) * height)
                here = spread_ref[r // 2, part].astype(f32)
                there = across_ref[r // 2, part].astype(f32)
                block = jnp.where(which == p, jnp.where(c == crop, here, there), block)
            flat[at : at + lines, :] = block[:lines]
            tail += block[lines : lines + 1]
    scale = 1.0 / (tail[:, 1:2] + tail[:, 3:4] + tail[:, 5:6])

    def early(block):
        return flat[block * CZ : (block + 1) * CZ, :] * scale

    for block in range(3):
        wide_s[:, block * CZ : (block + 1) * CZ] = (
            late_ref[block * CZ : (block + 1) * CZ, :] * scale
        )
    for block in range(GATE_BLOCK, DOWN_BLOCK):
        wide_s[:, (3 + block) * CZ : (4 + block) * CZ] = early(block)
    for block in range(DOWN_BLOCK, HEAD_BLOCK):
        down_s[(block - DOWN_BLOCK) * CZ : (block - DOWN_BLOCK + 1) * CZ, :] = early(block).T
    head = early(HEAD_BLOCK)
    pbias = pbias[:HEADS] * scale
    small_grad = jnp.concatenate([pbias, head[:BINS] + head[BINS:]], 0)
    small = small_ref[...]
    plain(small, small_grad, small_second_ref[...], 0.03, outs[11:])

    through = wide_s[...] * full_ref[...].astype(f32)
    behind = small_grad * rounded(small)
    lane = lax.broadcasted_iota(jnp.int32, (CZ, CZ), 1)
    gain_grad = jnp.where(
        lane == 0,
        jnp.sum(through[:, : 4 * CZ], 1, keepdims=True),
        jnp.sum(through[:, 5 * CZ :], 1, keepdims=True),
    ).T
    gain_grad = jnp.concatenate(
        [
            gain_grad[:1] + jnp.sum(behind[:HEADS], 0, keepdims=True),
            gain_grad[1:2],
            jnp.sum(behind[HEADS:], 0, keepdims=True),
        ],
        0,
    )
    gains = gains_ref[...]
    plain(gains, gain_grad / gains, gain_second_ref[...], 0.3, outs[8:11])

    per, down_per = CZ // rows, FF // rows
    for r in range(rows):
        block = pick(info_ref, packs_ref, other_packs_ref, 0, r, rows)
        table[r : r + 1, :] = block[0:1, :CZ] + block[1:2, :CZ]

    def column(size, start):
        tall = jnp.broadcast_to(table[...][:, None, :], (rows, size, CZ)).reshape(rows * size, CZ)
        lane = lax.broadcasted_iota(jnp.int32, tall.shape, 1)
        line = lax.broadcasted_iota(jnp.int32, tall.shape, 0)
        return jnp.sum(jnp.where(lane == start + line % size, tall, 0.0), 1, keepdims=True)

    cols, span = WIDE // crops, CZ // crops
    for c in range(crops):
        block = pick(info_ref, packs_ref, other_packs_ref, c, 0, rows)[:, :STATS]
        block = block[2:5] + block[5:8]
        stats = jnp.concatenate([block[part : part + 1] for part in range(3)], 1)
        wide_cols[:, c * cols : (c + 1) * cols] = stats[:, :cols]
        down_cols[:, c * span : (c + 1) * span] = stats[:, cols : cols + span]
    factored(
        wide_s,
        column(per, 0),
        wide_cols[...],
        wide_ref,
        crop,
        row * wide_ref.shape[0],
        wide_c,
        outs[:4],
    )
    factored(
        down_s,
        column(down_per, per),
        down_cols[...],
        down_ref,
        crop,
        row * down_ref.shape[0],
        down_c,
        outs[4:8],
    )


def late_kernel(spread_ref, keep_ref, got_ref, zbt_ref, out_ref, send_ref, dbias, acc):
    group, _, width = zbt_ref.shape
    tall = dbias.shape[0]
    lines = tall // (HEADS * (width // CZ))
    step = pl.program_id(0)

    @pl.when(step == 0)
    def _():
        total = spread_ref[0, :tall].astype(f32)
        for chip in range(1, spread_ref.shape[0]):
            total += spread_ref[chip, :tall].astype(f32)
        dbias[...] = rounded(total)
        acc[...] = jnp.zeros_like(acc)

    some = jnp.concatenate(
        [
            dbias[pl.ds(c * HEADS * lines + step * group + g, HEADS, stride=lines), :]
            for g in range(group)
            for c in range(width // CZ)
        ],
        1,
    )
    some = jnp.concatenate([some, jnp.zeros((16 - HEADS, some.shape[1]), f32)], 0)
    acc[...] += dot_nt(lanes(zbt_ref), some.astype(bf16))

    @pl.when(step == pl.num_programs(0) - 1)
    def _():
        half = keep_ref.shape[0]
        for at, x in ((0, keep_ref[...] + got_ref[...]), (half, acc[...].T[:8])):
            out_ref[at : at + x.shape[0], :] = rounded(x)
        send_ref[...] = out_ref[...].astype(bf16)


def whole(shape):
    return pl.BlockSpec(shape, lambda i: (0,) * len(shape))


def rows_of(group, lines, columns, line=0, column=0):
    return pl.BlockSpec((group, lines, columns), lambda i: (i, line, column))


def of(shape, dtype):
    return jax.ShapeDtypeStruct(shape, dtype)


SMEM = pl.BlockSpec(memory_space=pltpu.SMEM)


def call(kernel, name, micros, grid, in_specs, outs, scratch, args, mebibytes=52):
    return pl.pallas_call(
        kernel,
        grid=(grid,),
        in_specs=in_specs,
        out_specs=[o[0] for o in outs],
        out_shape=[of(o[1], o[2]) for o in outs],
        scratch_shapes=scratch,
        compiler_params=pltpu.CompilerParams(vmem_limit_bytes=mebibytes << 20),
        cost_estimate=pl.CostEstimate(
            flops=int(micros * 8e8), bytes_accessed=1 << 20, transcendentals=0
        ),
        name=name,
    )(*args)


def group_of(count, most):
    return next(g for g in range(most, 0, -1) if count % g == 0)


def pack_weights(peers, wide, down, *stats):
    args = (wide, down, *stats)
    shape = (peers, 8, STATS + wide.shape[1] + (FF // CZ) * down.shape[1])
    return call(
        pack_kernel,
        "pack",
        1,
        1,
        [whole(x.shape) for x in args],
        [(whole(shape), shape, bf16)],
        [pltpu.VMEM(shape[1:], f32)],
        args,
        60,
    )[0]


def front(pair, gains, small):
    count, width = pair.shape[0], pair.shape[1]
    g = group_of(count, FRONT_ROWS)
    return call(
        front_kernel,
        "front",
        6,
        count // g,
        [rows_of(g, width, CZ), whole(gains.shape), whole(small.shape)],
        [
            (rows_of(g, CZ, width), (count, CZ, width), bf16),
            (rows_of(g, CZ, width), (count, CZ, width), bf16),
            (whole((HEADS, count, width)), (HEADS, count, width), bf16),
        ],
        [
            pltpu.VMEM((CZ, CZ), f32),
            pltpu.VMEM((16, CZ), bf16),
            pltpu.VMEM((HEADS, count, width), f32),
        ],
        (pair, gains, small),
    )


def project(crops, rows, info, mine, other, zbt):
    count, _, width = zbt.shape
    g = group_of(count, 8)
    return call(
        partial(project_kernel, crops, rows),
        "project",
        40,
        count // g,
        [SMEM, whole(mine.shape), whole(other.shape), rows_of(g, CZ, width)],
        [
            (rows_of(g, 3 * CZ, width), (count, 3 * CZ, width), bf16),
            (rows_of(g, width, CZ), (count, width, CZ), bf16),
            (pl.BlockSpec((8, g * width), lambda i: (0, i)), (8, count * width), f32),
            (whole((CZ, WIDE)), (CZ, WIDE), bf16),
            (whole((FF, CZ)), (FF, CZ), bf16),
            (whole((1, 1)), (1, 1), f32),
        ],
        [pltpu.VMEM((CZ, WIDE), f32), pltpu.VMEM((FF, CZ), f32), pltpu.VMEM((3 * CZ, CZ), bf16)],
        (info, mine, other, zbt),
    )


FRONT_ROWS = 12
ATTEND_ROWS = 3
MIDDLE_ROWS = 8
MIDDLE_PART = 2
MIDDLE_LAG = 1
SCORE_ROWS = 6
BACK_ROWS = 4
LATE_ROWS = 12


def attend(masks, info, norms, bias, other_bias, qkv):
    count, _, width = qkv.shape
    g = group_of(count, ATTEND_ROWS)
    return call(
        partial(attend_kernel, masks),
        "attend",
        25,
        count // g,
        [
            SMEM,
            pl.BlockSpec((8, g * width), lambda i: (0, i)),
            whole(bias.shape),
            whole(bias.shape),
            rows_of(g, CZ, width),
            rows_of(g, CZ, width, 1),
            rows_of(g, CZ, width, 2),
        ],
        [
            (rows_of(g, width, HEADS * width), (count, width, HEADS * width), bf16),
            (rows_of(g, CZ, width), (count, CZ, width), f32),
            (rows_of(g, 8, width), (count, 8, width), f32),
        ],
        [
            pltpu.VMEM((width, HEADS * width), f32),
            pltpu.VMEM((width, width), f32),
            pltpu.VMEM((g, 2 * CZ, HEADS * width), bf16),
            pltpu.VMEM((g, width, 2 * CZ), bf16),
            pltpu.SMEM((1,), f32),
        ],
        (info, norms, bias, other_bias, qkv, qkv, qkv),
    )


def middle(info, wide, down, small, gains, zt, zbt, o, r, tgt, nbr):
    count, _, width = zt.shape
    g = group_of(count, MIDDLE_ROWS)
    return call(
        middle_kernel,
        "middle",
        30,
        count // g,
        [
            SMEM,
            whole((CZ, WIDE)),
            whole((FF, CZ)),
            whole(small.shape),
            whole(gains.shape),
            rows_of(g, CZ, width),
            rows_of(g, CZ, width),
            rows_of(g, CZ, width),
            rows_of(g, 8, width),
            whole(tgt.shape),
            whole(nbr.shape),
        ],
        [
            (rows_of(g, CZ, width), (count, CZ, width), bf16),
            (rows_of(g, 2 * HEADS, width), (count, 2 * HEADS, width), f32),
            (whole((BLOCKS, CZ, CZ)), (BLOCKS, CZ, CZ), bf16),
            (whole((16, CZ)), (16, CZ), bf16),
        ],
        [
            pltpu.VMEM((BLOCKS, CZ, CZ), f32),
            pltpu.VMEM((2, 128 * MIDDLE_PART), f32),
            pltpu.VMEM((CZ, CZ), f32),
            pltpu.VMEM((CZ, CZ), f32),
            pltpu.VMEM((CZ, CZ), bf16),
            pltpu.VMEM((CZ, CZ), bf16),
            pltpu.VMEM((FF, CZ), bf16),
            pltpu.VMEM((CZ, FF), bf16),
            pltpu.VMEM((BINS, CZ), bf16),
            pltpu.VMEM((CZ, 2 * CZ), bf16),
            pltpu.VMEM((FF, 2 * CZ), bf16),
            pltpu.VMEM((CZ, 2 * BINS), bf16),
        ],
        (info, wide, down, small, gains, zt, zbt, o, r, tgt, nbr),
    )


def score(info, p, vn, do, nd):
    count, _, width = do.shape
    g = group_of(count, SCORE_ROWS)
    shape = (width // count // 2, HEADS * count * (width // CZ), CZ)
    return call(
        score_kernel,
        "score",
        17,
        count // g,
        [
            SMEM,
            rows_of(g, width, HEADS * width),
            rows_of(g, width, CZ),
            rows_of(g, CZ, width),
            rows_of(g, 2 * HEADS, width),
        ],
        [(whole(shape), shape, bf16)] * 2,
        [
            pltpu.VMEM((width, HEADS * width), f32),
            pltpu.VMEM((g, 2 * CZ, HEADS * width), bf16),
            pltpu.VMEM((g, width, 2 * CZ), bf16),
            pltpu.VMEM((HEADS, width, width), f32),
        ],
        (info, p, vn, do, nd),
    )


def late_sums(parcel, keep, got, zbt):
    count, _, width = zbt.shape
    shape = (keep.shape[0] + 8, CZ)
    g = group_of(count, LATE_ROWS)
    tall = HEADS * count * (width // CZ)
    return call(
        late_kernel,
        "late",
        3,
        count // g,
        [
            whole((parcel.shape[0], tall if tall % 16 == 0 else parcel.shape[1], CZ)),
            whole(keep.shape),
            whole(keep.shape),
            rows_of(g, CZ, width),
        ],
        [(whole(shape), shape, f32), (whole(shape), shape, bf16)],
        [pltpu.VMEM((tall, CZ), f32), pltpu.VMEM((CZ, 16), f32)],
        (parcel, keep, got, zbt),
    )


def back(info, p, qkv, vn, do, nd, zbt):
    count, _, width = zbt.shape
    half = 3 * CZ // 2
    g = group_of(count, BACK_ROWS)
    return call(
        back_kernel,
        "back",
        38,
        count // g,
        [
            SMEM,
            rows_of(g, width, HEADS * width),
            rows_of(g, CZ, width),
            rows_of(g, CZ, width, 1),
            rows_of(g, width, CZ),
            rows_of(g, CZ, width),
            rows_of(g, 2 * HEADS, width),
            rows_of(g, CZ, width),
        ],
        [(whole((half, CZ)), (half, CZ), f32)] * 2,
        [
            pltpu.VMEM((3 * CZ, CZ), f32),
            pltpu.VMEM((g, 2 * CZ, HEADS * width), bf16),
            pltpu.VMEM((g, width, HEADS * width), bf16),
            pltpu.VMEM((g, width, 2 * CZ), bf16),
            pltpu.VMEM((3 * CZ, g * width), bf16),
        ],
        (info, p, qkv, qkv, vn, do, nd, zbt),
    )


def finish(crops, rows, *args):
    wide, down, gains, small = args[8], args[9], args[10], args[12]
    shapes = []
    for weight in (wide, down):
        shapes += [weight.shape, weight.shape[:1], weight.shape[1:], weight.shape]
    shapes += [gains.shape] * 3 + [small.shape] * 3
    return call(
        partial(finish_kernel, crops, rows),
        "finish",
        4,
        1,
        [SMEM] + [whole(x.shape) for x in args[1:]],
        [(whole(shape), shape, f32) for shape in shapes],
        [
            pltpu.VMEM((BLOCKS * CZ, CZ), f32),
            pltpu.VMEM((3 * CZ, CZ), f32),
            pltpu.VMEM((CZ, WIDE), f32),
            pltpu.VMEM((FF, CZ), f32),
            pltpu.VMEM((CZ, 1), f32),
            pltpu.VMEM((FF, 1), f32),
            pltpu.VMEM((rows, CZ), f32),
            pltpu.VMEM((1, WIDE), f32),
            pltpu.VMEM((1, CZ), f32),
        ],
        args,
    )


def bits(n):
    return [1 << t for t in reversed(range(n.bit_length() - 1))]


def swap(x, axes, size, mask):
    return lax.ppermute(x, axes, [(i, i ^ mask) for i in range(size)])


def gathered(x, axes, size, masks):
    x = x[None]
    for mask in masks:
        x = jnp.concatenate([x, swap(x, axes, size, mask)], 0)
    return x


def places(me, size, masks):
    apart = jnp.arange(size, dtype=jnp.int32) ^ me
    place = jnp.zeros((size,), jnp.int32)
    for t, mask in enumerate(masks):
        place = place + jnp.where((apart & mask) != 0, 1 << t, 0)
    return place


def build(crops, rows):
    both = ("crop", "row")
    devices = crops * rows
    row_masks = bits(rows)
    all_masks = row_masks[:-1] + [m * rows for m in bits(crops)] + row_masks[-1:]

    sides = [[2 * chip + side for chip in range(devices // 2)] for side in range(2)]
    row_sides = [[2 * chip + side for chip in range(rows // 2)] for side in range(2)]

    def body(
        pair,
        crop_len,
        targets,
        neighbours,
        wide,
        wide_rows,
        wide_cols,
        down,
        down_rows,
        down_cols,
        gains,
        gain_second,
        small,
        small_second,
    ):
        row_index = lax.axis_index("row")
        crop_index = lax.axis_index("crop")
        count_rows, width = pair.shape[1], pair.shape[2]
        info = jnp.stack([row_index, crop_index, crop_len[0], jnp.int32(count_rows)])

        pack = pack_weights(
            devices // 2, wide, down, wide_rows, down_rows, wide_cols, down_cols
        )
        small_t = small.T
        packs = lax.all_to_all(pack, both, 0, 0, axis_index_groups=sides, tiled=True)
        zt, zbt, bias_part = front(pair[0], gains, small_t)
        bias = gathered(bias_part, "row", rows, row_masks[:-1])
        other_packs = swap(packs, both, devices, 1)
        qkv, vn, norms, wide_full, down_full, done = project(
            crops, rows, info, packs, other_packs, zbt
        )
        bias = bias + done.astype(bf16)[..., None, None]
        other_bias = swap(bias, "row", rows, row_masks[-1])
        if count_rows % 8:
            bias = jnp.concatenate([bias, other_bias], 0)
            bias = jnp.take(bias, places(row_index, rows, row_masks), axis=0)
            bias = bias.transpose(1, 0, 2, 3).reshape(1, HEADS, width, width)
            other_bias = bias
        bias_masks = [] if count_rows % 8 else row_masks
        p, o, r = attend(bias_masks, info, norms, bias, other_bias, qkv)
        do, nd, early, scalars = middle(
            info,
            wide_full,
            down_full,
            small_t,
            gains,
            zt,
            zbt,
            o,
            r,
            targets,
            neighbours,
        )

        early = lax.all_to_all(early.reshape(devices, -1, CZ), both, 0, 0, tiled=True)
        keep, give = score(info, p, vn, do, nd)
        early, keep, give = lax.optimization_barrier((early, keep, give))
        got = swap(give, both, devices, 1)
        early = jnp.concatenate([jnp.sum(early.astype(f32), 0).astype(bf16), scalars], 0)
        early_lines = early.shape[0]
        early = gathered(early, both, devices, [1])
        early = early.reshape(-1, CZ)
        early = jnp.broadcast_to(early[None], (rows // 2, *early.shape))
        parcel = jnp.concatenate([(keep.astype(f32) + got.astype(f32)).astype(bf16), early], 1)
        parcel, do = lax.optimization_barrier((parcel, do))
        parcel = lax.all_to_all(parcel, "row", 0, 0, axis_index_groups=row_sides, tiled=True)
        keep, give = back(info, p, qkv, vn, do, nd, zbt)
        got = swap(give, both, devices, 1)
        ours = parcel[:, -2 * early_lines :]
        across = swap(ours, both, devices, rows)
        keep, send = late_sums(parcel, keep, got, zbt)
        for n, mask in enumerate(all_masks[:-1]):
            if n == 0:
                keep = keep + swap(send, both, devices, mask).astype(f32)
            else:
                if n == len(all_masks) - 2:
                    keep = keep + across[0, -16:-15].astype(f32) * 0.0
                keep = keep + swap(keep, both, devices, mask)
        other = swap(keep, both, devices, 1)
        scalars = jnp.stack([ours, across])
        scalars = scalars.reshape(crops, rows, -1, CZ)[:, :, -16, :6]
        scalars = jnp.sum(scalars.astype(f32), (0, 1)).reshape(3, 2)
        loss_sum, pair_count = jnp.sum(scalars[:, 0]), jnp.sum(scalars[:, 1])
        (
            wide_g,
            wide_r_new,
            wide_c_new,
            wide_new,
            down_g,
            down_r_new,
            down_c_new,
            down_new,
            gain_grad,
            gain_s,
            gain_n,
            small_grad,
            small_s,
            small_n,
        ) = finish(
            crops,
            rows,
            info,
            keep,
            other,
            ours,
            across,
            packs,
            other_packs,
            wide_full,
            wide,
            down,
            gains,
            gain_second,
            small_t,
            small_second.T,
        )
        return (
            loss_sum,
            pair_count,
            wide_g,
            wide_r_new,
            wide_c_new,
            wide_new,
            down_g,
            down_r_new,
            down_c_new,
            down_new,
            gain_grad,
            gain_s,
            gain_n,
            small_grad.T,
            small_s.T,
            small_n.T,
        )

    return body


def solution(mesh):
    return jax.shard_map(
        build(mesh.shape["crop"], mesh.shape["row"]),
        mesh=mesh,
        in_specs=(
            P("crop", "row", None, None),
            P("crop"),
            P("crop", "row", None),
            P("crop", "row", None),
            P("row", "crop"),
            P("row"),
            P("crop"),
            P("row", "crop"),
            P("row"),
            P("crop"),
            P(),
            P(),
            P(),
            P(),
        ),
        out_specs=(
            P(),
            P(),
            P("row", "crop"),
            P("row"),
            P("crop"),
            P("row", "crop"),
            P("row", "crop"),
            P("row"),
            P("crop"),
            P("row", "crop"),
            P(),
            P(),
            P(),
            P(),
            P(),
            P(),
        ),
        check_vma=False,
    )
```

```python
import math
from functools import partial

import jax
import jax.numpy as jnp
from jax import lax
from jax.experimental import pallas as pl
from jax.experimental.pallas import tpu as pltpu
from jax.sharding import PartitionSpec as P

CZ = 128
HEADS = 4
HEAD_DIM = 32
FF = 512
BINS = 64
WIDE = 5 * CZ + FF

DECAY = 1.0 - 10.0 ** (-0.8)
TINY = 1e-30
LOG2E = math.log2(math.e)
ROOT = 1.0 / math.sqrt(HEAD_DIM)
BLK = 256
SAFE = 40.0
STATS = 256

GATE_BLOCK, OUT_BLOCK, IN_BLOCK, DOWN_BLOCK, HEAD_BLOCK, BLOCKS = 0, 1, 2, 6, 10, 12

f32 = jnp.float32
bf16 = jnp.bfloat16


def dot(a, b):
    return lax.dot_general(a, b, (((1,), (0,)), ((), ())), preferred_element_type=f32)


def dot_nt(a, b):
    return lax.dot_general(a, b, (((1,), (1,)), ((), ())), preferred_element_type=f32)


def rounded(v):
    return v.astype(bf16).astype(f32)


def halves(v):
    high = v.astype(bf16)
    return high, (v - high.astype(f32)).astype(bf16)


def normed(x):
    centre = x - jnp.sum(x, 0, keepdims=True) * (1.0 / CZ)
    var = jnp.sum(centre * centre, 0, keepdims=True) * (1.0 / CZ)
    inv = lax.rsqrt(var + 1e-05)
    return centre * inv, inv


def normed_back(d, xhat, inv):
    one = jnp.sum(d, 0, keepdims=True) * (1.0 / CZ)
    two = jnp.sum(d * xhat, 0, keepdims=True) * (1.0 / CZ)
    return inv * (d - one - xhat * two)


def sigmoid(x):
    return 0.5 * jnp.tanh(0.5 * x) + 0.5


def wider(column, x):
    return jnp.concatenate([column] * (x.shape[1] // 128), 1)


def lanes(ref):
    return jnp.concatenate([ref[g] for g in range(ref.shape[0])], 1)


def spread(ref, x):
    width = ref.shape[2]
    for g in range(ref.shape[0]):
        ref[g] = x[:, g * width : (g + 1) * width]


def columns_of(gains_ref, which, scratch):
    scratch[...] = jnp.broadcast_to(gains_ref[...].T[:, which : which + 1], (CZ, CZ))


def place(source, me, masks):
    apart = source ^ me
    where = 0
    for t, mask in enumerate(masks):
        where = where + ((apart >> (mask.bit_length() - 1)) & 1) * (1 << t)
    return where


def pack_kernel(
    wide_ref, down_ref, wide_rows_ref, down_rows_ref, wide_cols_ref, down_cols_ref, pack_ref, pack
):
    lines, cols = wide_ref.shape
    span = down_ref.shape[1]
    pack[...] = jnp.zeros_like(pack)
    for at, ref in ((0, wide_rows_ref), (lines, down_rows_ref)):
        some = ref[...].reshape(1, -1)
        upper = rounded(some)
        pack[0:1, at : at + some.shape[1]] = upper
        pack[1:2, at : at + some.shape[1]] = some - upper
    stats = jnp.concatenate(
        [wide_cols_ref[...].reshape(1, -1), down_cols_ref[...].reshape(1, -1)], 1
    )
    for part in range(-(-stats.shape[1] // STATS)):
        some = stats[:, part * STATS : (part + 1) * STATS]
        upper = rounded(some)
        pack[2 + part : 3 + part, : some.shape[1]] = upper
        pack[5 + part : 6 + part, : some.shape[1]] = some - upper
    pack[:lines, STATS : STATS + cols] = wide_ref[...]
    for part in range(FF // CZ):
        at = STATS + cols + part * span
        pack[:lines, at : at + span] = down_ref[part * lines : (part + 1) * lines, :]
    for peer in range(pack_ref.shape[0]):
        pack_ref[peer] = pack[...].astype(bf16)


def front_kernel(
    pair_ref, gains_ref, small_ref, zt_ref, zbt_ref, bias_ref, gain, wb, part
):
    rows, width, _ = pair_ref.shape
    step = pl.program_id(0)

    @pl.when(step == 0)
    def _():
        columns_of(gains_ref, 0, gain)
        wb[...] = small_ref[:16].astype(bf16)

    x = pair_ref[...].astype(f32).reshape(rows * width, CZ).T
    spread(zt_ref, x.astype(bf16))
    xhat, _ = normed(x)
    zb = (xhat * wider(gain[...], x)).astype(bf16)
    spread(zbt_ref, zb)
    bias = dot(wb[...], zb)
    for g in range(rows):
        for h in range(HEADS):
            part[h, pl.ds(step * rows + g, 1), :] = bias[h : h + 1, g * width : (g + 1) * width]

    @pl.when(step == pl.num_programs(0) - 1)
    def _():
        bias_ref[...] = part[...].astype(bf16)


def pick(info_ref, mine_ref, other_ref, crop, row, rows):
    chip = crop * (rows // 2) + row // 2
    side = info_ref[0] & 1
    return jnp.where(
        side == row % 2, mine_ref[chip].astype(f32), other_ref[chip].astype(f32)
    )


def project_kernel(
    crops,
    rows,
    info_ref,
    mine_ref,
    other_ref,
    zbt_ref,
    qkv_ref,
    vn_ref,
    norm_ref,
    wide_ref,
    down_ref,
    done_ref,
    wide_s,
    down_s,
    wqt,
):
    lines, cols, span = CZ // rows, WIDE // crops, CZ // crops

    @pl.when(pl.program_id(0) == 0)
    def _():
        for c in range(crops):
            for r in range(rows):
                block = pick(info_ref, mine_ref, other_ref, c, r, rows)[:lines]
                wide_s[r * lines : (r + 1) * lines, c * cols : (c + 1) * cols] = block[
                    :, STATS : STATS + cols
                ]
                for part in range(FF // CZ):
                    at = (r * (FF // CZ) + part) * lines
                    left = STATS + cols + part * span
                    down_s[at : at + lines, c * span : (c + 1) * span] = block[:, left : left + span]
        wide_ref[...] = wide_s[...].astype(bf16)
        down_ref[...] = down_s[...].astype(bf16)
        wqt[...] = wide_s[:, : 3 * CZ].T.astype(bf16)
        done_ref[...] = jnp.zeros_like(done_ref)

    qkv = dot(wqt[...], lanes(zbt_ref)).astype(bf16)
    spread(qkv_ref, qkv)
    q = qkv[:CZ].astype(f32)
    k = qkv[CZ : 2 * CZ].astype(f32)
    vn_ref[...] = qkv[2 * CZ :].T.reshape(vn_ref.shape)
    norm_ref[...] = jnp.concatenate(
        [
            jnp.sum((x * x)[h * HEAD_DIM : (h + 1) * HEAD_DIM], 0, keepdims=True)
            for x in (q, k)
            for h in range(HEADS)
        ],
        0,
    )


def attend_kernel(
    masks,
    info_ref,
    norm_ref,
    bias_ref,
    other_bias_ref,
    q_ref,
    k_ref,
    v_ref,
    p_ref,
    o_ref,
    r_ref,
    biast,
    nat,
    qbd,
    kk,
    bound,
):
    group, _, width = q_ref.shape
    rows = bias_ref.shape[2]
    shards = width // rows
    step = pl.program_id(0)

    @pl.when(step == 0)
    def _():
        top = 0.0
        key = lax.broadcasted_iota(jnp.int32, (1, width), 1)
        kb = jnp.where(key < info_ref[2], 0.0, -1000000000.0 * LOG2E)
        for h in range(HEADS):
            for s in range(shards):
                at = place(s, info_ref[0], masks[:-1])
                block = bias_ref[at, h].astype(f32)
                if shards > 1:
                    here = (info_ref[0] & 1) == s % 2
                    block = jnp.where(here, block, other_bias_ref[at, h].astype(f32))
                nat[s * rows : (s + 1) * rows, :] = block
            top = jnp.maximum(top, jnp.max(jnp.abs(nat[...])))
            biast[:, h * width : (h + 1) * width] = (nat[...] * LOG2E + kb).T
        bound[0] = top * LOG2E
        qbd[...] = jnp.zeros_like(qbd)
        r_ref[...] = jnp.zeros_like(r_ref)

    def attend(shift):
        for g in range(group):
            high, low = halves(q_ref[g].astype(f32) * (LOG2E * ROOT))
            for h in range(HEADS):
                a, b = h * HEAD_DIM, (h + 1) * HEAD_DIM
                qbd[g, a:b, h * width : (h + 1) * width] = high[a:b]
                qbd[g, CZ + a : CZ + b, h * width : (h + 1) * width] = low[a:b]
            kn = k_ref[g].T
            kk[g, :, :CZ] = kn
            kk[g, :, CZ:] = kn
            sums = []
            for c in range(0, HEADS * width, BLK):
                s = dot(kk[g], qbd[g, :, c : c + BLK]) + biast[:, c : c + BLK]
                if shift:
                    s = s - jnp.max(s, 0, keepdims=True)
                e = jnp.exp2(s)
                sums.append(jnp.sum(e, 0, keepdims=True))
                p_ref[g, :, c : c + BLK] = e.astype(bf16)
            r = 1.0 / jnp.concatenate(sums, 1)
            for h in range(HEADS):
                a, b = h * HEAD_DIM, (h + 1) * HEAD_DIM
                mine = r[:, h * width : (h + 1) * width]
                r_ref[g, h : h + 1] = mine
                out = dot(v_ref[g, a:b], p_ref[g, :, h * width : (h + 1) * width]) * mine
                o_ref[g, a:b] = out.astype(bf16)

    norms = jnp.max(norm_ref[...], 1, keepdims=True)
    reach = jnp.max(jnp.sqrt(norms[:HEADS] * norms[HEADS:])) * (1.01 * LOG2E * ROOT)
    safe = reach + bound[0] < SAFE

    @pl.when(safe)
    def _():
        attend(False)

    @pl.when(jnp.logical_not(safe))
    def _():
        attend(True)


def middle_kernel(
    info_ref,
    wide_ref,
    down_ref,
    head_ref,
    gains_ref,
    zt_ref,
    zbt_ref,
    o_ref,
    r_ref,
    tgt_ref,
    nbr_ref,
    do_ref,
    nd_ref,
    grads_ref,
    scalars_ref,
    acc,
    sums,
    g1,
    g2,
    wgt,
    wot,
    wint,
    wdownt,
    wht,
    wo2,
    wdown2,
    wh2,
):
    step = pl.program_id(0)

    @pl.when(step == 0)
    def _():
        wo = wide_ref[:, 4 * CZ : 5 * CZ]
        wot[...] = wo.T
        wgt[...] = wide_ref[:, 3 * CZ : 4 * CZ].T
        wint[...] = wide_ref[:, 5 * CZ :].T * 0.5
        wdownt[...] = down_ref[...].T
        head = head_ref[...][HEADS:]
        wht[...] = head.astype(bf16)
        head = head.T.astype(bf16)
        wo2[...] = jnp.concatenate([wo, wo], 1)
        wdown2[...] = jnp.concatenate([down_ref[...], down_ref[...]], 1) * 0.5
        wh2[...] = jnp.concatenate([head, head], 1)
        acc[...] = jnp.zeros_like(acc)
        columns_of(gains_ref, 1, g1)
        columns_of(gains_ref, 2, g2)
        sums[...] = jnp.zeros_like(sums)

    group, _, width = o_ref.shape
    first = step * group

    def add(block, grad):
        for c in range(0, grad.shape[1], CZ):
            acc[block + c // CZ] += grad[:, c : c + CZ]

    def stages(low, high):
        spots = [divmod(block * 128, width) for block in range(low, high)]

        def mine(ref):
            return jnp.concatenate([ref[g, :, at : at + 128] for g, at in spots], 1)

        def line(ref):
            return jnp.concatenate(
                [ref[0, pl.ds(first + g, 1), :][:, at : at + 128] for g, at in spots], 1
            )

        def out(ref, x):
            for n, (g, at) in enumerate(spots):
                ref[g, :, at : at + 128] = x[:, n * 128 : (n + 1) * 128]

        o = mine(o_ref).astype(f32)
        zb = mine(zbt_ref)
        gate = sigmoid(dot(wgt[...], zb))
        gain1 = wider(g1[...], o)
        gain2 = wider(g2[...], o)
        og = (o * gate).astype(bf16)
        z1 = mine(zt_ref).astype(f32) + dot(wot[...], og)
        yield
        xhat1, inv1 = normed(z1)
        zb2 = (xhat1 * gain1).astype(bf16)
        yield
        hidden, slopes = [], []
        for f in range(0, FF, CZ):
            hid = dot(wint[f : f + CZ], zb2)
            t = jnp.tanh(hid)
            sg = 1.0 + t
            act = hid * sg
            hidden.append(act.astype(bf16))
            slopes.append(sg + act * (1.0 - t))
            yield
        a = jnp.concatenate(hidden, 0)
        z2 = z1 + dot(wdownt[...], a)
        yield
        xhat2, inv2 = normed(z2)
        zb3 = (xhat2 * gain2).astype(bf16)
        logits = dot(wht[...], zb3)
        yield
        top = jnp.max(logits, 0, keepdims=True)
        ex = jnp.exp(logits - top)
        total = jnp.sum(ex, 0, keepdims=True)
        hot = lax.broadcasted_iota(jnp.int32, logits.shape, 0) == line(tgt_ref)
        picked = jnp.sum(jnp.where(hot, logits, 0.0), 0, keepdims=True)
        column = lax.broadcasted_iota(jnp.int32, (1, 128), 1)
        length = info_ref[2]
        valid = jnp.concatenate(
            [
                column + at < jnp.where(info_ref[0] * info_ref[3] + first + g < length, length, 0)
                for g, at in spots
            ],
            1,
        )
        mask = jnp.where((line(nbr_ref) > 0) & valid, 1.0, 0.0)
        at = slice(0, mask.shape[1])
        sums[0:1, at] += (jnp.log(total) + top - picked) * mask
        sums[1:2, at] += mask
        dl = ex * (mask / total) - jnp.where(hot, mask, 0.0)
        dl2 = jnp.concatenate(halves(dl), 0)
        yield
        add(HEAD_BLOCK, dot_nt(dl2, zb3))
        dzb3 = rounded(dot(wh2[...], dl2))
        yield
        dz2 = normed_back(dzb3 * gain2, xhat2, inv2)
        high2, low2 = halves(dz2)
        both2 = jnp.concatenate([high2, low2], 0)
        yield
        dh = []
        for f in range(0, FF, CZ):
            dh.append((dot(wdown2[f : f + CZ], both2) * slopes[f // CZ]).astype(bf16))
            yield
        dh = jnp.concatenate(dh, 0)
        add(DOWN_BLOCK, dot_nt(high2, a))
        yield
        dzb2 = rounded(dot(wide_ref[:, 5 * CZ :], dh))
        yield
        add(IN_BLOCK, dot_nt(zb2, dh))
        dz1 = dz2 + normed_back(dzb2 * gain1, xhat1, inv1)
        high1, low1 = halves(dz1)
        yield
        add(OUT_BLOCK, dot_nt(og, high1))
        dog = rounded(dot(wo2[...], jnp.concatenate([high1, low1], 0)))
        yield
        do = dog * gate
        doo = do * o
        add(GATE_BLOCK, dot_nt(zb, (doo * (1.0 - gate)).astype(bf16)))
        yield
        r = mine(r_ref)
        parts, minus = [], []
        for h in range(HEADS):
            x, y = h * HEAD_DIM, (h + 1) * HEAD_DIM
            share = r[h : h + 1]
            parts.append((do[x:y] * share).astype(bf16))
            minus.append(-jnp.sum(doo[x:y], 0, keepdims=True) * share)
        out(do_ref, jnp.concatenate(parts, 0))
        out(nd_ref, jnp.concatenate(minus + minus, 0))

    blocks = group * width // 128
    running = [
        stages(low, min(low + MIDDLE_PART, blocks)) for low in range(0, blocks, MIDDLE_PART)
    ]
    turn = 0
    waiting = list(enumerate(running))
    while waiting:
        for item in list(waiting):
            if turn >= item[0] * MIDDLE_LAG and next(item[1], item) is item:
                waiting.remove(item)
        turn += 1

    @pl.when(step == pl.num_programs(0) - 1)
    def _():
        for block in range(BLOCKS):
            grads_ref[block] = acc[block].astype(bf16)
        both = jnp.sum(sums[...], 1, keepdims=True)
        lane = lax.broadcasted_iota(jnp.int32, scalars_ref.shape, 1)
        out = jnp.zeros(scalars_ref.shape, f32)
        for part in range(3):
            upper = rounded(both)
            for which in range(2):
                out = jnp.where(lane == 2 * part + which, upper[which : which + 1], out)
            both = both - upper
        scalars_ref[...] = out.astype(bf16)


def score_kernel(info_ref, p_ref, vn_ref, do_ref, nd_ref, keep_ref, give_ref, acc, dobd, vv, nat):
    group, _, width = do_ref.shape
    step = pl.program_id(0)

    @pl.when(step == 0)
    def _():
        acc[...] = jnp.zeros_like(acc)
        prepare(dobd, vv)

    for g in range(group):
        score_operands(g, vn_ref, do_ref, nd_ref, dobd, vv)
        for c in range(0, HEADS * width, BLK):
            acc[:, c : c + BLK] += dot(vv[g], dobd[g, :, c : c + BLK]) * p_ref[
                g, :, c : c + BLK
            ].astype(f32)

    @pl.when(step == pl.num_programs(0) - 1)
    def _():
        chips, tall, _ = keep_ref.shape
        lines = width // (2 * chips)
        first = (info_ref[0] & 1) == 0
        for h in range(HEADS):
            nat[h] = acc[:, h * width : (h + 1) * width].T
        for chip in range(chips):
            sides = [
                jnp.concatenate(
                    [
                        nat[h, (2 * chip + side) * lines : (2 * chip + side + 1) * lines, c : c + CZ]
                        for c in range(0, width, CZ)
                        for h in range(HEADS)
                    ],
                    0,
                )
                for side in range(2)
            ]
            keep_ref[chip] = jnp.where(first, sides[0], sides[1]).astype(bf16)
            give_ref[chip] = jnp.where(first, sides[1], sides[0]).astype(bf16)


def prepare(dobd, vv):
    dobd[...] = jnp.zeros_like(dobd)
    vv[...] = jnp.ones_like(vv)


def score_operands(g, vn_ref, do_ref, nd_ref, dobd, vv):
    width = do_ref.shape[2]
    vv[g, :, :CZ] = vn_ref[g]
    for h in range(HEADS):
        a, b = h * HEAD_DIM, (h + 1) * HEAD_DIM
        at = slice(h * width, (h + 1) * width)
        dobd[g, a:b, at] = do_ref[g, a:b]
        minus = nd_ref[g, h : h + 1]
        upper = rounded(minus)
        dobd[g, CZ : CZ + 16, at] = jnp.concatenate(
            [upper, minus - upper, jnp.zeros((14, width), f32)], 0
        ).astype(bf16)


def back_kernel(
    info_ref,
    p_ref,
    q_ref,
    k_ref,
    vn_ref,
    do_ref,
    nd_ref,
    zbt_ref,
    keep_ref,
    give_ref,
    dwq,
    dobd,
    dst,
    vv,
    dproj,
):
    group, _, width = do_ref.shape
    step = pl.program_id(0)

    @pl.when(step == 0)
    def _():
        dwq[...] = jnp.zeros_like(dwq)
        prepare(dobd, vv)

    for g in range(group):
        score_operands(g, vn_ref, do_ref, nd_ref, dobd, vv)
        for c in range(0, HEADS * width, BLK):
            ds = dot(vv[g], dobd[g, :, c : c + BLK]) * p_ref[g, :, c : c + BLK].astype(f32)
            dst[g, :, c : c + BLK] = ds.astype(bf16)
        at = slice(g * width, (g + 1) * width)
        for h in range(HEADS):
            a, b = h * HEAD_DIM, (h + 1) * HEAD_DIM
            mine = dst[g, :, h * width : (h + 1) * width]
            dproj[a:b, at] = (dot(k_ref[g, a:b], mine) * ROOT).astype(bf16)
            dproj[CZ + a : CZ + b, at] = (dot_nt(q_ref[g, a:b], mine) * ROOT).astype(bf16)
            dproj[2 * CZ + a : 2 * CZ + b, at] = dot_nt(
                do_ref[g, a:b], p_ref[g, :, h * width : (h + 1) * width]
            ).astype(bf16)
    grad = dot_nt(lanes(zbt_ref), dproj[...])
    for block in range(3):
        dwq[block * CZ : (block + 1) * CZ, :] += grad[:, block * CZ : (block + 1) * CZ]

    @pl.when(step == pl.num_programs(0) - 1)
    def _():
        half = keep_ref.shape[0]
        first = (info_ref[0] & 1) == 0
        one, two = dwq[:half, :], dwq[half:, :]
        keep_ref[...] = jnp.where(first, one, two)
        give_ref[...] = jnp.where(first, two, one)


def factored(grad_ref, rows, cols, weight_ref, crop, row_start, scratch, outs):
    grad_out, rows_out, cols_out, new_out = outs
    lines, span = weight_ref.shape
    grad = grad_ref[...]
    count, columns = grad.shape
    sq = grad * grad
    rows_new = DECAY * rows + (1.0 - DECAY) * (jnp.sum(sq, 1, keepdims=True) / columns + TINY)
    cols_new = DECAY * cols + (1.0 - DECAY) * (jnp.sum(sq, 0, keepdims=True) / count + TINY)
    mean = jnp.sum(rows_new, 0, keepdims=True) / count
    rows_factor = mean / rows_new
    cols_factor = 1.0 / cols_new
    size = jnp.sum(jnp.sum(sq * rows_factor * cols_factor, 1, keepdims=True), 0, keepdims=True)
    clip = jnp.maximum(0.1, jnp.sqrt(size / (count * columns)))
    scratch[...] = rows_factor
    mine = grad_ref[pl.ds(row_start, lines), :]
    update = mine * lax.rsqrt((1.0 / scratch[pl.ds(row_start, lines), :]) * (1.0 / cols_factor))
    update = weight_step(update, clip)
    scratch[...] = rows_new
    own_rows = jnp.broadcast_to(scratch[pl.ds(row_start, lines), :], (lines, CZ))
    rows_out[...] = own_rows.T[0]

    def own(x):
        part = x[:, :span]
        for c in range(1, columns // span):
            part = jnp.where(crop == c, x[:, c * span : (c + 1) * span], part)
        return part

    grad_out[...] = own(mine)
    cols_out[...] = own(cols_new)[0]
    new_out[...] = weight_ref[...] - own(update)


def weight_step(update, clip):
    return update * (0.03 / clip)


def plain(weight, grad, second, rate, outs):
    second_new = DECAY * second + (1.0 - DECAY) * (grad * grad + TINY)
    update = grad * lax.rsqrt(second_new)
    square = jnp.sum(jnp.sum(update * update, 1, keepdims=True), 0, keepdims=True)
    clip = jnp.maximum(1.0, jnp.sqrt(square / (grad.shape[0] * grad.shape[1])))
    outs[0][...] = grad
    outs[1][...] = second_new
    outs[2][...] = weight - rate * update / clip


def finish_kernel(
    crops,
    rows,
    info_ref,
    keep_ref,
    other_ref,
    spread_ref,
    across_ref,
    packs_ref,
    other_packs_ref,
    full_ref,
    wide_ref,
    down_ref,
    gains_ref,
    gain_second_ref,
    small_ref,
    small_second_ref,
    *refs,
):
    outs, (flat, late_ref, wide_s, down_s, wide_c, down_c, table, wide_cols, down_cols) = (
        refs[:14],
        refs[14:],
    )
    row, crop = info_ref[0], info_ref[1]
    side = row & 1
    half = 3 * CZ // 2
    mine, other = keep_ref[...], other_ref[...]
    late_ref[:half, :] = jnp.where(side == 0, mine[:half], other[:half])
    late_ref[half:, :] = jnp.where(side == 0, other[:half], mine[:half])
    pbias = mine[half:] + other[half:]

    lines = BLOCKS * CZ // (crops * rows)
    height = lines + 16
    tail = jnp.zeros((1, CZ), f32)
    for c in range(crops):
        for r in range(rows):
            at = (c * rows + r) * lines
            which = (r % 2) ^ side
            block = jnp.zeros((height, CZ), f32)
            for p in range(2):
                part = slice(p * height, (p + 1) * height)
                here = spread_ref[r // 2, part].astype(f32)
                there = across_ref[r // 2, part].astype(f32)
                block = jnp.where(which == p, jnp.where(c == crop, here, there), block)
            flat[at : at + lines, :] = block[:lines]
            tail += block[lines : lines + 1]
    scale = 1.0 / (tail[:, 1:2] + tail[:, 3:4] + tail[:, 5:6])

    def early(block):
        return flat[block * CZ : (block + 1) * CZ, :] * scale

    for block in range(3):
        wide_s[:, block * CZ : (block + 1) * CZ] = (
            late_ref[block * CZ : (block + 1) * CZ, :] * scale
        )
    for block in range(GATE_BLOCK, DOWN_BLOCK):
        wide_s[:, (3 + block) * CZ : (4 + block) * CZ] = early(block)
    for block in range(DOWN_BLOCK, HEAD_BLOCK):
        down_s[(block - DOWN_BLOCK) * CZ : (block - DOWN_BLOCK + 1) * CZ, :] = early(block).T
    head = early(HEAD_BLOCK)
    pbias = pbias[:HEADS] * scale
    small_grad = jnp.concatenate([pbias, head[:BINS] + head[BINS:]], 0)
    small = small_ref[...]
    plain(small, small_grad, small_second_ref[...], 0.03, outs[11:])

    through = wide_s[...] * full_ref[...].astype(f32)
    behind = small_grad * rounded(small)
    lane = lax.broadcasted_iota(jnp.int32, (CZ, CZ), 1)
    gain_grad = jnp.where(
        lane == 0,
        jnp.sum(through[:, : 4 * CZ], 1, keepdims=True),
        jnp.sum(through[:, 5 * CZ :], 1, keepdims=True),
    ).T
    gain_grad = jnp.concatenate(
        [
            gain_grad[:1] + jnp.sum(behind[:HEADS], 0, keepdims=True),
            gain_grad[1:2],
            jnp.sum(behind[HEADS:], 0, keepdims=True),
        ],
        0,
    )
    gains = gains_ref[...]
    plain(gains, gain_grad / gains, gain_second_ref[...], 0.3, outs[8:11])

    per, down_per = CZ // rows, FF // rows
    for r in range(rows):
        block = pick(info_ref, packs_ref, other_packs_ref, 0, r, rows)
        table[r : r + 1, :] = block[0:1, :CZ] + block[1:2, :CZ]

    def column(size, start):
        tall = jnp.broadcast_to(table[...][:, None, :], (rows, size, CZ)).reshape(rows * size, CZ)
        lane = lax.broadcasted_iota(jnp.int32, tall.shape, 1)
        line = lax.broadcasted_iota(jnp.int32, tall.shape, 0)
        return jnp.sum(jnp.where(lane == start + line % size, tall, 0.0), 1, keepdims=True)

    cols, span = WIDE // crops, CZ // crops
    for c in range(crops):
        block = pick(info_ref, packs_ref, other_packs_ref, c, 0, rows)[:, :STATS]
        block = block[2:5] + block[5:8]
        stats = jnp.concatenate([block[part : part + 1] for part in range(3)], 1)
        wide_cols[:, c * cols : (c + 1) * cols] = stats[:, :cols]
        down_cols[:, c * span : (c + 1) * span] = stats[:, cols : cols + span]
    factored(
        wide_s,
        column(per, 0),
        wide_cols[...],
        wide_ref,
        crop,
        row * wide_ref.shape[0],
        wide_c,
        outs[:4],
    )
    factored(
        down_s,
        column(down_per, per),
        down_cols[...],
        down_ref,
        crop,
        row * down_ref.shape[0],
        down_c,
        outs[4:8],
    )


def late_kernel(spread_ref, keep_ref, got_ref, zbt_ref, out_ref, send_ref, dbias, acc):
    group, _, width = zbt_ref.shape
    tall = dbias.shape[0]
    lines = tall // (HEADS * (width // CZ))
    step = pl.program_id(0)

    @pl.when(step == 0)
    def _():
        total = spread_ref[0, :tall].astype(f32)
        for chip in range(1, spread_ref.shape[0]):
            total += spread_ref[chip, :tall].astype(f32)
        dbias[...] = rounded(total)
        acc[...] = jnp.zeros_like(acc)

    some = jnp.concatenate(
        [
            dbias[pl.ds(c * HEADS * lines + step * group + g, HEADS, stride=lines), :]
            for g in range(group)
            for c in range(width // CZ)
        ],
        1,
    )
    some = jnp.concatenate([some, jnp.zeros((16 - HEADS, some.shape[1]), f32)], 0)
    acc[...] += dot_nt(lanes(zbt_ref), some.astype(bf16))

    @pl.when(step == pl.num_programs(0) - 1)
    def _():
        half = keep_ref.shape[0]
        for at, x in ((0, keep_ref[...] + got_ref[...]), (half, acc[...].T[:8])):
            out_ref[at : at + x.shape[0], :] = rounded(x)
        send_ref[...] = out_ref[...].astype(bf16)


def whole(shape):
    return pl.BlockSpec(shape, lambda i: (0,) * len(shape))


def rows_of(group, lines, columns, line=0, column=0):
    return pl.BlockSpec((group, lines, columns), lambda i: (i, line, column))


def of(shape, dtype):
    return jax.ShapeDtypeStruct(shape, dtype)


SMEM = pl.BlockSpec(memory_space=pltpu.SMEM)


def call(kernel, name, micros, grid, in_specs, outs, scratch, args, mebibytes=52):
    return pl.pallas_call(
        kernel,
        grid=(grid,),
        in_specs=in_specs,
        out_specs=[o[0] for o in outs],
        out_shape=[of(o[1], o[2]) for o in outs],
        scratch_shapes=scratch,
        compiler_params=pltpu.CompilerParams(vmem_limit_bytes=mebibytes << 20),
        cost_estimate=pl.CostEstimate(
            flops=int(micros * 8e8), bytes_accessed=1 << 20, transcendentals=0
        ),
        name=name,
    )(*args)


def group_of(count, most):
    return next(g for g in range(most, 0, -1) if count % g == 0)


def pack_weights(peers, wide, down, *stats):
    args = (wide, down, *stats)
    shape = (peers, 8, STATS + wide.shape[1] + (FF // CZ) * down.shape[1])
    return call(
        pack_kernel,
        "pack",
        1,
        1,
        [whole(x.shape) for x in args],
        [(whole(shape), shape, bf16)],
        [pltpu.VMEM(shape[1:], f32)],
        args,
        60,
    )[0]


def front(pair, gains, small):
    count, width = pair.shape[0], pair.shape[1]
    g = group_of(count, FRONT_ROWS)
    return call(
        front_kernel,
        "front",
        6,
        count // g,
        [rows_of(g, width, CZ), whole(gains.shape), whole(small.shape)],
        [
            (rows_of(g, CZ, width), (count, CZ, width), bf16),
            (rows_of(g, CZ, width), (count, CZ, width), bf16),
            (whole((HEADS, count, width)), (HEADS, count, width), bf16),
        ],
        [
            pltpu.VMEM((CZ, CZ), f32),
            pltpu.VMEM((16, CZ), bf16),
            pltpu.VMEM((HEADS, count, width), f32),
        ],
        (pair, gains, small),
    )


def project(crops, rows, info, mine, other, zbt):
    count, _, width = zbt.shape
    g = group_of(count, 8)
    return call(
        partial(project_kernel, crops, rows),
        "project",
        40,
        count // g,
        [SMEM, whole(mine.shape), whole(other.shape), rows_of(g, CZ, width)],
        [
            (rows_of(g, 3 * CZ, width), (count, 3 * CZ, width), bf16),
            (rows_of(g, width, CZ), (count, width, CZ), bf16),
            (pl.BlockSpec((8, g * width), lambda i: (0, i)), (8, count * width), f32),
            (whole((CZ, WIDE)), (CZ, WIDE), bf16),
            (whole((FF, CZ)), (FF, CZ), bf16),
            (whole((1, 1)), (1, 1), f32),
        ],
        [pltpu.VMEM((CZ, WIDE), f32), pltpu.VMEM((FF, CZ), f32), pltpu.VMEM((3 * CZ, CZ), bf16)],
        (info, mine, other, zbt),
    )


FRONT_ROWS = 12
ATTEND_ROWS = 3
MIDDLE_ROWS = 8
MIDDLE_PART = 2
MIDDLE_LAG = 1
SCORE_ROWS = 6
BACK_ROWS = 4
LATE_ROWS = 12


def attend(masks, info, norms, bias, other_bias, qkv):
    count, _, width = qkv.shape
    g = group_of(count, ATTEND_ROWS)
    return call(
        partial(attend_kernel, masks),
        "attend",
        25,
        count // g,
        [
            SMEM,
            pl.BlockSpec((8, g * width), lambda i: (0, i)),
            whole(bias.shape),
            whole(bias.shape),
            rows_of(g, CZ, width),
            rows_of(g, CZ, width, 1),
            rows_of(g, CZ, width, 2),
        ],
        [
            (rows_of(g, width, HEADS * width), (count, width, HEADS * width), bf16),
            (rows_of(g, CZ, width), (count, CZ, width), bf16),
            (rows_of(g, 8, width), (count, 8, width), f32),
        ],
        [
            pltpu.VMEM((width, HEADS * width), f32),
            pltpu.VMEM((width, width), f32),
            pltpu.VMEM((g, 2 * CZ, HEADS * width), bf16),
            pltpu.VMEM((g, width, 2 * CZ), bf16),
            pltpu.SMEM((1,), f32),
        ],
        (info, norms, bias, other_bias, qkv, qkv, qkv),
    )


def middle(info, wide, down, small, gains, zt, zbt, o, r, tgt, nbr):
    count, _, width = zt.shape
    g = group_of(count, MIDDLE_ROWS)
    return call(
        middle_kernel,
        "middle",
        30,
        count // g,
        [
            SMEM,
            whole((CZ, WIDE)),
            whole((FF, CZ)),
            whole(small.shape),
            whole(gains.shape),
            rows_of(g, CZ, width),
            rows_of(g, CZ, width),
            rows_of(g, CZ, width),
            rows_of(g, 8, width),
            whole(tgt.shape),
            whole(nbr.shape),
        ],
        [
            (rows_of(g, CZ, width), (count, CZ, width), bf16),
            (rows_of(g, 2 * HEADS, width), (count, 2 * HEADS, width), f32),
            (whole((BLOCKS, CZ, CZ)), (BLOCKS, CZ, CZ), bf16),
            (whole((16, CZ)), (16, CZ), bf16),
        ],
        [
            pltpu.VMEM((BLOCKS, CZ, CZ), f32),
            pltpu.VMEM((2, 128 * MIDDLE_PART), f32),
            pltpu.VMEM((CZ, CZ), f32),
            pltpu.VMEM((CZ, CZ), f32),
            pltpu.VMEM((CZ, CZ), bf16),
            pltpu.VMEM((CZ, CZ), bf16),
            pltpu.VMEM((FF, CZ), bf16),
            pltpu.VMEM((CZ, FF), bf16),
            pltpu.VMEM((BINS, CZ), bf16),
            pltpu.VMEM((CZ, 2 * CZ), bf16),
            pltpu.VMEM((FF, 2 * CZ), bf16),
            pltpu.VMEM((CZ, 2 * BINS), bf16),
        ],
        (info, wide, down, small, gains, zt, zbt, o, r, tgt, nbr),
    )


def score(info, p, vn, do, nd):
    count, _, width = do.shape
    g = group_of(count, SCORE_ROWS)
    shape = (width // count // 2, HEADS * count * (width // CZ), CZ)
    return call(
        score_kernel,
        "score",
        17,
        count // g,
        [
            SMEM,
            rows_of(g, width, HEADS * width),
            rows_of(g, width, CZ),
            rows_of(g, CZ, width),
            rows_of(g, 2 * HEADS, width),
        ],
        [(whole(shape), shape, bf16)] * 2,
        [
            pltpu.VMEM((width, HEADS * width), f32),
            pltpu.VMEM((g, 2 * CZ, HEADS * width), bf16),
            pltpu.VMEM((g, width, 2 * CZ), bf16),
            pltpu.VMEM((HEADS, width, width), f32),
        ],
        (info, p, vn, do, nd),
    )


def late_sums(parcel, keep, got, zbt):
    count, _, width = zbt.shape
    shape = (keep.shape[0] + 8, CZ)
    g = group_of(count, LATE_ROWS)
    tall = HEADS * count * (width // CZ)
    return call(
        late_kernel,
        "late",
        3,
        count // g,
        [
            whole((parcel.shape[0], tall if tall % 16 == 0 else parcel.shape[1], CZ)),
            whole(keep.shape),
            whole(keep.shape),
            rows_of(g, CZ, width),
        ],
        [(whole(shape), shape, f32), (whole(shape), shape, bf16)],
        [pltpu.VMEM((tall, CZ), f32), pltpu.VMEM((CZ, 16), f32)],
        (parcel, keep, got, zbt),
    )


def back(info, p, qkv, vn, do, nd, zbt):
    count, _, width = zbt.shape
    half = 3 * CZ // 2
    g = group_of(count, BACK_ROWS)
    return call(
        back_kernel,
        "back",
        38,
        count // g,
        [
            SMEM,
            rows_of(g, width, HEADS * width),
            rows_of(g, CZ, width),
            rows_of(g, CZ, width, 1),
            rows_of(g, width, CZ),
            rows_of(g, CZ, width),
            rows_of(g, 2 * HEADS, width),
            rows_of(g, CZ, width),
        ],
        [(whole((half, CZ)), (half, CZ), f32)] * 2,
        [
            pltpu.VMEM((3 * CZ, CZ), f32),
            pltpu.VMEM((g, 2 * CZ, HEADS * width), bf16),
            pltpu.VMEM((g, width, HEADS * width), bf16),
            pltpu.VMEM((g, width, 2 * CZ), bf16),
            pltpu.VMEM((3 * CZ, g * width), bf16),
        ],
        (info, p, qkv, qkv, vn, do, nd, zbt),
    )


def finish(crops, rows, *args):
    wide, down, gains, small = args[8], args[9], args[10], args[12]
    shapes = []
    for weight in (wide, down):
        shapes += [weight.shape, weight.shape[:1], weight.shape[1:], weight.shape]
    shapes += [gains.shape] * 3 + [small.shape] * 3
    return call(
        partial(finish_kernel, crops, rows),
        "finish",
        4,
        1,
        [SMEM] + [whole(x.shape) for x in args[1:]],
        [(whole(shape), shape, f32) for shape in shapes],
        [
            pltpu.VMEM((BLOCKS * CZ, CZ), f32),
            pltpu.VMEM((3 * CZ, CZ), f32),
            pltpu.VMEM((CZ, WIDE), f32),
            pltpu.VMEM((FF, CZ), f32),
            pltpu.VMEM((CZ, 1), f32),
            pltpu.VMEM((FF, 1), f32),
            pltpu.VMEM((rows, CZ), f32),
            pltpu.VMEM((1, WIDE), f32),
            pltpu.VMEM((1, CZ), f32),
        ],
        args,
    )


def bits(n):
    return [1 << t for t in reversed(range(n.bit_length() - 1))]


def swap(x, axes, size, mask):
    return lax.ppermute(x, axes, [(i, i ^ mask) for i in range(size)])


def gathered(x, axes, size, masks):
    x = x[None]
    for mask in masks:
        x = jnp.concatenate([x, swap(x, axes, size, mask)], 0)
    return x


def places(me, size, masks):
    apart = jnp.arange(size, dtype=jnp.int32) ^ me
    place = jnp.zeros((size,), jnp.int32)
    for t, mask in enumerate(masks):
        place = place + jnp.where((apart & mask) != 0, 1 << t, 0)
    return place


def build(crops, rows):
    both = ("crop", "row")
    devices = crops * rows
    row_masks = bits(rows)
    all_masks = row_masks[:-1] + [m * rows for m in bits(crops)] + row_masks[-1:]

    sides = [[2 * chip + side for chip in range(devices // 2)] for side in range(2)]
    row_sides = [[2 * chip + side for chip in range(rows // 2)] for side in range(2)]

    def body(
        pair,
        crop_len,
        targets,
        neighbours,
        wide,
        wide_rows,
        wide_cols,
        down,
        down_rows,
        down_cols,
        gains,
        gain_second,
        small,
        small_second,
    ):
        row_index = lax.axis_index("row")
        crop_index = lax.axis_index("crop")
        count_rows, width = pair.shape[1], pair.shape[2]
        info = jnp.stack([row_index, crop_index, crop_len[0], jnp.int32(count_rows)])

        pack = pack_weights(
            devices // 2, wide, down, wide_rows, down_rows, wide_cols, down_cols
        )
        small_t = small.T
        packs = lax.all_to_all(pack, both, 0, 0, axis_index_groups=sides, tiled=True)
        zt, zbt, bias_part = front(pair[0], gains, small_t)
        bias = gathered(bias_part, "row", rows, row_masks[:-1])
        other_packs = swap(packs, both, devices, 1)
        qkv, vn, norms, wide_full, down_full, done = project(
            crops, rows, info, packs, other_packs, zbt
        )
        bias = bias + done.astype(bf16)[..., None, None]
        other_bias = swap(bias, "row", rows, row_masks[-1])
        if count_rows % 8:
            bias = jnp.concatenate([bias, other_bias], 0)
            bias = jnp.take(bias, places(row_index, rows, row_masks), axis=0)
            bias = bias.transpose(1, 0, 2, 3).reshape(1, HEADS, width, width)
            other_bias = bias
        bias_masks = [] if count_rows % 8 else row_masks
        p, o, r = attend(bias_masks, info, norms, bias, other_bias, qkv)
        do, nd, early, scalars = middle(
            info,
            wide_full,
            down_full,
            small_t,
            gains,
            zt,
            zbt,
            o,
            r,
            targets,
            neighbours,
        )

        early = lax.all_to_all(early.reshape(devices, -1, CZ), both, 0, 0, tiled=True)
        keep, give = score(info, p, vn, do, nd)
        early, keep, give = lax.optimization_barrier((early, keep, give))
        got = swap(give, both, devices, 1)
        early = jnp.concatenate([jnp.sum(early.astype(f32), 0).astype(bf16), scalars], 0)
        early_lines = early.shape[0]
        early = gathered(early, both, devices, [1])
        early = early.reshape(-1, CZ)
        early = jnp.broadcast_to(early[None], (rows // 2, *early.shape))
        parcel = jnp.concatenate([(keep.astype(f32) + got.astype(f32)).astype(bf16), early], 1)
        parcel, do = lax.optimization_barrier((parcel, do))
        parcel = lax.all_to_all(parcel, "row", 0, 0, axis_index_groups=row_sides, tiled=True)
        keep, give = back(info, p, qkv, vn, do, nd, zbt)
        got = swap(give, both, devices, 1)
        ours = parcel[:, -2 * early_lines :]
        across = swap(ours, both, devices, rows)
        keep, send = late_sums(parcel, keep, got, zbt)
        for n, mask in enumerate(all_masks[:-1]):
            if n == 0:
                keep = keep + swap(send, both, devices, mask).astype(f32)
            else:
                if n == len(all_masks) - 2:
                    keep = keep + across[0, -16:-15].astype(f32) * 0.0
                keep = keep + swap(keep, both, devices, mask)
        other = swap(keep, both, devices, 1)
        scalars = jnp.stack([ours, across])
        scalars = scalars.reshape(crops, rows, -1, CZ)[:, :, -16, :6]
        scalars = jnp.sum(scalars.astype(f32), (0, 1)).reshape(3, 2)
        loss_sum, pair_count = jnp.sum(scalars[:, 0]), jnp.sum(scalars[:, 1])
        (
            wide_g,
            wide_r_new,
            wide_c_new,
            wide_new,
            down_g,
            down_r_new,
            down_c_new,
            down_new,
            gain_grad,
            gain_s,
            gain_n,
            small_grad,
            small_s,
            small_n,
        ) = finish(
            crops,
            rows,
            info,
            keep,
            other,
            ours,
            across,
            packs,
            other_packs,
            wide_full,
            wide,
            down,
            gains,
            gain_second,
            small_t,
            small_second.T,
        )
        return (
            loss_sum,
            pair_count,
            wide_g,
            wide_r_new,
            wide_c_new,
            wide_new,
            down_g,
            down_r_new,
            down_c_new,
            down_new,
            gain_grad,
            gain_s,
            gain_n,
            small_grad.T,
            small_s.T,
            small_n.T,
        )

    return body


def solution(mesh):
    return jax.shard_map(
        build(mesh.shape["crop"], mesh.shape["row"]),
        mesh=mesh,
        in_specs=(
            P("crop", "row", None, None),
            P("crop"),
            P("crop", "row", None),
            P("crop", "row", None),
            P("row", "crop"),
            P("row"),
            P("crop"),
            P("row", "crop"),
            P("row"),
            P("crop"),
            P(),
            P(),
            P(),
            P(),
        ),
        out_specs=(
            P(),
            P(),
            P("row", "crop"),
            P("row"),
            P("crop"),
            P("row", "crop"),
            P("row", "crop"),
            P("row"),
            P("crop"),
            P("row", "crop"),
            P(),
            P(),
            P(),
            P(),
            P(),
            P(),
        ),
        check_vma=False,
    )
```
